32 devices in a mesh: row: 2 (over x), col: 16 (over z, y, core).
Axes of the slice: x: 2, y: 2, z: 4, core: 2. Of those that a mesh axis runs over, the one named last changes fastest.
Arguments:
- tokens: bfloat16 [4096, 2048], P('row', 'col'), may hold values from -6 to 6
- cotangent: bfloat16 [4096, 2048], P('row', 'col'), may hold values from -6 to 6
- segments: int32 [4, 1024], P('row'), may hold values from 0 to 3, never falling along the last dimension, each value on 1 to 512 neighbouring positions
- routes: int32 [4096, 6], P('row'), may hold values from 0 to 15, all different within a row; in each aligned block of 2048 rows (0 to 2047, 2048 to 4095, ...) at most 1024 rows name the same one
- first_gain: float32 [2048], P('col'), may hold values from 0.5 to 1.5
- query_proj: bfloat16 [2048, 3072], P('row', 'col'), may hold values from -0.1875 to 0.1875
- latent_down: bfloat16 [2048, 576], P('row', 'col'), may hold values from -0.125 to 0.125
- latent_gain: float32 [512], replicated, may hold values from 0.5 to 1.5
- latent_up: bfloat16 [512, 4096], P('row', 'col'), may hold values from -0.25 to 0.25
- output_proj: bfloat16 [2048, 2048], P('col', 'row'), may hold values from -0.75 to 0.75
- second_gain: float32 [2048], P('col'), may hold values from 0.5 to 1.5
- router_weight: bfloat16 [2048, 16], P('row'), may hold values from -0.0625 to 0.0625
- expert_gate: bfloat16 [16, 2048, 1408], P('col', 'row'), may hold values from -0.125 to 0.125
- expert_up: bfloat16 [16, 2048, 1408], P('col', 'row'), may hold values from -0.125 to 0.125
- expert_down: bfloat16 [16, 1408, 2048], P('col', None, 'row'), may hold values from -1.25 to 1.25
- shared_gate: bfloat16 [2048, 2816], P('row', 'col'), may hold values from -0.125 to 0.125
- shared_up: bfloat16 [2048, 2816], P('row', 'col'), may hold values from -0.125 to 0.125
- shared_down: bfloat16 [2816, 2048], P('col', 'row'), may hold values from -0.21875 to 0.21875
Outputs:
- output: bfloat16 [4096, 2048], P('row', 'col')
- grad_input: bfloat16 [4096, 2048], P('row', 'col')
- grad_first_gain: float32 [2048], P('col')
- grad_query_proj: float32 [2048, 3072], P('row', 'col')
- grad_latent_down: float32 [2048, 576], P('row', 'col')
- grad_latent_gain: float32 [512], replicated
- grad_latent_up: float32 [512, 4096], P('row', 'col')
- grad_output_proj: float32 [2048, 2048], P('col', 'row')
- grad_second_gain: float32 [2048], P('col')
- grad_router_weight: float32 [2048, 16], P('row')
- grad_expert_gate: float32 [16, 2048, 1408], P('col', 'row')
- grad_expert_up: float32 [16, 2048, 1408], P('col', 'row')
- grad_expert_down: float32 [16, 1408, 2048], P('col', None, 'row')
- grad_shared_gate: float32 [2048, 2816], P('row', 'col')
- grad_shared_up: float32 [2048, 2816], P('row', 'col')
- grad_shared_down: float32 [2816, 2048], P('col', 'row')
The draws below stay inside these ranges and needn't reach their ends.
Inputs may be any that keep to these rules, and one draw needn't show every extreme that they name: `routes`: each row names 6 different experts. In each aligned block of 2048 rows no expert is named by more than 1024 rows, a bound that some block reaches. `segments`: within each sequence the numbers never fall; each document holds 1 to 512 positions, one exactly that many.
All inputs are finite; a program needn't handle non-finite values.
Results may differ from the reference program's by a relative error of at most 0.018.
Values may be sent and summed in bfloat16 or wider, within the bound.
A program may use at most 256 MiB of HBM per device.

```python
import math
import jax
import jax.numpy as jnp
import numpy as np
from jax import lax

D = 2048
HEADS = 16
NOPE = 128
ROPE = 64
VD = 128
LATENT = 512
FF = 1408
SFF = 2816
TOP = 6
LEN = 1024
DOCS = 4
WINDOW = 1024
SEQS_ROW = 2
EXPERTS = 16
TOK_ROW = 2048
TOKENS = 4096
SEQUENCES = 4
CAPACITY = 1024
N_ROW = 2


def shard_levels(stream_key, shape, split, smallest, high):
    def one(axis_at, shards_of):
        steps = jax.random.uniform(jax.random.fold_in(jax.random.fold_in(stream_key, 6), axis_at), (shards_of,), jnp.float32, smallest / len(split), high / len(split))
        return jnp.repeat(jnp.exp(steps), shape[axis_at] // shards_of).reshape((-1,) + (1,) * (len(shape) - axis_at - 1))

    factor_of = one(*split[0])
    for cut in split[1:]:
        factor_of = factor_of * one(*cut)
    return factor_of


def split_up(count, total, reach, slope):
    loads = [(1 << 20) // math.isqrt(rank ** slope) + 1 for rank in range(2, count + 1)]
    spare, counts = total - reach - (count - 1), [1] * (count - 1)
    while spare > 0:
        free = [i for i in range(count - 1) if counts[i] < reach]
        whole, remaining = sum([loads[i] for i in free]), spare
        for i in free:
            more = min(reach - counts[i], max(1, remaining * loads[i] // whole), spare)
            counts[i] = counts[i] + more
            spare = spare - more
    return np.array([reach] + counts)


def ragged_sizes(stream_key, amount, total, bound, skew):
    if amount == 2:
        one = jax.random.randint(stream_key, (), max(1, total - bound), min(bound, total - 1) + 1)
        return jnp.stack([one, total - one])
    lengths = jnp.asarray(split_up(amount, total, bound, skew), jnp.int32)
    twos = (amount - 1) // 2
    source_of, taker = lengths[1:1 + 2 * twos:2], lengths[2:2 + 2 * twos:2]
    margin = jnp.minimum(source_of - 1, bound - taker)
    shifted = jax.random.randint(jax.random.fold_in(stream_key, 1), (twos,), 0, 1 << 20) % (margin + 1)
    lengths = lengths.at[1:1 + 2 * twos:2].set(source_of - shifted).at[2:2 + 2 * twos:2].set(taker + shifted)
    return lengths[jax.random.permutation(jax.random.fold_in(stream_key, 2), amount)]


def assign_block(key, own, number, rows, amount, top, reach, lean):
    ranking = jax.random.permutation(key, amount)
    packed, common = load_shares(amount, rows * top, reach, lean, True), load_shares(amount, rows * top, reach, lean, False)
    places = jnp.arange(amount)

    def named(lengths, rotation):
        used = int((lengths > 0).sum())
        fixed = max(1, used // 4)
        passed = fixed + (places - fixed + rotation * (used - fixed)) % max(1, amount - fixed)
        return jnp.zeros((amount,), jnp.int32).at[ranking[jnp.where(places < fixed, places, passed)]].set(jnp.asarray(lengths, jnp.int32))

    lengths = jnp.where(number % 4 == 0, named(packed, number // 4), named(common, number - number // 4 - 1))
    mixed = jax.random.permutation(jax.random.fold_in(own, 3), amount)
    source_of, sink = mixed[0:amount // 2 * 2:2], mixed[1:amount // 2 * 2:2]
    room = jnp.minimum(lengths[source_of] - 1, reach - lengths[sink]) // 2
    room = jnp.where((source_of == ranking[0]) | (sink == ranking[0]) | (lengths[sink] == 0), 0, jnp.maximum(room, 0))
    passed = jax.random.randint(jax.random.fold_in(own, 4), (amount // 2,), 0, 1 << 20) % (room + 1)
    lengths = lengths.at[source_of].add(-passed).at[sink].add(passed)
    members = jnp.searchsorted(jnp.cumsum(lengths), jnp.arange(rows * top), side="right").astype(jnp.int32)
    grid = members.reshape(top, rows).T
    grid = grid[jax.random.permutation(jax.random.fold_in(own, 1), rows)]
    rotation = jax.random.randint(jax.random.fold_in(own, 2), (rows, 1), 0, top)
    return jnp.take_along_axis(grid, (jnp.arange(top)[None, :] + rotation) % top, axis=1)


def load_shares(amount, total, most, slope, full):
    portions = [(1 << 20) // math.isqrt(rank ** slope) + 1 for rank in range(1, amount + 1)]
    largest = most if full else min(most, max(-(-total // amount), total * portions[0] // sum(portions)))
    least = 1 if total - largest >= amount - 1 else 0
    given, surplus = [largest] + [least] * (amount - 1), total - largest - least * (amount - 1)
    while surplus > 0:
        candidates = [i for i in range(1, amount) if given[i] < largest] or [i for i in range(1, amount) if given[i] < most]
        whole, remaining = sum([portions[i] for i in candidates]), surplus
        for i in candidates:
            more = min(most - given[i], max(1, remaining * portions[i] // whole), surplus)
            given[i] = given[i] + more
            surplus = surplus - more
    return np.array(given)


def noise(stream_key, extent, spread, limit, cuts=(), kind=jnp.bfloat16):
    loudness = shard_levels(stream_key, extent, cuts, -0.22, 0.18) if cuts else 1.0
    values = jax.random.normal(stream_key, extent, jnp.float32) * spread * loudness
    return jnp.minimum(jnp.maximum(values, -limit), limit).astype(kind)


def setup_inputs(seed: int = 0) -> dict:
    seeds = jax.random.split(jax.random.key(seed), 19)
    tokens = noise(seeds[0], (TOKENS, D), 1.0, 6.0, ((0, 2), (1, 16)))
    cotangent = noise(seeds[1], (TOKENS, D), 1.0, 6.0, ((0, 2), (1, 16)))
    segments = jax.vmap(lambda own: jnp.searchsorted(jnp.cumsum(ragged_sizes(own, DOCS, LEN, LEN // 2, 0)), jnp.arange(LEN), side="right"))(jax.random.split(seeds[2], SEQUENCES)).reshape((SEQUENCES, LEN)).astype(jnp.int32)
    routes_keys = jax.random.split(jax.random.fold_in(seeds[3], 1), TOKENS // TOK_ROW)
    routes_turns = jax.random.permutation(jax.random.fold_in(seeds[3], 3), TOKENS // TOK_ROW)
    routes = jax.vmap(lambda own, number: assign_block(jax.random.fold_in(seeds[3], 2), own, number, TOK_ROW, EXPERTS, TOP, CAPACITY, 1))(routes_keys, routes_turns).reshape((TOKENS, TOP))
    first_gain = jnp.clip(1.0 + 0.1 * jax.random.normal(seeds[4], (D,), jnp.float32), 0.5, 1.5)
    query_proj = noise(seeds[5], (D, HEADS * (NOPE + ROPE)), (D // 2) ** -0.5, 0.1875, ((0, 2), (1, 16)))
    latent_down = noise(seeds[6], (D, LATENT + ROPE), D ** -0.5, 0.125, ((0, 2), (1, 16)))
    latent_gain = jnp.clip(1.0 + 0.1 * jax.random.normal(seeds[7], (LATENT,), jnp.float32), 0.5, 1.5)
    latent_up = noise(seeds[8], (LATENT, HEADS * (NOPE + VD)), LATENT ** -0.5, 0.25, ((0, 2), (1, 16)))
    output_proj = noise(seeds[9], (HEADS * VD, D), (HEADS * VD // 32) ** -0.5, 0.75, ((0, 16), (1, 2)))
    second_gain = jnp.clip(1.0 + 0.1 * jax.random.normal(seeds[10], (D,), jnp.float32), 0.5, 1.5)
    router_weight = noise(seeds[11], (D, EXPERTS), (4 * D) ** -0.5, 0.0625, ((0, 2),))
    expert_gate = noise(seeds[12], (EXPERTS, D, FF), D ** -0.5, 0.125, ((0, 16), (1, 2)))
    expert_up = noise(seeds[13], (EXPERTS, D, FF), D ** -0.5, 0.125, ((0, 16), (1, 2)))
    expert_down = noise(seeds[14], (EXPERTS, FF, D), (max(FF // 64, 1)) ** -0.5, 1.25, ((0, 16), (2, 2)))
    shared_gate = noise(seeds[15], (D, SFF), D ** -0.5, 0.125, ((0, 2), (1, 16)))
    shared_up = noise(seeds[16], (D, SFF), D ** -0.5, 0.125, ((0, 2), (1, 16)))
    shared_down = noise(seeds[17], (SFF, D), (SFF // 4) ** -0.5, 0.21875, ((0, 16), (1, 2)))
    return dict(tokens=tokens, cotangent=cotangent, segments=segments, routes=routes, first_gain=first_gain, query_proj=query_proj, latent_down=latent_down, latent_gain=latent_gain, latent_up=latent_up, output_proj=output_proj, second_gain=second_gain, router_weight=router_weight, expert_gate=expert_gate, expert_up=expert_up, expert_down=expert_down, shared_gate=shared_gate, shared_up=shared_up, shared_down=shared_down)


@jax.custom_vjp
def low(v):
    return lax.optimization_barrier(v.astype(jnp.bfloat16)).astype(jnp.float32)

@jax.custom_vjp
def low_back(v):
    return v

def low_keep(v):
    return (low(v), None)

def low_pass(kept, grad):
    return (grad,)

def back_keep(v):
    return (v, None)

def back_low(kept, grad):
    return (low(grad),)
low.defvjp(low_keep, low_pass)
low_back.defvjp(back_keep, back_low)
EPSILON = 1e-06
HIGHEST = lax.Precision.HIGHEST

def multiplied_result(left_side, right_side):
    return jnp.dot(left_side, right_side, precision=HIGHEST, preferred_element_type=jnp.float32)

def inverse_root(values):
    return lax.rsqrt(lax.optimization_barrier(jnp.mean(values * values, axis=-1, keepdims=True)) + EPSILON)

def rotate(values, cosines, sine_part):
    half_width = values.shape[-1] // 2
    first = values[..., :half_width]
    second = values[..., half_width:]
    return jnp.concatenate([first * cosines - second * sine_part, first * sine_part + second * cosines], -1)

def attend(pieces):
    queries, keys_full, values, segment = pieces
    scores = jnp.einsum('qhd,khd->hqk', queries, keys_full, precision=HIGHEST) * (NOPE + ROPE) ** (-0.5)
    position = jnp.arange(LEN)
    allowed = (segment[:, None] == segment[None, :]) & (position[:, None] >= position[None, :]) & (position[:, None] - position[None, :] < WINDOW)
    scores = low_back(jnp.where(allowed[None], scores, -1e+30))
    weights = jnp.exp(scores - lax.optimization_barrier(jnp.max(scores, -1, keepdims=True)))
    attn_probs = low(weights / lax.optimization_barrier(jnp.sum(weights, -1, keepdims=True)))
    return jnp.einsum('hqk,khd->qhd', attn_probs, values, precision=HIGHEST)

def block_forward(params, stream, segment, route_rows):
    first_gain, query_proj, latent_down, latent_gain, latent_up, output_proj, second_gain, router_weight, expert_gate, expert_up, expert_down, shared_gate, shared_up, shared_down = params
    row_count = stream.shape[0]
    position = (jnp.arange(row_count) % LEN).astype(jnp.float32)
    frequency = 10000.0 ** (-jnp.arange(ROPE // 2).astype(jnp.float32) * 2.0 / ROPE)
    angles = position[:, None] * frequency[None, :]
    cosines = jnp.cos(angles)
    sine_part = jnp.sin(angles)
    normed = low(stream * inverse_root(stream) * first_gain)
    query_pre = low_back(multiplied_result(normed, query_proj)).reshape(row_count, HEADS, NOPE + ROPE)
    queries = low(jnp.concatenate([query_pre[..., :NOPE], rotate(query_pre[..., NOPE:], cosines[:, None, :], sine_part[:, None, :])], -1))
    compressed_all = low_back(low(multiplied_result(normed, latent_down)))
    compressed = compressed_all[:, :LATENT]
    latent = low(compressed * inverse_root(compressed) * latent_gain)
    key_rope = low(rotate(compressed_all[:, LATENT:], cosines, sine_part))
    expanded = low_back(low(multiplied_result(latent, latent_up))).reshape(row_count, HEADS, NOPE + VD)
    keys_full = jnp.concatenate([expanded[..., :NOPE], jnp.broadcast_to(key_rope[:, None, :], (row_count, HEADS, ROPE))], -1)
    values = expanded[..., NOPE:]
    seqs_here = row_count // LEN
    attended = lax.map(jax.checkpoint(attend), (queries.reshape(seqs_here, LEN, HEADS, NOPE + ROPE), keys_full.reshape(seqs_here, LEN, HEADS, NOPE + ROPE), values.reshape(seqs_here, LEN, HEADS, VD), segment))
    mixed_rows = low_back(low(attended.reshape(row_count, HEADS * VD)))
    hidden = stream + low_back(multiplied_result(mixed_rows, output_proj))
    normed_two = low(hidden * inverse_root(hidden) * second_gain)
    router_probs = jax.nn.softmax(multiplied_result(normed_two, router_weight), -1)
    member = jnp.any(route_rows[:, :, None] == jnp.arange(EXPERTS)[None, None, :], 1)
    gate_table = router_probs * member
    slot_number = jnp.cumsum(member.astype(jnp.int32), 0) - 1
    target = jnp.where(member, slot_number, CAPACITY)
    expert_ids = jnp.broadcast_to(jnp.arange(EXPERTS, dtype=jnp.int32)[None, :], (row_count, EXPERTS))
    token_ids = jnp.broadcast_to(jnp.arange(row_count, dtype=jnp.int32)[:, None], (row_count, EXPERTS))
    slot_token = jnp.zeros((EXPERTS, CAPACITY), jnp.int32).at[expert_ids, target].set(token_ids, mode='drop')
    filled = jnp.arange(CAPACITY)[None, :] < lax.optimization_barrier(jnp.sum(member.astype(jnp.int32), 0))[:, None]
    slot_gate = jnp.take_along_axis(gate_table.T, slot_token, 1) * filled
    collected_rows = normed_two[slot_token]
    gate_in = low_back(jnp.einsum('ecd,edf->ecf', collected_rows, expert_gate, precision=HIGHEST))
    up_projection_input = low_back(jnp.einsum('ecd,edf->ecf', collected_rows, expert_up, precision=HIGHEST))
    activation = low(jax.nn.silu(gate_in) * up_projection_input)
    expert_out = low_back(jnp.einsum('ecf,efd->ecd', activation, expert_down, precision=HIGHEST))
    routed = jnp.zeros((row_count, D), jnp.float32).at[slot_token].add(slot_gate[..., None] * expert_out)
    shared_in = low_back(multiplied_result(normed_two, shared_gate))
    shared_lift = low_back(multiplied_result(normed_two, shared_up))
    shared_act = low(jax.nn.silu(shared_in) * shared_lift)
    return hidden + routed + multiplied_result(shared_act, shared_down)

def reference(tokens, cotangent, segments, routes, first_gain, query_proj, latent_down, latent_gain, latent_up, output_proj, second_gain, router_weight, expert_gate, expert_up, expert_down, shared_gate, shared_up, shared_down):
    params = tuple((weight.astype(jnp.float32) for weight in (first_gain, query_proj, latent_down, latent_gain, latent_up, output_proj, second_gain, router_weight, expert_gate, expert_up, expert_down, shared_gate, shared_up, shared_down)))
    streams = tokens.astype(jnp.float32).reshape(N_ROW, TOK_ROW, D)
    seed_grads = cotangent.astype(jnp.float32).reshape(N_ROW, TOK_ROW, D)
    segment_rows = segments.reshape(N_ROW, SEQS_ROW, LEN)
    route_blocks = routes.reshape(N_ROW, TOK_ROW, TOP)

    def group(grad_total, pieces):
        stream, seed_grad, segment, route_rows = pieces
        result, pullback = jax.vjp(lambda weights, values: block_forward(weights, values, segment, route_rows), params, stream)
        weight_grads, grad_stream = pullback(seed_grad)
        return (jax.tree.map(lambda first, second: first + second, grad_total, weight_grads), (result, grad_stream))
    starting = jax.tree.map(jnp.zeros_like, params)
    grad_total, (results, grad_streams) = lax.scan(group, starting, (streams, seed_grads, segment_rows, route_blocks))
    return (results.reshape(TOKENS, D).astype(jnp.bfloat16), grad_streams.reshape(TOKENS, D).astype(jnp.bfloat16), grad_total[0], grad_total[1], grad_total[2], grad_total[3], grad_total[4], grad_total[5], grad_total[6], grad_total[7], grad_total[8], grad_total[9], grad_total[10], grad_total[11], grad_total[12], grad_total[13])
```

```python
import functools

import jax
import jax.numpy as jnp
from jax import lax
from jax.experimental import pallas as pl
from jax.experimental.pallas import tpu as pltpu
from jax.sharding import PartitionSpec as P

NOPE = 128
ROPE = 64
VD = 128
LATENT = 512
LEN = 1024
WINDOW = 1024
EPSILON = 1e-06
LANES = 128
MESH = pl.DeviceIdType.MESH
BF16 = jnp.bfloat16
F32 = jnp.float32
UP, DOWN, SIDE, CORE = range(4)


def dot_nn(a, b):
    return jnp.dot(a, b, preferred_element_type=F32)


def dot_nt(a, b):
    return lax.dot_general(a, b, (((1,), (1,)), ((), ())), preferred_element_type=F32)


def dot_tn(a, b):
    return lax.dot_general(a, b, (((0,), (0,)), ((), ())), preferred_element_type=F32)


def place():
    me = lax.axis_index("col")
    return lax.axis_index("row"), me // 4, (me // 2) % 2, me % 2


def col_of(z, y, c):
    return z * 4 + y * 2 + c


def rolled(index, row, n_row, count):
    return lax.rem(index + count - row * (count // n_row), count)


def signal(row, target):
    pl.semaphore_signal(
        pltpu.get_barrier_semaphore(), inc=1, device_id=(row, target), device_id_type=MESH
    )


def greet_neighbours(row, z, y, c, depth):
    signal(row, col_of(z, 1 - y, c))
    signal(row, col_of(z, y, 1 - c))

    @pl.when(z > 0)
    def _():
        signal(row, col_of(z - 1, y, c))

    @pl.when(z < depth - 1)
    def _():
        signal(row, col_of(z + 1, y, c))

    count = 2 + (z > 0).astype(jnp.int32) + (z < depth - 1).astype(jnp.int32)
    pl.semaphore_wait(pltpu.get_barrier_semaphore(), count)


def greet_all(row, me, n):
    def hello(step, carry):
        signal(row, lax.rem(me + step, n))
        return carry

    lax.fori_loop(1, n, hello, 0)
    pl.semaphore_wait(pltpu.get_barrier_semaphore(), n - 1)


def gather_kernel(depth, n_row, pieces, count, *refs):
    ins, outs = refs[:count], refs[count : 2 * count]
    local_sem, send_sem, recv_sem = refs[2 * count :]
    row, z, y, c = place()
    me, n = col_of(z, y, c), 4 * depth
    greet_neighbours(row, z, y, c, depth)
    keeps = [
        pltpu.make_async_copy(ins[a], outs[a].at[rolled(me, row, n_row, n)], local_sem.at[a])
        for a in range(count)
    ]
    for keep in keeps:
        keep.start()

    def copy(way, block, piece, target, own=False):
        a, first, size = pieces[piece]
        rows = pl.ds(first, size)
        slot = rolled(block, row, n_row, n)
        return pltpu.make_async_remote_copy(
            src_ref=ins[a].at[rows] if own else outs[a].at[slot, rows],
            dst_ref=outs[a].at[slot, rows],
            send_sem=send_sem.at[way, block, piece],
            recv_sem=recv_sem.at[block, piece],
            device_id=(row, target),
            device_id_type=MESH,
        )

    def start(way, block, piece, target, own=False):
        copy(way, block, piece, target, own).start()

    def finish(way, block, piece, target, own=False):
        copy(way, block, piece, target, own).wait_send()

    def arrive(block, piece):
        copy(CORE, block, piece, me).wait_recv()

    up, down = col_of(z + 1, y, c), col_of(z - 1, y, c)
    side, core = col_of(z, 1 - y, c), col_of(z, y, 1 - c)

    def line(d, p, act):
        if d == 0:
            act(SIDE, me, p, side, True)

            @pl.when(z + 1 < depth)
            def _():
                act(UP, me, p, up, True)

            @pl.when(z > 0)
            def _():
                act(DOWN, me, p, down, True)

            act(CORE, me, p, core, True)
            return

        @pl.when(z - d >= 0)
        def _():
            block = col_of(z - d, y, c)
            if act is start:
                arrive(block, p)

            @pl.when(z + 1 < depth)
            def _():
                act(UP, block, p, up)

            act(SIDE, block, p, side)
            act(CORE, block, p, core)

        @pl.when(z + d < depth)
        def _():
            block = col_of(z + d, y, c)
            if act is start:
                arrive(block, p)

            @pl.when(z > 0)
            def _():
                act(DOWN, block, p, down)

            act(SIDE, block, p, side)
            act(CORE, block, p, core)

    def sides(d, p, act):
        for sign in (-1, 1) if d else (1,):
            at = z + sign * d

            @pl.when((at >= 0) & (at < depth))
            def _():
                block = col_of(at, 1 - y, c)
                if act is start:
                    arrive(block, p)
                act(CORE, block, p, core)

    span = range(len(pieces))
    for d in range(depth):
        for p in span:
            line(d, p, start)
        if d:
            for p in span:
                sides(d - 1, p, start)
    for p in span:
        sides(depth - 1, p, start)
    for p in span:
        for zz in range(depth):
            for yy in range(2):
                arrive(col_of(zz, yy, 1 - c), p)
    for d in range(depth):
        for p in span:
            line(d, p, finish)
            sides(d, p, finish)
    for keep in keeps:
        keep.wait()


def gather_cols(arrays, parts, collective_id):
    n, n_row = lax.axis_size("col"), lax.axis_size("row")
    pieces = []
    for a, array in enumerate(arrays):
        cuts = parts if array.shape[0] >= 1024 else 1
        size = array.shape[0] // cuts
        pieces += [(a, i * size, size) for i in range(cuts)]
    pieces.sort(key=lambda piece: (arrays[piece[0]].shape[0], piece[1]))
    count = len(arrays)
    anywhere = pl.BlockSpec(memory_space=pl.ANY)
    return pl.pallas_call(
        functools.partial(gather_kernel, n // 4, n_row, tuple(pieces), count),
        out_shape=[jax.ShapeDtypeStruct((n,) + a.shape, a.dtype) for a in arrays],
        in_specs=[anywhere] * count,
        out_specs=[anywhere] * count,
        scratch_shapes=[
            pltpu.SemaphoreType.DMA((count,)),
            pltpu.SemaphoreType.DMA((4, n, len(pieces))),
            pltpu.SemaphoreType.DMA((n, len(pieces))),
        ],
        compiler_params=pltpu.CompilerParams(collective_id=collective_id, has_side_effects=True),
        name="gather_cols",
    )(*arrays)


def scatter_kernel(depth, n_row, parts, kinds, has_stat, *refs):
    count = 2 * len(kinds) + has_stat
    operands, stat = refs[: 2 * len(kinds)], refs[count - 1] if has_stat else None
    out = refs[count]
    stats = refs[count + 1] if has_stat else None
    rest = refs[count + 1 + has_stat :]
    mine, core_send, core_recv, side_send, side_recv, line_send, line_recv = rest[:7]
    cs, cr, ss, sr, ls, lr = rest[7:13]
    row, z, y, c = place()
    me, n = col_of(z, y, c), 4 * depth
    pairs = 2 * depth
    rows = out.shape[0]
    size = rows // parts
    tile = min(256, size)
    if has_stat:
        stat_held, stat_send, stat_recv = rest[13:16]
        greet_all(row, me, n)

        def stat_copy(step):
            target = lax.rem(me + step, n)
            return pltpu.make_async_remote_copy(
                src_ref=stat,
                dst_ref=stat_held.at[me],
                send_sem=stat_send.at[step],
                recv_sem=stat_recv.at[me],
                device_id=(row, target),
                device_id_type=MESH,
            )

        for step in range(1, n):
            stat_copy(step).start()
    else:
        greet_neighbours(row, z, y, c, depth)
    up, down = col_of(z + 1, y, c), col_of(z - 1, y, c)
    side, core = col_of(z, 1 - y, c), col_of(z, y, 1 - c)

    def remote(src, dst, send, recv, target):
        return pltpu.make_async_remote_copy(
            src_ref=src, dst_ref=dst, send_sem=send, recv_sem=recv,
            device_id=(row, target), device_id_type=MESH,
        )

    def span(h):
        return pl.ds(h * size, size)

    def core_copy(s, h):
        return remote(core_send.at[s, span(h)], core_recv.at[s, span(h)], cs.at[s, h], cr.at[s, h], core)

    def side_copy(k, h):
        return remote(side_send.at[k, span(h)], side_recv.at[k, span(h)], ss.at[k, h], sr.at[k, h], side)

    def line_copy(way, zz, h, target):
        return remote(
            line_send.at[zz, span(h)], line_recv.at[way, zz, span(h)], ls.at[zz, h], lr.at[way, zz, h], target
        )

    low_half = z < depth // 2

    def order(k):
        if k == depth - 1:
            return z
        from_top = depth - 1 - k
        from_top = from_top - (from_top <= z).astype(jnp.int32)
        from_low = k + (k >= z).astype(jnp.int32)
        return jnp.where(low_half, from_top, from_low)

    def tiles(body):
        def step(i, carry):
            body(i)
            return carry

        lax.fori_loop(0, size // tile, step, 0)

    def multiply(s, h):
        yy = 1 - y if s < depth else y
        pair = rolled(order(s % depth) * 2 + yy, row, n_row, pairs)
        cols = pl.ds(pl.multiple_of(pair * 2 * LANES, 2 * LANES), 2 * LANES)

        def body(i):
            at = pl.ds(pl.multiple_of(h * size + i * tile, tile), tile)
            total = None
            for j, kind in enumerate(kinds):
                left, right = operands[2 * j], operands[2 * j + 1]
                if kind == "nn":
                    term = dot_nn(left[at, :], right[:, cols])
                else:
                    term = dot_nt(left[at, :], right[cols, :])
                total = term if total is None else total + term
            first, second = total[:, :LANES], total[:, LANES:]
            mine[s, at, :] = jnp.where(c == 0, first, second)
            core_send[s, at, :] = jnp.where(c == 0, second, first).astype(BF16)

        tiles(body)
        core_copy(s, h).start()

    def summed(target, at, sources):
        total = sources[0][at, :]
        for source in sources[1:]:
            total = total + source[at, :].astype(F32)
        target[at, :] = total.astype(target.dtype)

    def add_up(target, h, sources):
        def body(i):
            summed(target, pl.ds(pl.multiple_of(h * size + i * tile, tile), tile), sources)

        tiles(body)

    def fold(s, h):
        core_copy(s, h).wait_recv()
        k = s % depth
        sources = [mine.at[s], core_recv.at[s]]
        if s < depth:
            add_up(side_send.at[k], h, sources)
            side_copy(k, h).start()
            return
        side_copy(k, h).wait_recv()
        sources.append(side_recv.at[k])
        zz = order(k)
        if k < depth - 1:

            @pl.when(zz > z)
            def _():
                @pl.when(z > 0)
                def _():
                    line_copy(0, zz, h, up).wait_recv()
                    add_up(line_send.at[zz], h, sources + [line_recv.at[0, zz]])

                @pl.when(z == 0)
                def _():
                    add_up(line_send.at[zz], h, sources)

                line_copy(0, zz, h, up).start()

            @pl.when(zz < z)
            def _():
                @pl.when(z < depth - 1)
                def _():
                    line_copy(1, zz, h, down).wait_recv()
                    add_up(line_send.at[zz], h, sources + [line_recv.at[1, zz]])

                @pl.when(z == depth - 1)
                def _():
                    add_up(line_send.at[zz], h, sources)

                line_copy(1, zz, h, down).start()

            return

        @pl.when((z > 0) & (z < depth - 1))
        def _():
            line_copy(0, z, h, me).wait_recv()
            line_copy(1, z, h, me).wait_recv()
            add_up(out, h, sources + [line_recv.at[0, z], line_recv.at[1, z]])

        @pl.when(z == 0)
        def _():
            line_copy(1, z, h, me).wait_recv()
            add_up(out, h, sources + [line_recv.at[1, z]])

        @pl.when(z == depth - 1)
        def _():
            line_copy(0, z, h, me).wait_recv()
            add_up(out, h, sources + [line_recv.at[0, z]])

    steps = [(s, h) for s in range(2 * depth) for h in range(parts)]
    for i, (s, h) in enumerate(steps):
        multiply(s, h)
        if i >= 2:
            fold(*steps[i - 2])
    for s, h in steps[-2:]:
        fold(s, h)
    for s, h in steps:
        core_copy(s, h).wait_send()
    for k in range(depth):
        for h in range(parts):
            side_copy(k, h).wait_send()
    for k in range(depth - 1):
        zz = order(k)
        for h in range(parts):
            line_copy(0, zz, h, me).wait_send()
    if has_stat:
        stat_held[me] = stat[...]
        for step in range(1, n):
            stat_copy(step).wait_send()
            source = lax.rem(me + step, n)
            remote(stat, stat_held.at[source], stat_send.at[step], stat_recv.at[source], me).wait_recv()
        stats[...] = stat_held[...]


def scatter_cols(products, stat, parts, collective_id):
    n, n_row = lax.axis_size("col"), lax.axis_size("row")
    depth = n // 4
    kinds = tuple(kind for kind, _, _ in products)
    operands = [x for _, a, b in products for x in (a, b)]
    rows = operands[0].shape[0]
    in_vmem = pl.BlockSpec(memory_space=pltpu.VMEM)
    out_shape = [jax.ShapeDtypeStruct((rows, LANES), F32)]
    dma = pltpu.SemaphoreType.DMA
    scratch = [
        pltpu.VMEM((2 * depth, rows, LANES), F32),
        pltpu.VMEM((2 * depth, rows, LANES), BF16),
        pltpu.VMEM((2 * depth, rows, LANES), BF16),
        pltpu.VMEM((depth, rows, LANES), BF16),
        pltpu.VMEM((depth, rows, LANES), BF16),
        pltpu.VMEM((depth, rows, LANES), BF16),
        pltpu.VMEM((2, depth, rows, LANES), BF16),
        dma((2 * depth, parts)),
        dma((2 * depth, parts)),
        dma((depth, parts)),
        dma((depth, parts)),
        dma((depth, parts)),
        dma((2, depth, parts)),
    ]
    if stat is not None:
        operands.append(stat)
        out_shape.append(jax.ShapeDtypeStruct((n,) + stat.shape, F32))
        scratch += [pltpu.VMEM((n,) + stat.shape, F32), dma((n,)), dma((n,))]
    return pl.pallas_call(
        functools.partial(scatter_kernel, depth, n_row, parts, kinds, stat is not None),
        out_shape=out_shape,
        in_specs=[in_vmem] * len(operands),
        out_specs=[in_vmem] * len(out_shape),
        scratch_shapes=scratch,
        compiler_params=pltpu.CompilerParams(
            collective_id=collective_id, has_side_effects=True, vmem_limit_bytes=60 << 20
        ),
        name="scatter_cols",
    )(*operands)


def row_shift(array, step):
    n = lax.axis_size("row")
    return lax.ppermute(array, "row", [(i, (i - step) % n) for i in range(n)])


def row_parts(array):
    return [array] + [row_shift(array, s) for s in range(1, lax.axis_size("row"))]


def row_sum(parts):
    n = lax.axis_size("row")
    total = parts[0]
    for s in range(1, n):
        total = total + row_shift(parts[s].astype(BF16), n - s).astype(F32)
    return total


def unroll_parts(parts, axis):
    n = len(parts)
    size = parts[0].shape[axis]
    doubled = jnp.concatenate(parts + parts[:-1], axis)
    start = lax.rem(n - lax.axis_index("row"), n) * size
    return lax.dynamic_slice_in_dim(doubled, start, n * size, axis)


def own_parts(array, axis):
    n = lax.axis_size("row")
    size = array.shape[axis] // n
    row = lax.axis_index("row")
    return [
        lax.dynamic_slice_in_dim(array, lax.rem(row + s, n) * size, size, axis) for s in range(n)
    ]


def cut(array, axis):
    return jnp.split(array, lax.axis_size("row"), axis)


def rotation_tables(row_count):
    position = (jnp.arange(row_count, dtype=jnp.int32) % LEN).astype(F32)
    frequency = 10000.0 ** (-jnp.arange(ROPE // 2).astype(F32) * 2.0 / ROPE)
    angles = position[:, None] * frequency[None, :]
    return (jnp.cos(angles), jnp.sin(angles))


def rotate(values, cosines, sine_part):
    half = values.shape[-1] // 2
    first, second = values[..., :half], values[..., half:]
    return jnp.concatenate(
        [first * cosines - second * sine_part, first * sine_part + second * cosines], -1
    )


def silu_slope(values):
    sigmoid = jax.nn.sigmoid(values)
    return sigmoid * (1.0 + values * (1.0 - sigmoid))


def score_block(queries, keys, segment):
    scores = dot_nt(queries, keys) * (NOPE + ROPE) ** (-0.5)
    position = jnp.arange(segment.shape[0])
    allowed = (
        (segment[:, None] == segment[None, :])
        & (position[:, None] >= position[None, :])
        & (position[:, None] - position[None, :] < WINDOW)
    )
    return jnp.where(allowed, scores, -1e30)


def attend_forward(queries, keys, values, segment):
    scores = score_block(queries, keys, segment)
    top = jnp.max(scores, -1, keepdims=True)
    weights = jnp.exp(scores - top)
    total = jnp.sum(weights, -1, keepdims=True)
    probs = (weights / total).astype(BF16)
    return dot_nn(probs, values).astype(BF16), top + jnp.log(total)


def attend_backward(queries, keys, values, segment, log_total, grad_mixed):
    scale = (NOPE + ROPE) ** (-0.5)
    probs = jnp.exp(score_block(queries, keys, segment) - log_total)
    grad_probs = dot_nt(grad_mixed, values)
    grad_scores = (
        probs * (grad_probs - jnp.sum(probs * grad_probs, -1, keepdims=True))
    ).astype(BF16)
    return (
        dot_nn(grad_scores, keys) * scale,
        dot_tn(grad_scores, queries) * scale,
        dot_tn(probs.astype(BF16), grad_mixed),
    )


def natural(slabs):
    n, rows, width = slabs.shape
    return jnp.swapaxes(slabs, 0, 1).reshape(rows, n * width)


def as_stat(*vectors):
    return jnp.concatenate([v.reshape(-1, LANES) for v in vectors], 0)


def per_device(
    tokens,
    cotangent,
    segments,
    routes,
    first_gain,
    query_proj,
    latent_down,
    latent_gain,
    latent_up,
    output_proj,
    second_gain,
    router_weight,
    expert_gate,
    expert_up,
    expert_down,
    shared_gate,
    shared_up,
    shared_down,
):
    row_count, share = tokens.shape
    n = lax.axis_size("col")
    width = share * n
    column = lax.axis_index("col")
    seqs = segments.shape[0]
    cosines, sine_part = rotation_tables(row_count)

    down_rows = jnp.concatenate(row_parts(latent_down), 0)
    down_full = lax.all_gather(down_rows, "col", axis=1, tiled=True)
    query_full = jnp.concatenate(row_parts(query_proj), 0)
    up_full = unroll_parts(row_parts(latent_up), 0)
    out_full = jnp.concatenate(row_parts(output_proj), 1)
    router_full = jnp.concatenate(row_parts(router_weight), 0)
    gate_parts = row_parts(expert_gate[0])
    lift_parts = row_parts(expert_up[0])
    shared_gate_full = jnp.concatenate(row_parts(shared_gate), 0)
    shared_up_full = jnp.concatenate(row_parts(shared_up), 0)
    shared_down_full = jnp.concatenate(row_parts(shared_down), 1)
    fall_parts = row_parts(expert_down[0])

    gain_rows = jnp.broadcast_to(first_gain[None, :], (8, share))
    token_slabs, gain_slabs = gather_cols([tokens, gain_rows], 2, 1)
    slabs = token_slabs.astype(F32)
    first_root = lax.rsqrt(jnp.sum(slabs * slabs, (0, 2)) / width + EPSILON)[:, None]
    normed = natural((slabs * first_root[None] * gain_slabs[:, :1]).astype(BF16))
    query_pre = dot_nn(normed, query_full)
    queries = jnp.concatenate(
        [query_pre[:, :NOPE], rotate(query_pre[:, NOPE:], cosines, sine_part)], -1
    ).astype(BF16)
    low = dot_nn(normed, down_full).astype(BF16)
    compressed = low[:, :LATENT].astype(F32)
    latent_root = lax.rsqrt(jnp.mean(compressed * compressed, 1, keepdims=True) + EPSILON)
    latent = (compressed * latent_root * latent_gain).astype(BF16)
    key_rope = rotate(low[:, LATENT:].astype(F32), cosines, sine_part).astype(BF16)
    expanded = dot_nn(latent, up_full).astype(BF16)
    keys = jnp.concatenate([expanded[:, :NOPE], key_rope], -1)
    values = expanded[:, NOPE:]

    def by_seq(array):
        return [array[i * LEN : (i + 1) * LEN] for i in range(seqs)]

    forward = [
        attend_forward(q, k, v, segments[i])
        for i, (q, k, v) in enumerate(zip(by_seq(queries), by_seq(keys), by_seq(values)))
    ]
    mixed = jnp.concatenate([f[0] for f in forward], 0)
    (branch,) = scatter_cols([("nn", mixed, out_full)], None, 2, 2)
    hidden = tokens.astype(F32) + branch
    squares = as_stat(jnp.sum(hidden * hidden, 1))
    second_slabs, square_slabs = gather_cols(
        [(hidden * second_gain).astype(BF16), squares], 2, 3
    )
    second_root = lax.rsqrt(
        jnp.sum(square_slabs, 0).reshape(row_count, 1) / width + EPSILON
    )
    normed_two = natural((second_slabs.astype(F32) * second_root[None]).astype(BF16))

    experts = router_full.shape[1]
    logits = dot_nn(normed_two, router_full)
    router_probs = jax.nn.softmax(logits, -1)
    own_expert = jnp.arange(experts) == column
    member = jnp.any(routes == column, 1)
    own_gate = jnp.sum(jnp.where(own_expert[None, :], router_probs, 0.0), 1)
    capacity = row_count * routes.shape[1] * 4 // (3 * experts)
    slot_number = jnp.cumsum(member.astype(jnp.int32)) - 1
    chosen = (slot_number[None, :] == jnp.arange(capacity)[:, None]) & member[None, :]
    pick = chosen.astype(BF16)
    slot_gate = jnp.sum(jnp.where(chosen, own_gate[None, :], 0.0), 1)

    (cotangent_slabs,) = gather_cols([cotangent], 2, 4)
    grad_full = natural(cotangent_slabs)

    picked = dot_nn(pick, normed_two).astype(BF16)
    picked_parts = cut(picked, 1)
    gate_in = sum(dot_nn(a, b) for a, b in zip(picked_parts, gate_parts))
    up_in = sum(dot_nn(a, b) for a, b in zip(picked_parts, lift_parts))
    activation = (jax.nn.silu(gate_in) * up_in).astype(BF16)
    picked_grad = dot_nn(pick, grad_full).astype(BF16)
    grad_parts = cut(picked_grad, 1)
    act_raw = sum(dot_nt(a, b) for a, b in zip(grad_parts, fall_parts))
    gate_dot = jnp.sum(activation.astype(F32) * act_raw, 1)
    act_grad = act_raw * slot_gate[:, None]
    grad_gate_in = (act_grad * up_in * silu_slope(gate_in)).astype(BF16)
    grad_up_in = (act_grad * jax.nn.silu(gate_in)).astype(BF16)
    slot_dot = jnp.sum(
        gate_in * grad_gate_in.astype(F32) + up_in * grad_up_in.astype(F32), 1
    )
    picked_back = jnp.concatenate(
        [
            (dot_nt(grad_gate_in, a) + dot_nt(grad_up_in, b)).astype(BF16)
            for a, b in zip(gate_parts, lift_parts)
        ],
        1,
    )
    shared_in = dot_nn(normed_two, shared_gate_full)
    shared_lift = dot_nn(normed_two, shared_up_full)
    shared_act = (jax.nn.silu(shared_in) * shared_lift).astype(BF16)
    shared_grad = dot_nt(grad_full, shared_down_full)
    shared_gin = (shared_grad * shared_lift * silu_slope(shared_in)).astype(BF16)
    shared_gup = (shared_grad * jax.nn.silu(shared_in)).astype(BF16)

    token_dot = jnp.sum(jnp.where(chosen, gate_dot[:, None], 0.0), 0)
    gate_share = own_gate * token_dot
    coefficient = (
        gate_share[:, None] * (own_expert[None, :].astype(F32) - router_probs)
    ).astype(BF16)
    inner = (
        jnp.sum(jnp.where(chosen, slot_dot[:, None], 0.0), 0)
        + jnp.sum(shared_in * shared_gin.astype(F32) + shared_lift * shared_gup.astype(F32), 1)
        + jnp.sum(coefficient.astype(F32) * logits, 1)
    )
    narrow = shared_gin.shape[1]
    pad = -(2 * narrow + experts) % LANES
    shared_left = jnp.concatenate(
        [shared_gin, shared_gup, coefficient, jnp.zeros((row_count, pad), BF16)], 1
    )
    shared_right = jnp.concatenate(
        [shared_gate_full, shared_up_full, router_full, jnp.zeros((width, pad), BF16)], 1
    )
    pick_back = pick.T
    grad_normed_two, stats = scatter_cols(
        [("nn", pick_back, picked_back), ("nt", shared_left, shared_right)],
        as_stat(inner, gate_share),
        2,
        5,
    )
    stats = stats.reshape(n, 2, row_count)
    inner_total = jnp.sum(stats[:, 0], 0)[:, None]
    shares = stats[:, 1].T
    logit_grad = shares - router_probs * jnp.sum(shares, 1, keepdims=True)
    grad_stream = cotangent.astype(F32)
    grad_hidden = (
        grad_stream
        + second_root * (grad_normed_two * second_gain)
        - hidden * (second_root * second_root * inner_total / width)
    )
    second_gain_grad = jnp.sum(grad_normed_two * hidden * second_root, 0)
    (hidden_slabs,) = gather_cols([grad_hidden.astype(BF16)], 2, 6)
    attn_grad = natural(hidden_slabs)

    expert_out = jnp.concatenate(
        [(slot_gate[:, None] * dot_nn(activation, b)).astype(BF16) for b in fall_parts], 1
    )
    (mixture,) = scatter_cols(
        [("nn", pick_back, expert_out), ("nn", shared_act, shared_down_full)], None, 2, 7
    )
    output = (hidden + mixture).astype(BF16)

    slot_grad = (slot_gate[:, None] * picked_grad.astype(F32)).astype(BF16)
    moe_grads = (
        row_sum([dot_tn(a, grad_gate_in) for a in picked_parts])[None],
        row_sum([dot_tn(a, grad_up_in) for a in picked_parts])[None],
        row_sum([dot_tn(activation, a) for a in cut(slot_grad, 1)])[None],
        row_sum(cut(dot_tn(normed_two, shared_gin), 0)),
        row_sum(cut(dot_tn(normed_two, shared_gup), 0)),
        row_sum(cut(dot_tn(shared_act, grad_full), 1)),
        row_sum(cut(dot_tn(normed_two, logit_grad.astype(BF16)), 0)),
    )

    output_grad = dot_tn(mixed, attn_grad)
    mixed_grad = dot_nt(attn_grad, out_full).astype(BF16)
    backward = [
        attend_backward(q, k, v, segments[i], forward[i][1], g)
        for i, (q, k, v, g) in enumerate(
            zip(by_seq(queries), by_seq(keys), by_seq(values), by_seq(mixed_grad))
        )
    ]
    query_grad, key_grad, value_grad = (
        jnp.concatenate([b[j] for b in backward], 0) for j in range(3)
    )
    query_back = jnp.concatenate(
        [query_grad[:, :NOPE], rotate(query_grad[:, NOPE:], cosines, -sine_part)], -1
    ).astype(BF16)
    expanded_grad = jnp.concatenate([key_grad[:, :NOPE], value_grad], -1).astype(BF16)
    latent_grad = dot_nt(expanded_grad, up_full)
    latent_dot = jnp.sum(latent_grad * latent.astype(F32), 1, keepdims=True)
    compressed_grad = (
        latent_root * latent_grad * latent_gain
        - compressed * (latent_root * latent_root * latent_dot / LATENT)
    )
    latent_gain_grad = jnp.sum(latent_grad * compressed * latent_root, 0)
    low_grad = jnp.concatenate(
        [compressed_grad, rotate(key_grad[:, NOPE:], cosines, -sine_part)], 1
    ).astype(BF16)
    inner = jnp.sum(query_grad * queries.astype(F32), 1) + jnp.sum(
        low_grad.astype(F32) * low.astype(F32), 1
    )
    grad_normed, stats = scatter_cols(
        [
            (
                "nt",
                jnp.concatenate([query_back, low_grad], 1),
                jnp.concatenate([query_full, down_full], 1),
            )
        ],
        as_stat(inner),
        2,
        8,
    )
    low_own = lax.psum_scatter(low_grad, "col", scatter_dimension=1, tiled=True)
    inner_total = jnp.sum(stats, 0).reshape(row_count, 1)
    stream = tokens.astype(F32)
    grad_input = (
        grad_hidden
        + first_root * (grad_normed * first_gain)
        - stream * (first_root * first_root * inner_total / width)
    )
    first_gain_grad = jnp.sum(grad_normed * stream * first_root, 0)
    attn_grads = (
        row_sum(cut(dot_tn(normed, query_back), 0)),
        row_sum(cut(dot_tn(normed, low_own), 0)),
        row_sum(own_parts(dot_tn(latent, expanded_grad), 0)),
        row_sum(cut(output_grad, 1)),
    )
    gain_grads = lax.psum((first_gain_grad, second_gain_grad), "row")
    latent_gain_total = lax.psum(latent_gain_grad, ("row", "col"))
    return (
        output,
        grad_input.astype(BF16),
        gain_grads[0],
        attn_grads[0],
        attn_grads[1],
        latent_gain_total,
        attn_grads[2],
        attn_grads[3],
        gain_grads[1],
        moe_grads[6],
        moe_grads[0],
        moe_grads[1],
        moe_grads[2],
        moe_grads[3],
        moe_grads[4],
        moe_grads[5],
    )


def solution(mesh):
    return jax.shard_map(
        per_device,
        mesh=mesh,
        in_specs=(
            P("row", "col"),
            P("row", "col"),
            P("row", None),
            P("row", None),
            P("col"),
            P("row", "col"),
            P("row", "col"),
            P(),
            P("row", "col"),
            P("col", "row"),
            P("col"),
            P("row", None),
            P("col", "row", None),
            P("col", "row", None),
            P("col", None, "row"),
            P("row", "col"),
            P("row", "col"),
            P("col", "row"),
        ),
        out_specs=(
            P("row", "col"),
            P("row", "col"),
            P("col"),
            P("row", "col"),
            P("row", "col"),
            P(),
            P("row", "col"),
            P("col", "row"),
            P("col"),
            P("row", None),
            P("col", "row", None),
            P("col", "row", None),
            P("col", None, "row"),
            P("row", "col"),
            P("row", "col"),
            P("col", "row"),
        ),
        check_vma=False,
    )
```

```python
import functools

import jax
import jax.numpy as jnp
from jax import lax
from jax.experimental import pallas as pl
from jax.experimental.pallas import tpu as pltpu
from jax.sharding import PartitionSpec as P

NOPE = 128
ROPE = 64
VD = 128
LATENT = 512
LEN = 1024
WINDOW = 1024
EPSILON = 1e-06
LANES = 128
MESH = pl.DeviceIdType.MESH
BF16 = jnp.bfloat16
F32 = jnp.float32
UP, DOWN, SIDE, CORE = range(4)


def dot_nn(a, b):
    return jnp.dot(a, b, preferred_element_type=F32)


def dot_nt(a, b):
    return lax.dot_general(a, b, (((1,), (1,)), ((), ())), preferred_element_type=F32)


def dot_tn(a, b):
    return lax.dot_general(a, b, (((0,), (0,)), ((), ())), preferred_element_type=F32)


def place():
    me = lax.axis_index("col")
    return lax.axis_index("row"), me // 4, (me // 2) % 2, me % 2


def col_of(z, y, c):
    return z * 4 + y * 2 + c


def rolled(index, row, n_row, count):
    return lax.rem(index + count - row * (count // n_row), count)


def signal(row, target):
    pl.semaphore_signal(
        pltpu.get_barrier_semaphore(), inc=1, device_id=(row, target), device_id_type=MESH
    )


def greet_row(row, me, n_row):
    for t in range(1, n_row):
        signal(lax.rem(row + t, n_row), me)
    pl.semaphore_wait(pltpu.get_barrier_semaphore(), n_row - 1)


def greet_neighbours(row, z, y, c, depth, n_row=1):
    for t in range(1, n_row):
        signal(lax.rem(row + t, n_row), col_of(z, y, c))
    signal(row, col_of(z, 1 - y, c))
    signal(row, col_of(z, y, 1 - c))

    @pl.when(z > 0)
    def _():
        signal(row, col_of(z - 1, y, c))

    @pl.when(z < depth - 1)
    def _():
        signal(row, col_of(z + 1, y, c))

    count = 1 + n_row + (z > 0).astype(jnp.int32) + (z < depth - 1).astype(jnp.int32)
    pl.semaphore_wait(pltpu.get_barrier_semaphore(), count)


def swap_copy(row, me, n_row, source, target, t, send_sem, recv_sem):
    return pltpu.make_async_remote_copy(
        src_ref=source, dst_ref=target, send_sem=send_sem, recv_sem=recv_sem,
        device_id=(lax.rem(row + t, n_row), me), device_id_type=MESH,
    )


def greet_all(row, me, n, n_row=1):
    for t in range(1, n_row):
        signal(lax.rem(row + t, n_row), me)

    def hello(step, carry):
        signal(row, lax.rem(me + step, n))
        return carry

    lax.fori_loop(1, n, hello, 0)
    pl.semaphore_wait(pltpu.get_barrier_semaphore(), n + n_row - 2)


def gather_kernel(depth, n_row, pieces, count, *refs):
    ins, outs = refs[:count], refs[count : 2 * count]
    local_sem, send_sem, recv_sem = refs[2 * count :]
    row, z, y, c = place()
    me, n = col_of(z, y, c), 4 * depth
    greet_neighbours(row, z, y, c, depth)

    def lanes(block):
        return pl.ds(pl.multiple_of(rolled(block, row, n_row, n) * LANES, LANES), LANES)

    keeps = [
        pltpu.make_async_copy(ins[a], outs[a].at[:, lanes(me)], local_sem.at[a])
        for a in range(count)
    ]
    for keep in keeps:
        keep.start()

    def copy(way, block, piece, target, own=False):
        a, first, size = pieces[piece]
        rows = pl.ds(first, size)
        slot = lanes(block)
        return pltpu.make_async_remote_copy(
            src_ref=ins[a].at[rows] if own else outs[a].at[rows, slot],
            dst_ref=outs[a].at[rows, slot],
            send_sem=send_sem.at[way, block, piece],
            recv_sem=recv_sem.at[block, piece],
            device_id=(row, target),
            device_id_type=MESH,
        )

    def start(way, block, piece, target, own=False):
        copy(way, block, piece, target, own).start()

    def finish(way, block, piece, target, own=False):
        copy(way, block, piece, target, own).wait_send()

    def arrive(block, piece):
        copy(CORE, block, piece, me).wait_recv()

    up, down = col_of(z + 1, y, c), col_of(z - 1, y, c)
    side, core = col_of(z, 1 - y, c), col_of(z, y, 1 - c)

    def line(d, p, act):
        if d == 0:
            act(SIDE, me, p, side, True)

            @pl.when(z + 1 < depth)
            def _():
                act(UP, me, p, up, True)

            @pl.when(z > 0)
            def _():
                act(DOWN, me, p, down, True)

            act(CORE, me, p, core, True)
            return

        @pl.when(z - d >= 0)
        def _():
            block = col_of(z - d, y, c)
            if act is start:
                arrive(block, p)

            @pl.when(z + 1 < depth)
            def _():
                act(UP, block, p, up)

            act(SIDE, block, p, side)
            act(CORE, block, p, core)

        @pl.when(z + d < depth)
        def _():
            block = col_of(z + d, y, c)
            if act is start:
                arrive(block, p)

            @pl.when(z > 0)
            def _():
                act(DOWN, block, p, down)

            act(SIDE, block, p, side)
            act(CORE, block, p, core)

    def sides(d, p, act):
        for sign in (-1, 1) if d else (1,):
            at = z + sign * d

            @pl.when((at >= 0) & (at < depth))
            def _():
                block = col_of(at, 1 - y, c)
                if act is start:
                    arrive(block, p)
                act(CORE, block, p, core)

    span = range(len(pieces))
    for d in range(depth):
        for p in span:
            line(d, p, start)
        if d:
            for p in span:
                sides(d - 1, p, start)
    for p in span:
        sides(depth - 1, p, start)
    for p in span:
        for zz in range(depth):
            for yy in range(2):
                arrive(col_of(zz, yy, 1 - c), p)
    for d in range(depth):
        for p in span:
            line(d, p, finish)
            sides(d, p, finish)
    for keep in keeps:
        keep.wait()


def gather_cols(arrays, parts, collective_id):
    n, n_row = lax.axis_size("col"), lax.axis_size("row")
    pieces = []
    for a, array in enumerate(arrays):
        cuts = parts if array.shape[0] >= 1024 else 1
        size = array.shape[0] // cuts
        pieces += [(a, i * size, size) for i in range(cuts)]
    pieces.sort(key=lambda piece: (arrays[piece[0]].shape[0], piece[1]))
    count = len(arrays)
    anywhere = pl.BlockSpec(memory_space=pl.ANY)
    return pl.pallas_call(
        functools.partial(gather_kernel, n // 4, n_row, tuple(pieces), count),
        out_shape=[jax.ShapeDtypeStruct((a.shape[0], n * LANES), a.dtype) for a in arrays],
        in_specs=[anywhere] * count,
        out_specs=[anywhere] * count,
        scratch_shapes=[
            pltpu.SemaphoreType.DMA((count,)),
            pltpu.SemaphoreType.DMA((4, n, len(pieces))),
            pltpu.SemaphoreType.DMA((n, len(pieces))),
        ],
        compiler_params=pltpu.CompilerParams(collective_id=collective_id, has_side_effects=True),
        name="gather_cols",
    )(*arrays)


def scatter_kernel(depth, n_row, parts, kinds, has_stat, has_extra, shifts, *refs):
    count = 2 * len(kinds) + has_stat + has_extra
    extra = refs[count - 1 - has_stat] if has_extra else None
    operands, stat = refs[: 2 * len(kinds)], refs[count - 1] if has_stat else None
    swaps_in, refs = refs[count : count + len(shifts)], refs[count + len(shifts) :]
    out = refs[0]
    extra_out = refs[1] if has_extra else None
    refs = refs[has_extra:]
    stats = refs[1] if has_stat else None
    swaps_out = refs[1 + has_stat : 1 + has_stat + len(shifts)]
    rest = refs[1 + has_stat + len(shifts) :]
    mine, core_send, core_recv, side_send, side_recv, line_send, line_recv = rest[:7]
    cs, cr, ss, sr, ls, lr = rest[7:13]
    extra_core, extra_side_send, extra_side, extra_line_send, extra_line = rest[-7:-2] if has_extra else [None] * 5
    row, z, y, c = place()
    me, n = col_of(z, y, c), 4 * depth
    pairs = 2 * depth
    rows = out.shape[0]
    size = rows // parts
    tile = min(256, size)
    if has_stat:
        stat_held, stat_send, stat_recv = rest[13:16]
        greet_all(row, me, n, n_row if shifts else 1)

        def stat_copy(step):
            target = lax.rem(me + step, n)
            return pltpu.make_async_remote_copy(
                src_ref=stat,
                dst_ref=stat_held.at[me],
                send_sem=stat_send.at[step],
                recv_sem=stat_recv.at[me],
                device_id=(row, target),
                device_id_type=MESH,
            )

        for step in range(1, n):
            stat_copy(step).start()
    else:
        greet_neighbours(row, z, y, c, depth, n_row if shifts else 1)
    swaps = [
        swap_copy(row, me, n_row, a, b, t, rest[-2].at[i], rest[-1].at[i])
        for i, (a, b, t) in enumerate(zip(swaps_in, swaps_out, shifts))
    ]
    for swap in swaps:
        swap.start()
    up, down = col_of(z + 1, y, c), col_of(z - 1, y, c)
    side, core = col_of(z, 1 - y, c), col_of(z, y, 1 - c)

    def remote(src, dst, send, recv, target):
        return pltpu.make_async_remote_copy(
            src_ref=src, dst_ref=dst, send_sem=send, recv_sem=recv,
            device_id=(row, target), device_id_type=MESH,
        )

    def span(h):
        return pl.ds(h * size, size)

    def block_of(s, cc):
        return col_of(order(s % depth), 1 - y if s < depth else y, cc)

    def extra_rows(s, cc):
        size = extra.shape[0] // n
        return extra.at[pl.ds(pl.multiple_of(block_of(s, cc) * size, 16), size)]

    def mine_at(s, h):
        return mine.at[s, span(h)] if h < parts else extra_rows(s, c)

    def core_recv_at(s, h):
        return core_recv.at[s, span(h)] if h < parts else extra_core.at[s]

    def side_send_at(k, h):
        return side_send.at[k, span(h)] if h < parts else extra_side_send.at[k]

    def side_recv_at(k, h):
        return side_recv.at[k, span(h)] if h < parts else extra_side.at[k]

    def line_send_at(zz, h):
        return line_send.at[zz, span(h)] if h < parts else extra_line_send.at[zz]

    def line_recv_at(way, zz, h):
        return line_recv.at[way, zz, span(h)] if h < parts else extra_line.at[way, zz]

    def out_at(h):
        return out.at[span(h)] if h < parts else extra_out

    def core_copy(s, h):
        source = core_send.at[s, span(h)] if h < parts else extra_rows(s, 1 - c)
        return remote(source, core_recv_at(s, h), cs.at[s, h], cr.at[s, h], core)

    def side_copy(k, h):
        return remote(side_send_at(k, h), side_recv_at(k, h), ss.at[k, h], sr.at[k, h], side)

    def line_copy(way, zz, h, target):
        return remote(
            line_send_at(zz, h), line_recv_at(way, zz, h), ls.at[zz, h], lr.at[way, zz, h], target
        )

    low_half = z < depth // 2

    def order(k):
        if k == depth - 1:
            return z
        from_top = depth - 1 - k
        from_top = from_top - (from_top <= z).astype(jnp.int32)
        from_low = k + (k >= z).astype(jnp.int32)
        return jnp.where(low_half, from_top, from_low)

    def tiles(body):
        def step(i, carry):
            body(i)
            return carry

        lax.fori_loop(0, size // tile, step, 0)

    def multiply(s, h):
        if h == parts:
            core_copy(s, h).start()
            return
        yy = 1 - y if s < depth else y
        pair = rolled(order(s % depth) * 2 + yy, row, n_row, pairs)
        cols = pl.ds(pl.multiple_of(pair * 2 * LANES, 2 * LANES), 2 * LANES)

        def body(i):
            at = pl.ds(pl.multiple_of(h * size + i * tile, tile), tile)
            total = None
            for j, kind in enumerate(kinds):
                left, right = operands[2 * j], operands[2 * j + 1]
                if kind == "nn":
                    term = dot_nn(left[at, :], right[:, cols])
                elif kind == "tn":
                    term = dot_tn(left[:, at], right[:, cols])
                else:
                    term = dot_nt(left[at, :], right[cols, :])
                total = term if total is None else total + term
            first, second = total[:, :LANES], total[:, LANES:]
            mine[s, at, :] = jnp.where(c == 0, first, second).astype(BF16)
            core_send[s, at, :] = jnp.where(c == 0, second, first).astype(BF16)

        tiles(body)
        core_copy(s, h).start()

    def add_up(target, sources):
        step = min(tile, target.shape[0])

        def body(i, carry):
            at = pl.ds(pl.multiple_of(i * step, step), step)
            total = sources[0][at, :].astype(F32)
            for source in sources[1:]:
                total = total + source[at, :].astype(F32)
            target[at, :] = total.astype(target.dtype)
            return carry

        lax.fori_loop(0, target.shape[0] // step, body, 0)

    def fold(s, h):
        core_copy(s, h).wait_recv()
        k = s % depth
        sources = [mine_at(s, h), core_recv_at(s, h)]
        if s < depth:
            add_up(side_send_at(k, h), sources)
            side_copy(k, h).start()
            return
        side_copy(k, h).wait_recv()
        sources.append(side_recv_at(k, h))
        zz = order(k)
        if k < depth - 1:

            @pl.when(zz > z)
            def _():
                @pl.when(z > 0)
                def _():
                    line_copy(0, zz, h, up).wait_recv()
                    add_up(line_send_at(zz, h), sources + [line_recv_at(0, zz, h)])

                @pl.when(z == 0)
                def _():
                    add_up(line_send_at(zz, h), sources)

                line_copy(0, zz, h, up).start()

            @pl.when(zz < z)
            def _():
                @pl.when(z < depth - 1)
                def _():
                    line_copy(1, zz, h, down).wait_recv()
                    add_up(line_send_at(zz, h), sources + [line_recv_at(1, zz, h)])

                @pl.when(z == depth - 1)
                def _():
                    add_up(line_send_at(zz, h), sources)

                line_copy(1, zz, h, down).start()

            return

        @pl.when((z > 0) & (z < depth - 1))
        def _():
            line_copy(0, z, h, me).wait_recv()
            line_copy(1, z, h, me).wait_recv()
            add_up(out_at(h), sources + [line_recv_at(0, z, h), line_recv_at(1, z, h)])

        @pl.when(z == 0)
        def _():
            line_copy(1, z, h, me).wait_recv()
            add_up(out_at(h), sources + [line_recv_at(1, z, h)])

        @pl.when(z == depth - 1)
        def _():
            line_copy(0, z, h, me).wait_recv()
            add_up(out_at(h), sources + [line_recv_at(0, z, h)])

    chunks = parts + has_extra
    steps = [(s, h) for s in range(2 * depth) for h in range(chunks)]
    for i, (s, h) in enumerate(steps):
        multiply(s, h)
        if i >= 2:
            fold(*steps[i - 2])
    for s, h in steps[-2:]:
        fold(s, h)
    for s, h in steps:
        core_copy(s, h).wait_send()
    for k in range(depth):
        for h in range(chunks):
            side_copy(k, h).wait_send()
    for k in range(depth - 1):
        zz = order(k)
        for h in range(chunks):
            line_copy(0, zz, h, me).wait_send()
    if has_stat:
        stat_held[me] = stat[...]
        for step in range(1, n):
            stat_copy(step).wait_send()
            source = lax.rem(me + step, n)
            remote(stat, stat_held.at[source], stat_send.at[step], stat_recv.at[source], me).wait_recv()
        stats[...] = stat_held[...]
    for swap in swaps:
        swap.wait()


def scatter_cols(products, stat, parts, collective_id, swaps=(), extra=None):
    n, n_row = lax.axis_size("col"), lax.axis_size("row")
    depth = n // 4
    chunks = parts + (extra is not None)
    kinds = tuple(kind for kind, _, _ in products)
    operands = [x for _, a, b in products for x in (a, b)]
    rows = operands[0].shape[kinds[0] == "tn"]
    in_vmem = pl.BlockSpec(memory_space=pltpu.VMEM)
    out_shape = [jax.ShapeDtypeStruct((rows, LANES), F32)]
    dma = pltpu.SemaphoreType.DMA
    scratch = [
        pltpu.VMEM((2 * depth, rows, LANES), BF16),
        pltpu.VMEM((2 * depth, rows, LANES), BF16),
        pltpu.VMEM((2 * depth, rows, LANES), BF16),
        pltpu.VMEM((depth, rows, LANES), BF16),
        pltpu.VMEM((depth, rows, LANES), BF16),
        pltpu.VMEM((depth, rows, LANES), BF16),
        pltpu.VMEM((2, depth, rows, LANES), BF16),
        dma((2 * depth, chunks)),
        dma((2 * depth, chunks)),
        dma((depth, chunks)),
        dma((depth, chunks)),
        dma((depth, chunks)),
        dma((2, depth, chunks)),
    ]
    if extra is not None:
        operands.append(extra)
        block = (extra.shape[0] // n, extra.shape[1])
        out_shape.append(jax.ShapeDtypeStruct(block, F32))
    if stat is not None:
        operands.append(stat)
        out_shape.append(jax.ShapeDtypeStruct((n,) + stat.shape, F32))
        scratch += [pltpu.VMEM((n,) + stat.shape, F32), dma((n,)), dma((n,))]
    held = [in_vmem] * len(operands)
    kept = [in_vmem] * len(out_shape)
    anywhere = pl.BlockSpec(memory_space=pl.ANY)
    if extra is not None:
        scratch += [
            pltpu.VMEM((2 * depth,) + block, BF16),
            pltpu.VMEM((depth,) + block, BF16),
            pltpu.VMEM((depth,) + block, BF16),
            pltpu.VMEM((depth,) + block, BF16),
            pltpu.VMEM((2, depth) + block, BF16),
        ]
    if swaps:
        operands += [array for array, _ in swaps]
        held += [anywhere] * len(swaps)
        kept += [anywhere] * len(swaps)
        out_shape += [jax.ShapeDtypeStruct(array.shape, array.dtype) for array, _ in swaps]
    scratch += [dma((max(1, len(swaps)),)), dma((max(1, len(swaps)),))]
    shifts = tuple(t for _, t in swaps)
    return pl.pallas_call(
        functools.partial(scatter_kernel, depth, n_row, parts, kinds, stat is not None, extra is not None, shifts),
        out_shape=out_shape,
        in_specs=held,
        out_specs=kept,
        scratch_shapes=scratch,
        compiler_params=pltpu.CompilerParams(
            collective_id=collective_id, has_side_effects=True, vmem_limit_bytes=60 << 20
        ),
        name="scatter_cols",
    )(*operands)


def gather_steps(row, z, y, c, depth, pieces, send_sem, recv_sem):
    n = 4 * depth
    me = col_of(z, y, c)
    up, down = col_of(z + 1, y, c), col_of(z - 1, y, c)
    side, core = col_of(z, 1 - y, c), col_of(z, y, 1 - c)

    def copy(way, block, p, target, own=False):
        source, spot = pieces[p]
        index = block // 4 + way * depth if way < CORE else 3 * depth + block // 2
        return pltpu.make_async_remote_copy(
            src_ref=source if own else spot(block),
            dst_ref=spot(block),
            send_sem=send_sem.at[p, index],
            recv_sem=recv_sem.at[p, block],
            device_id=(row, target),
            device_id_type=MESH,
        )

    def start(way, block, p, target, own=False):
        copy(way, block, p, target, own).start()

    def finish(way, block, p, target, own=False):
        copy(way, block, p, target, own).wait_send()

    def arrive(block, p):
        copy(CORE, block, p, me).wait_recv()

    def line(d, p, act):
        if d == 0:
            act(SIDE, me, p, side, True)

            @pl.when(z + 1 < depth)
            def _():
                act(UP, me, p, up, True)

            @pl.when(z > 0)
            def _():
                act(DOWN, me, p, down, True)

            act(CORE, me, p, core, True)
            return

        @pl.when(z - d >= 0)
        def _():
            block = col_of(z - d, y, c)
            if act is start:
                arrive(block, p)

            @pl.when(z + 1 < depth)
            def _():
                act(UP, block, p, up)

            act(SIDE, block, p, side)
            act(CORE, block, p, core)

        @pl.when(z + d < depth)
        def _():
            block = col_of(z + d, y, c)
            if act is start:
                arrive(block, p)

            @pl.when(z > 0)
            def _():
                act(DOWN, block, p, down)

            act(SIDE, block, p, side)
            act(CORE, block, p, core)

    def sides(d, p, act):
        for sign in (-1, 1) if d else (1,):
            at = z + sign * d

            @pl.when((at >= 0) & (at < depth))
            def _():
                block = col_of(at, 1 - y, c)
                if act is start:
                    arrive(block, p)
                act(CORE, block, p, core)

    count = len(pieces)
    for wave in range(count + depth + 1):
        for p in range(count):
            k = wave - p
            if k == -1 or (wave == 0 and p == 0):
                line(0, p, start)
            if 1 <= k < depth:
                line(k, p, start)
                sides(k - 1, p, start)
            if k == depth:
                sides(depth - 1, p, start)
            if k == depth + 1:
                for zz in range(depth):
                    for yy in range(2):
                        arrive(col_of(zz, yy, 1 - c), p)
                yield p
            elif 0 <= k <= depth:
                yield None
    for p in range(count):
        for d in range(depth):
            line(d, p, finish)
            sides(d, p, finish)


def work_through(steps, ready):
    tasks = []
    for p in steps:
        if p is not None:
            tasks += ready(p)
        if tasks:
            tasks.pop(0)()
    for task in tasks:
        task()


def rotary_tables():
    position = jnp.arange(LEN, dtype=jnp.int32).astype(F32)
    frequency = 10000.0 ** (-jnp.arange(ROPE // 2).astype(F32) * 2.0 / ROPE)
    angles = position[:, None] * frequency[None, :]
    cosines, sines = jnp.cos(angles), jnp.sin(angles)
    return (
        jnp.concatenate([cosines] * 4, 1),
        jnp.concatenate([-sines, sines, sines, -sines], 1),
    )


def with_exchanged(array):
    half = ROPE // 2
    return jnp.concatenate([array, array[:, -half:], array[:, -ROPE:-half]], 1)


def turn(tile, cosines, sines):
    return tile * cosines + pltpu.roll(tile, ROPE, 1) * sines


def spread(columns, like):
    return jnp.broadcast_to(columns, like.shape)


SCALE = (NOPE + ROPE) ** (-0.5)
QK = NOPE + ROPE
TILE = 256


def masked_scores(q, k, seg_col, seg_row, base, first, length):
    scores = dot_nt(q[pl.ds(base + first, TILE), :QK], k[pl.ds(base, length), :QK]) * SCALE
    here = first + lax.broadcasted_iota(jnp.int32, (TILE, length), 0)
    there = lax.broadcasted_iota(jnp.int32, (TILE, length), 1)
    allowed = (here >= there) & (
        seg_col[pl.ds(base + first, TILE), :1] == seg_row[:1, pl.ds(base, length)]
    )
    if WINDOW < LEN:
        allowed = allowed & (here - there < WINDOW)
    return jnp.where(allowed, scores, -1e30)


def forward_kernel(depth, n_row, sizes, shifts, *refs):
    (tokens, gain, query_own, down_own, up_own, choose, latent_gain, cosines, sines, seg_col, seg_row) = refs[:11]
    swaps_in, refs = refs[11 : 11 + len(shifts)], refs[11 + len(shifts) :]
    outs, swaps_out, refs = refs[:13], refs[13 : 13 + len(shifts)], refs[13 + len(shifts) :]
    (full, gains, held, query_full, down_mine, down_full, up_full) = refs[:7]
    (q, k, v, latent, low, first_root, latent_root, mixed, lse) = refs[7:16]
    (send_sem, recv_sem, swap_send, swap_recv, local_sem, out_sem, weight_sem, late_send, late_recv) = refs[16:]
    results = (held, q, k, v, latent, low, first_root, latent_root, mixed, lse)
    rows, width, seqs = sizes
    row, z, y, c = place()
    me, n = col_of(z, y, c), 4 * depth
    greet_neighbours(row, z, y, c, depth, n_row)
    share = width // n_row
    up_rows = up_own.shape[0]
    down_rows = down_own.shape[0]

    def part(s):
        return pl.ds(s * share, share)

    swaps = []
    for i, (source, spot) in enumerate(
        [
            (down_own, lambda slot: down_mine.at[:, part(slot)]),
            (query_own, lambda slot: query_full.at[part(slot)]),
        ]
    ):
        swaps.append(
            [
                swap_copy(row, me, n_row, source, spot(n_row - t), t, swap_send.at[i, t], swap_recv.at[i, t])
                for t in range(1, n_row)
            ]
        )
    own_up = pl.ds(pl.multiple_of(row * up_rows, up_rows), up_rows)
    swaps.append(
        [
            swap_copy(row, me, n_row, up_own, up_full.at[own_up], t, swap_send.at[2, t], swap_recv.at[2, t])
            for t in range(1, n_row)
        ]
    )
    for group in swaps:
        for swap in group:
            swap.start()
    late = [
        swap_copy(row, me, n_row, a, b, t, late_send.at[i], late_recv.at[i])
        for i, (a, b, t) in enumerate(zip(swaps_in, swaps_out, shifts))
    ]
    for swap in late:
        swap.start()

    def lanes(block):
        return pl.ds(pl.multiple_of(rolled(block, row, n_row, n) * LANES, LANES), LANES)

    locals_ = [
        pltpu.make_async_copy(down_own, down_mine.at[:, part(0)], local_sem.at[0]),
        pltpu.make_async_copy(query_own, query_full.at[part(0)], local_sem.at[1]),
        pltpu.make_async_copy(up_own, up_full.at[own_up], local_sem.at[2]),
        pltpu.make_async_copy(gain, gains.at[:, lanes(me)], local_sem.at[3]),
        pltpu.make_async_copy(tokens, full.at[:, lanes(me)], local_sem.at[4]),
    ]
    for copy in locals_:
        copy.start()
    pieces = [(gain, lambda block: gains.at[:, lanes(block)])]
    tile_pieces = []
    for first in range(0, rows, TILE):
        span = pl.ds(first, TILE)
        pieces.append((tokens.at[span], lambda block, span=span: full.at[span, lanes(block)]))
        tile_pieces.append(len(pieces) - 1)
    down_piece = 2
    pieces.insert(
        down_piece,
        (down_mine, lambda block: down_full.at[pl.ds(pl.multiple_of(block * down_rows, 16), down_rows)]),
    )
    tile_pieces = [p + (p >= down_piece) for p in tile_pieces]
    locals_[0].wait()
    for swap in swaps[0]:
        swap.wait_recv()
    keep_down = pltpu.make_async_copy(
        down_mine, down_full.at[pl.ds(pl.multiple_of(me * down_rows, 16), down_rows)], local_sem.at[5]
    )
    keep_down.start()

    def keep(array, seq):
        span = pl.ds(seq * LEN, LEN)
        return pltpu.make_async_copy(results[array].at[span], outs[array].at[span], out_sem.at[array, seq])

    def keep_some(arrays, seq):
        for array in arrays:
            keep(array, seq).start()

    weights_out = [
        pltpu.make_async_copy(source, target, weight_sem.at[i])
        for i, (source, target) in enumerate(zip((query_full, down_full, up_full), outs[10:]))
    ]

    def project(i):
        span = pl.ds(i * TILE, TILE)
        x = full[span, :].astype(F32)
        root = lax.rsqrt(jnp.sum(x * x, 1, keepdims=True) / width + EPSILON)
        first_root[span, :] = jnp.broadcast_to(root, (TILE, LANES))
        held[span, :] = (x * root * gains[:1, :]).astype(BF16)

    def project_more(i):
        span = pl.ds(i * TILE, TILE)
        at = pl.ds((i * TILE) % LEN, TILE)
        cos, sin = cosines[at, :], sines[at, :]
        xn = held[span, :]
        pre = dot_nn(xn, query_full[...])
        q[span, :NOPE] = pre[:, :NOPE].astype(BF16)
        q[span, NOPE:] = turn(pre[:, NOPE:], cos, sin).astype(BF16)
        wide = dot_nt(xn, down_full[...]).astype(BF16)
        chosen = dot_nn(wide, choose[...])
        low[span, :] = chosen.astype(BF16)
        compressed = chosen[:, :LATENT]
        root = lax.rsqrt(jnp.mean(compressed * compressed, 1, keepdims=True) + EPSILON)
        latent_root[span, :] = jnp.broadcast_to(root, (TILE, LANES))
        lat = (compressed * root * latent_gain[:1, :]).astype(BF16)
        latent[span, :] = lat
        expanded = dot_nn(lat, up_full[...]).astype(BF16)
        k[span, :NOPE] = expanded[:, :NOPE]
        k[span, NOPE:] = turn(chosen[:, LATENT:], cos, sin).astype(BF16)
        v[span, :] = expanded[:, NOPE:]

    def attend(seq, block):
        base, first = seq * LEN, block * TILE
        length = first + TILE
        scores = masked_scores(q, k, seg_col, seg_row, base, first, length)
        top = jnp.max(scores, -1, keepdims=True)
        weights = jnp.exp(scores - top)
        total = jnp.sum(weights, -1, keepdims=True)
        probs = (weights / total).astype(BF16)
        span = pl.ds(base + first, TILE)
        mixed[span, :] = dot_nn(probs, v[pl.ds(base, length), :]).astype(BF16)
        lse[span, :] = jnp.broadcast_to(top + jnp.log(total), (TILE, LANES))

    state = {"weights": False}
    per_seq = LEN // TILE
    waiting = []

    def weights_here():
        keep_down.wait()
        for copy in locals_[1:3]:
            copy.wait()
        for group in swaps[1:]:
            for swap in group:
                swap.wait_recv()
        for copy in weights_out:
            copy.start()

    def ready(p):
        tasks = []
        if p == 0:
            tasks.append(lambda: [copy.wait() for copy in locals_[3:]])
        if p == down_piece:
            tasks.append(weights_here)
            state["weights"] = True
        if p in tile_pieces:
            i = tile_pieces.index(p)
            tasks.append(functools.partial(project, i))
            waiting.append(i)
        if state["weights"]:
            for i in waiting:
                tasks.append(functools.partial(project_more, i))
                if i % per_seq == per_seq - 1:
                    seq = i // per_seq
                    tasks.append(functools.partial(keep_some, range(8), seq))
                    tasks.extend(functools.partial(attend, seq, b) for b in range(per_seq))
                    tasks.append(functools.partial(keep_some, (8, 9), seq))
            waiting.clear()
        return tasks

    work_through(gather_steps(row, z, y, c, depth, pieces, send_sem, recv_sem), ready)
    for group in swaps:
        for swap in group:
            swap.wait_send()
    for copy in weights_out:
        copy.wait()
    for seq in range(seqs):
        for array in range(10):
            keep(array, seq).wait()
    for swap in late:
        swap.wait()


def attention_forward(
    tokens, gain, query_own, down_own, up_own, choose, latent_gain, tables, seg_col, seg_row, collective_id, swaps=()
):
    n, n_row = lax.axis_size("col"), lax.axis_size("row")
    depth, rows = n // 4, tokens.shape[0]
    width, seqs = n * tokens.shape[1], rows // LEN
    padded = n * down_own.shape[0]
    in_vmem = pl.BlockSpec(memory_space=pltpu.VMEM)
    anywhere = pl.BlockSpec(memory_space=pl.ANY)
    count = 2 + rows // TILE
    dma = pltpu.SemaphoreType.DMA
    shape = jax.ShapeDtypeStruct
    kept = [
        shape((rows, 2 * LANES), BF16),
        shape((rows, 2 * LANES), BF16),
        shape((rows, VD), BF16),
        shape((rows, LATENT), BF16),
        shape((rows, LATENT + LANES), BF16),
        shape((rows, LANES), F32),
        shape((rows, LANES), F32),
        shape((rows, VD), BF16),
        shape((rows, LANES), F32),
    ]
    swapped = [array for array, _ in swaps]
    return pl.pallas_call(
        functools.partial(
            forward_kernel, depth, n_row, (rows, width, seqs), tuple(t for _, t in swaps)
        ),
        out_shape=[shape((rows, width), BF16)]
        + kept
        + [
            shape((width, 2 * LANES), BF16),
            shape((padded, width), BF16),
            shape((LATENT, 2 * LANES), BF16),
        ]
        + [shape(a.shape, a.dtype) for a in swapped],
        in_specs=[anywhere] * 5 + [in_vmem] * 6 + [anywhere] * len(swapped),
        out_specs=[anywhere] * (13 + len(swapped)),
        scratch_shapes=[
            pltpu.VMEM((rows, width), BF16),
            pltpu.VMEM((gain.shape[0], width), F32),
            pltpu.VMEM((rows, width), BF16),
            pltpu.VMEM((width, 2 * LANES), BF16),
            pltpu.VMEM((down_own.shape[0], width), BF16),
            pltpu.VMEM((padded, width), BF16),
            pltpu.VMEM((LATENT, 2 * LANES), BF16),
        ]
        + [pltpu.VMEM(a.shape, a.dtype) for a in kept]
        + [
            dma((count, 5 * depth)),
            dma((count, n)),
            dma((3, n_row)),
            dma((3, n_row)),
            dma((6,)),
            dma((10, seqs)),
            dma((3,)),
            dma((max(1, len(swapped)),)),
            dma((max(1, len(swapped)),)),
        ],
        compiler_params=pltpu.CompilerParams(
            collective_id=collective_id, has_side_effects=True, vmem_limit_bytes=60 << 20
        ),
        name="attention_forward",
    )(tokens, gain, query_own, down_own, up_own, choose, latent_gain, *tables, seg_col, seg_row, *swapped)


def backward_kernel(depth, n_row, sizes, shifts, *refs):
    grad, loads, refs = refs[0], refs[1:17], refs[17:]
    swaps_in, refs = refs[: len(shifts)], refs[len(shifts) :]
    (gain_back, out_back), outs, refs = refs[:2], refs[2:7], refs[7:]
    swaps_out, refs = refs[: len(shifts)], refs[len(shifts) :]
    held, refs = refs[:16], refs[16:]
    (out_full, q, k, v, latent, low, latent_root, mixed, lse, up_full, choose, latent_gain) = held[:12]
    (cosines, sines, seg_col, seg_row) = held[12:]
    (query_back, low_back, low_wide, expanded_back, inner), refs = refs[:5], refs[5:]
    results = (query_back, low_back, low_wide, expanded_back, inner)
    (full, keys_back, values_back, send_sem, recv_sem, local_sem, load_sem, out_sem, swap_send, swap_recv) = refs
    rows, width, seqs = sizes
    row, z, y, c = place()
    me, n = col_of(z, y, c), 4 * depth
    greet_neighbours(row, z, y, c, depth, n_row if shifts else 1)
    swaps = [
        swap_copy(row, me, n_row, a, b, t, swap_send.at[i], swap_recv.at[i])
        for i, (a, b, t) in enumerate(zip(swaps_in, swaps_out, shifts))
    ]

    def lanes(block):
        return pl.ds(pl.multiple_of(rolled(block, row, n_row, n) * LANES, LANES), LANES)

    keep = pltpu.make_async_copy(grad, full.at[:, lanes(me)], local_sem)
    keep.start()
    fetches = [
        pltpu.make_async_copy(a, b, load_sem.at[i]) for i, (a, b) in enumerate(zip(loads, held))
    ]

    def result(array, seq):
        span = pl.ds(seq * LEN, LEN)
        span = (slice(None), span) if array == 2 else (span,)
        return pltpu.make_async_copy(results[array].at[span], outs[array].at[span], out_sem.at[array, seq])

    def store(seq):
        for array in range(5):
            result(array, seq).start()

    pieces = []
    for first in range(0, rows, TILE):
        span = pl.ds(first, TILE)
        pieces.append((grad.at[span], lambda block, span=span: full.at[span, lanes(block)]))
    per_seq = LEN // TILE
    lower = lax.broadcasted_iota(jnp.int32, (TILE, LANES), 1) < ROPE

    def begin():
        keep.wait()
        for fetch in fetches:
            fetch.wait()
        gain_back[...] = jnp.zeros_like(gain_back)
        out_back[...] = jnp.zeros_like(out_back)

    def attend(seq, block):
        base, first = seq * LEN, block * TILE
        length = first + TILE
        span, keys = pl.ds(base + first, TILE), pl.ds(base, length)
        at = pl.ds(first, TILE)
        grad_rows = full[span, :]
        out_back[...] += dot_tn(mixed[span, :], grad_rows)
        grad_mixed = dot_nt(grad_rows, out_full[...]).astype(BF16)
        scores = masked_scores(q, k, seg_col, seg_row, base, first, length)
        probs = jnp.exp(scores - lse[span, :1])
        grad_probs = dot_nt(grad_mixed, v[keys, :])
        grad_scores = (
            probs * (grad_probs - jnp.sum(probs * grad_probs, -1, keepdims=True))
        ).astype(BF16)
        back = dot_nn(grad_scores, k[keys, :]) * SCALE
        nope, tile = back[:, :NOPE], back[:, NOPE:]
        inner[span, :] = jnp.broadcast_to(
            jnp.sum(nope * q[span, :NOPE].astype(F32), 1, keepdims=True)
            + 0.5 * jnp.sum(tile * q[span, NOPE:].astype(F32), 1, keepdims=True),
            (TILE, LANES),
        )
        query_back[span, :NOPE] = nope.astype(BF16)
        turned = turn(tile, cosines[at, :], -sines[at, :])
        query_back[span, NOPE:] = jnp.where(lower, turned, 0.0).astype(BF16)
        keys_term = dot_tn(grad_scores, q[span, :])
        values_term = dot_tn(probs.astype(BF16), grad_mixed)
        if block == per_seq - 1:
            keys_back[...] = keys_term
            values_back[...] = values_term
        else:
            keys_back[:length, :] += keys_term
            values_back[:length, :] += values_term

    def expand(seq, block):
        first = block * TILE
        span, at = pl.ds(seq * LEN + first, TILE), pl.ds(first, TILE)
        back = keys_back[at, :] * SCALE
        expanded = jnp.concatenate([back[:, :NOPE], values_back[at, :]], 1).astype(BF16)
        expanded_back[span, :] = expanded
        latent_grad = dot_nt(expanded, up_full[...])
        compressed = low[span, :LATENT].astype(F32)
        root = latent_root[span, :1]
        dots = jnp.sum(latent_grad * latent[span, :].astype(F32), 1, keepdims=True)
        gain_back[...] += jnp.broadcast_to(
            jnp.sum(latent_grad * compressed * root, 0, keepdims=True), gain_back.shape
        )
        compressed_grad = root * latent_grad * latent_gain[:1, :] - compressed * (
            root * root * dots / LATENT
        )
        turned = turn(back[:, NOPE:], cosines[at, :], -sines[at, :])
        low_grad = jnp.concatenate([compressed_grad, jnp.where(lower, turned, 0.0)], 1).astype(BF16)
        low_back[span, :] = low_grad
        low_wide[:, span] = dot_nt(choose[...], low_grad).astype(BF16)
        inner[span, :] += jnp.broadcast_to(
            jnp.sum(low_grad.astype(F32) * low[span, :].astype(F32), 1, keepdims=True),
            (TILE, LANES),
        )

    def ready(p):
        tasks = [begin] if p == 0 else []
        if p % per_seq == per_seq - 1:
            seq = p // per_seq
            tasks += [functools.partial(attend, seq, b) for b in reversed(range(per_seq))]
            tasks += [functools.partial(expand, seq, b) for b in range(per_seq)]
            tasks.append(functools.partial(store, seq))
        return tasks

    for swap in swaps:
        swap.start()
    for fetch in fetches:
        fetch.start()
    work_through(gather_steps(row, z, y, c, depth, pieces, send_sem, recv_sem), ready)
    for seq in range(seqs):
        for array in range(5):
            result(array, seq).wait()
    for swap in swaps:
        swap.wait()


def attention_backward(grad, operands, collective_id, swaps=()):
    n, n_row = lax.axis_size("col"), lax.axis_size("row")
    depth, rows = n // 4, grad.shape[0]
    width, seqs = n * grad.shape[1], rows // LEN
    in_vmem = pl.BlockSpec(memory_space=pltpu.VMEM)
    anywhere = pl.BlockSpec(memory_space=pl.ANY)
    count = rows // TILE
    dma = pltpu.SemaphoreType.DMA
    shape = jax.ShapeDtypeStruct
    swapped = [array for array, _ in swaps]
    kept = [
        shape((rows, 2 * LANES), BF16),
        shape((rows, LATENT + LANES), BF16),
        shape((operands[10].shape[0], rows), BF16),
        shape((rows, 2 * LANES), BF16),
        shape((rows, LANES), F32),
    ]
    return pl.pallas_call(
        functools.partial(
            backward_kernel, depth, n_row, (rows, width, seqs), tuple(t for _, t in swaps)
        ),
        out_shape=[shape((8, LATENT), F32), shape((VD, width), F32)]
        + kept
        + [shape(a.shape, a.dtype) for a in swapped],
        in_specs=[anywhere] * (17 + len(swapped)),
        out_specs=[in_vmem] * 2 + [anywhere] * (5 + len(swapped)),
        scratch_shapes=[pltpu.VMEM(a.shape, a.dtype) for a in [*operands, *kept]]
        + [
            pltpu.VMEM((rows, width), BF16),
            pltpu.VMEM((LEN, 2 * LANES), F32),
            pltpu.VMEM((LEN, VD), F32),
            dma((count, 5 * depth)),
            dma((count, n)),
            dma,
            dma((16,)),
            dma((5, seqs)),
            dma((max(1, len(swapped)),)),
            dma((max(1, len(swapped)),)),
        ],
        compiler_params=pltpu.CompilerParams(
            collective_id=collective_id, has_side_effects=True, vmem_limit_bytes=60 << 20
        ),
        name="attention_backward",
    )(grad, *operands, *swapped)


def row_shift(array, step):
    n = lax.axis_size("row")
    return lax.ppermute(array, "row", [(i, (i - step) % n) for i in range(n)])


def to_others(array):
    return [(array, t) for t in range(1, lax.axis_size("row"))]


def row_parts(array):
    return [array] + [row_shift(array, s) for s in range(1, lax.axis_size("row"))]


def row_sum(parts):
    return row_add(parts[0], [part.astype(BF16) for part in parts[1:]])


def row_add(total, parts):
    n = lax.axis_size("row")
    return row_sum_of(total, [row_shift(part, n - s) for s, part in enumerate(parts, 1)])


def row_sum_of(total, received):
    for part in received:
        total = total + part.astype(F32)
    return total


def unroll_parts(parts, axis):
    n = len(parts)
    size = parts[0].shape[axis]
    doubled = jnp.concatenate(parts + parts[:-1], axis)
    start = lax.rem(n - lax.axis_index("row"), n) * size
    return lax.dynamic_slice_in_dim(doubled, start, n * size, axis)


def own_parts(array, axis):
    n = lax.axis_size("row")
    size = array.shape[axis] // n
    row = lax.axis_index("row")
    return [
        lax.dynamic_slice_in_dim(array, lax.rem(row + s, n) * size, size, axis) for s in range(n)
    ]


def own_features(block):
    n, n_row = lax.axis_size("col"), lax.axis_size("row")
    row = lax.axis_index("row")
    moved = [lax.ppermute(block, "col", [(i, (i + s * (n // n_row)) % n) for i in range(n)]) for s in range(1, n_row)]
    for s, other in enumerate(moved, 1):
        block = jnp.where(row == s, other, block)
    return block


def cut(array, axis):
    return jnp.split(array, lax.axis_size("row"), axis)


def silu_slope(values):
    sigmoid = jax.nn.sigmoid(values)
    return sigmoid * (1.0 + values * (1.0 - sigmoid))


def as_stat(*vectors):
    return jnp.concatenate([v.reshape(-1, LANES) for v in vectors], 0)


def per_device(
    tokens,
    cotangent,
    segments,
    routes,
    first_gain,
    query_proj,
    latent_down,
    latent_gain,
    latent_up,
    output_proj,
    second_gain,
    router_weight,
    expert_gate,
    expert_up,
    expert_down,
    shared_gate,
    shared_up,
    shared_down,
):
    row_count, share = tokens.shape
    n = lax.axis_size("col")
    width = share * n
    column = lax.axis_index("col")
    seqs = segments.shape[0]
    narrow = latent_down.shape[1]
    padding = -narrow % 16
    tables = rotary_tables()
    seg_flat = segments.reshape(-1)
    seg_col = jnp.broadcast_to(seg_flat[:, None], (row_count, LANES))
    seg_row = jnp.broadcast_to(seg_flat[None, :], (8, row_count))
    column_of = jnp.arange(n * narrow)
    turned_of = jnp.concatenate([column_of, column_of[LATENT + 32 :], column_of[LATENT : LATENT + 32]])
    wide_of = turned_of // narrow * (narrow + padding) + turned_of % narrow
    choose = (jnp.arange(n * (narrow + padding))[:, None] == wide_of[None, :]).astype(BF16)

    router_full = jnp.concatenate(row_parts(router_weight), 0)
    shared_gate_full = jnp.concatenate(row_parts(shared_gate), 0)
    shared_up_full = jnp.concatenate(row_parts(shared_up), 0)
    shared_down_full = jnp.concatenate(row_parts(shared_down), 1)
    fall_parts = row_parts(expert_down[0])

    latent_gains = jnp.broadcast_to(latent_gain[None, :], (8, LATENT))
    (
        normed,
        queries,
        keys,
        values,
        latent,
        low,
        first_root,
        latent_root,
        mixed,
        log_total,
        query_full,
        down_full,
        up_full,
        *got,
    ) = attention_forward(
        tokens,
        jnp.broadcast_to(first_gain[None, :], (8, share)),
        with_exchanged(query_proj),
        jnp.pad(latent_down.T, ((0, padding), (0, 0))),
        latent_up,
        choose,
        latent_gains,
        tables,
        seg_col,
        seg_row,
        1,
        to_others(output_proj) + to_others(expert_gate[0]),
    )
    others = lax.axis_size("row") - 1
    out_full = jnp.concatenate([output_proj] + got[:others][::-1], 1)
    gate_parts = [expert_gate[0]] + got[others:][::-1]
    first_root = first_root[:, :1]
    cotangent_late, mixed = lax.optimization_barrier((cotangent, mixed))
    grad_natural = lax.all_gather(cotangent_late, "col", axis=1, tiled=True)
    branch, *got = scatter_cols(
        [("nn", mixed, out_full)], None, 2, 2, to_others(expert_up[0])
    )
    lift_parts = [expert_up[0]] + got[::-1]
    hidden = tokens.astype(F32) + branch
    squares = as_stat(jnp.sum(hidden * hidden, 1))
    second_full, square_full = gather_cols(
        [(hidden * second_gain).astype(BF16), squares], 2, 3
    )
    second_root = lax.rsqrt(
        jnp.sum(square_full.reshape(-1, n, LANES), 1).reshape(row_count, 1) / width + EPSILON
    )
    normed_two = (second_full.astype(F32) * second_root).astype(BF16)

    experts = router_full.shape[1]
    logits = dot_nn(normed_two, router_full)
    router_probs = jax.nn.softmax(logits, -1)
    own_expert = jnp.arange(experts) == column
    member = jnp.any(routes == column, 1)
    own_gate = jnp.sum(jnp.where(own_expert[None, :], router_probs, 0.0), 1)
    capacity = row_count * routes.shape[1] * 4 // (3 * experts)
    slot_number = jnp.cumsum(member.astype(jnp.int32)) - 1
    chosen = (slot_number[None, :] == jnp.arange(capacity)[:, None]) & member[None, :]
    pick = chosen.astype(BF16)
    slot_gate = jnp.sum(jnp.where(chosen, own_gate[None, :], 0.0), 1)

    grad_full = jnp.concatenate(own_parts(grad_natural, 1), 1)

    picked = dot_nn(pick, normed_two).astype(BF16)
    picked_parts = cut(picked, 1)
    gate_in = sum(dot_nn(a, b) for a, b in zip(picked_parts, gate_parts))
    up_in = sum(dot_nn(a, b) for a, b in zip(picked_parts, lift_parts))
    activation = (jax.nn.silu(gate_in) * up_in).astype(BF16)
    picked_grad = dot_nn(pick, grad_full).astype(BF16)
    grad_parts = cut(picked_grad, 1)
    act_raw = sum(dot_nt(a, b) for a, b in zip(grad_parts, fall_parts))
    gate_dot = jnp.sum(activation.astype(F32) * act_raw, 1)
    act_grad = act_raw * slot_gate[:, None]
    grad_gate_in = (act_grad * up_in * silu_slope(gate_in)).astype(BF16)
    grad_up_in = (act_grad * jax.nn.silu(gate_in)).astype(BF16)
    slot_dot = jnp.sum(
        gate_in * grad_gate_in.astype(F32) + up_in * grad_up_in.astype(F32), 1
    )
    slot_grad = (slot_gate[:, None] * picked_grad.astype(F32)).astype(BF16)
    slot_grad_parts = cut(slot_grad, 1)
    sent = (
        [dot_tn(a, grad_gate_in).astype(BF16) for a in picked_parts[1:]],
        [dot_tn(a, grad_up_in).astype(BF16) for a in picked_parts[1:]],
        [dot_tn(activation, a).astype(BF16) for a in slot_grad_parts[1:]],
    )
    picked_back = jnp.concatenate(
        [
            (dot_nt(grad_gate_in, a) + dot_nt(grad_up_in, b)).astype(BF16)
            for a, b in zip(gate_parts, lift_parts)
        ],
        1,
    )
    shared_in = dot_nn(normed_two, shared_gate_full)
    shared_lift = dot_nn(normed_two, shared_up_full)
    shared_act = (jax.nn.silu(shared_in) * shared_lift).astype(BF16)
    shared_grad = dot_nt(grad_full, shared_down_full)
    shared_gin = (shared_grad * shared_lift * silu_slope(shared_in)).astype(BF16)
    shared_gup = (shared_grad * jax.nn.silu(shared_in)).astype(BF16)

    token_dot = jnp.sum(jnp.where(chosen, gate_dot[:, None], 0.0), 0)
    gate_share = own_gate * token_dot
    coefficient = (
        gate_share[:, None] * (own_expert[None, :].astype(F32) - router_probs)
    ).astype(BF16)
    inner = (
        jnp.sum(jnp.where(chosen, slot_dot[:, None], 0.0), 0)
        + jnp.sum(shared_in * shared_gin.astype(F32) + shared_lift * shared_gup.astype(F32), 1)
        + jnp.sum(coefficient.astype(F32) * logits, 1)
    )
    pad = -(2 * shared_gin.shape[1] + experts) % LANES
    shared_left = jnp.concatenate(
        [shared_gin, shared_gup, coefficient, jnp.zeros((row_count, pad), BF16)], 1
    )
    shared_right = jnp.concatenate(
        [shared_gate_full, shared_up_full, router_full, jnp.zeros((width, pad), BF16)], 1
    )
    pick_back = pick.T
    grad_normed_two, stats, *fall_got = scatter_cols(
        [("nn", pick_back, picked_back), ("nt", shared_left, shared_right)],
        as_stat(inner, gate_share),
        2,
        5,
        [(array, t) for t, array in enumerate(sent[2], 1)],
    )
    stats = stats.reshape(n, 2, row_count)
    inner_total = jnp.sum(stats[:, 0], 0)[:, None]
    shares = stats[:, 1].T
    logit_grad = shares - router_probs * jnp.sum(shares, 1, keepdims=True)
    grad_stream = cotangent.astype(F32)
    grad_hidden = (
        grad_stream
        + second_root * (grad_normed_two * second_gain)
        - hidden * (second_root * second_root * inner_total / width)
    )
    second_gain_grad = jnp.sum(grad_normed_two * hidden * second_root, 0)
    latent_gain_grad, output_grad, query_back, low_back, low_wide, expanded_back, inner, *gate_got = (
        attention_backward(
            grad_hidden.astype(BF16),
            (
                out_full,
                queries,
                keys,
                values,
                latent,
                low,
                latent_root,
                mixed,
                log_total,
                up_full,
                choose,
                latent_gains,
                *tables,
                seg_col,
                seg_row,
            ),
            6,
            [(array, t) for t, array in enumerate(sent[0], 1)],
        )
    )

    expert_out = jnp.concatenate(
        [(slot_gate[:, None] * dot_nn(activation, b)).astype(BF16) for b in fall_parts], 1
    )
    mixture = dot_nn(pick_back, expert_out) + dot_nn(shared_act, shared_down_full)
    mixture = lax.psum_scatter(mixture.astype(BF16), "col", scatter_dimension=1, tiled=True)
    mixture = own_features(mixture)
    output = (hidden + mixture.astype(F32)).astype(BF16)

    grad_normed, low_own, stats, *up_got = scatter_cols(
        [("nt", query_back, query_full), ("tn", low_wide, down_full)],
        as_stat(inner[:, 0], latent_gain_grad[0], jnp.zeros((-LATENT % 1024,), F32)),
        2,
        8,
        [(array, t) for t, array in enumerate(sent[1], 1)],
        low_wide,
    )
    stats = jnp.sum(stats, 0).reshape(-1)
    inner_total = stats[:row_count, None]
    latent_gain_sum = stats[row_count : row_count + LATENT]
    stream = tokens.astype(F32)
    grad_input = (
        grad_hidden
        + first_root * (grad_normed * first_gain)
        - stream * (first_root * first_root * inner_total / width)
    )
    first_gain_grad = jnp.sum(grad_normed * stream * first_root, 0)
    moe_grads = (
        row_sum_of(dot_tn(picked_parts[0], grad_gate_in), gate_got)[None],
        row_sum_of(dot_tn(picked_parts[0], grad_up_in), up_got)[None],
        row_sum_of(dot_tn(activation, slot_grad_parts[0]), fall_got)[None],
        row_sum(cut(dot_tn(normed_two, shared_gin), 0)),
        row_sum(cut(dot_tn(normed_two, shared_gup), 0)),
        row_sum(cut(dot_tn(shared_act, grad_full), 1)),
        row_sum(cut(dot_tn(normed_two, logit_grad.astype(BF16)), 0)),
    )

    attn_grads = (
        row_sum(cut(dot_tn(normed, query_back[:, :QK]), 0)),
        row_sum(cut(dot_nn(low_own.astype(BF16), normed)[:narrow].T, 0)),
        row_sum(own_parts(dot_tn(latent, expanded_back), 0)),
        row_sum(cut(output_grad, 1)),
    )
    gain_grads = lax.psum((first_gain_grad, second_gain_grad, latent_gain_sum), "row")
    return (
        output,
        grad_input.astype(BF16),
        gain_grads[0],
        attn_grads[0],
        attn_grads[1],
        gain_grads[2],
        attn_grads[2],
        attn_grads[3],
        gain_grads[1],
        moe_grads[6],
        moe_grads[0],
        moe_grads[1],
        moe_grads[2],
        moe_grads[3],
        moe_grads[4],
        moe_grads[5],
    )


def solution(mesh):
    return jax.shard_map(
        per_device,
        mesh=mesh,
        in_specs=(
            P("row", "col"),
            P("row", "col"),
            P("row", None),
            P("row", None),
            P("col"),
            P("row", "col"),
            P("row", "col"),
            P(),
            P("row", "col"),
            P("col", "row"),
            P("col"),
            P("row", None),
            P("col", "row", None),
            P("col", "row", None),
            P("col", None, "row"),
            P("row", "col"),
            P("row", "col"),
            P("col", "row"),
        ),
        out_specs=(
            P("row", "col"),
            P("row", "col"),
            P("col"),
            P("row", "col"),
            P("row", "col"),
            P(),
            P("row", "col"),
            P("col", "row"),
            P("col"),
            P("row", None),
            P("col", "row", None),
            P("col", "row", None),
            P("col", None, "row"),
            P("row", "col"),
            P("row", "col"),
            P("col", "row"),
        ),
        check_vma=False,
    )
```

```python
import functools
import itertools

import jax
import jax.numpy as jnp
import numpy as np
from jax import lax
from jax.experimental import pallas as pl
from jax.experimental.pallas import tpu as pltpu
from jax.sharding import PartitionSpec as P

NOPE = 128
ROPE = 64
VD = 128
LATENT = 512
LEN = 1024
WINDOW = 1024
EPSILON = 1e-06
LANES = 128
MESH = pl.DeviceIdType.MESH
BF16 = jnp.bfloat16
F32 = jnp.float32
UP, DOWN, SIDE, CORE = range(4)
TILE = 256
PIECE = 2 * TILE


def dot_nn(a, b):
    return jnp.dot(a, b, preferred_element_type=F32)


def dot_nt(a, b):
    return lax.dot_general(a, b, (((1,), (1,)), ((), ())), preferred_element_type=F32)


def dot_tn(a, b):
    return lax.dot_general(a, b, (((0,), (0,)), ((), ())), preferred_element_type=F32)


def place():
    me = lax.axis_index("col")
    return lax.axis_index("row"), me // 4, (me // 2) % 2, me % 2


def col_of(z, y, c):
    return z * 4 + y * 2 + c


def rolled(index, row, n_row, count):
    return lax.rem(index + count - row * (count // n_row), count)


def signal(row, target):
    pl.semaphore_signal(
        pltpu.get_barrier_semaphore(), inc=1, device_id=(row, target), device_id_type=MESH
    )


def greet_row(row, me, n_row):
    for t in range(1, n_row):
        signal(lax.rem(row + t, n_row), me)
    pl.semaphore_wait(pltpu.get_barrier_semaphore(), n_row - 1)


def greet_neighbours(row, z, y, c, depth, n_row=1):
    for t in range(1, n_row):
        signal(lax.rem(row + t, n_row), col_of(z, y, c))
    signal(row, col_of(z, 1 - y, c))
    signal(row, col_of(z, y, 1 - c))

    @pl.when(z > 0)
    def _():
        signal(row, col_of(z - 1, y, c))

    @pl.when(z < depth - 1)
    def _():
        signal(row, col_of(z + 1, y, c))

    count = 1 + n_row + (z > 0).astype(jnp.int32) + (z < depth - 1).astype(jnp.int32)
    pl.semaphore_wait(pltpu.get_barrier_semaphore(), count)


class Swap:
    def __init__(self, array, t, index=()):
        self.array, self.t = array, t
        self.index = tuple(i if isinstance(i, int) else pl.ds(*i) for i in index)
        shape = [i[1] for i in index if not isinstance(i, int)] + list(array.shape[len(index) :])
        self.shape = jax.ShapeDtypeStruct(shape, array.dtype)


def swap_start(row, me, n_row, swaps, sources, targets, send_sem, recv_sem):
    copies = [
        swap_copy(
            row, me, n_row, source.at[index] if index else source, target, t,
            send_sem.at[i], recv_sem.at[i],
        )
        for i, ((t, index), source, target) in enumerate(zip(swaps, sources, targets))
    ]
    for copy in copies:
        copy.start()
    return copies


def swap_copy(row, me, n_row, source, target, t, send_sem, recv_sem):
    return pltpu.make_async_remote_copy(
        src_ref=source, dst_ref=target, send_sem=send_sem, recv_sem=recv_sem,
        device_id=(lax.rem(row + t, n_row), me), device_id_type=MESH,
    )


def greet_all(row, me, n, n_row=1):
    for t in range(1, n_row):
        signal(lax.rem(row + t, n_row), me)

    def hello(step, carry):
        signal(row, lax.rem(me + step, n))
        return carry

    lax.fori_loop(1, n, hello, 0)
    pl.semaphore_wait(pltpu.get_barrier_semaphore(), n + n_row - 2)


class Job:
    def __init__(self, kind, left, right, tiles, dtype, scale=None, add=None):
        self.kind, self.tiles, self.dtype, self.add = kind, tiles, dtype, add
        self.operands = [left, right] + ([scale] if scale is not None else [])
        shapes = [Swap(array, 0, index).shape.shape for array, index in (left, right)]
        self.shape = jax.ShapeDtypeStruct((shapes[0][kind == "tn"], shapes[1][1]), dtype)


class Jobs:
    def __init__(self, jobs):
        self.jobs, self.arrays, self.indices, self.shapes, self.uses = jobs, [], [], [], []
        known = {}
        for job in jobs:
            use = []
            for array, index in job.operands:
                key = (id(array), index)
                if key not in known:
                    known[key] = len(self.arrays)
                    swap = Swap(array, 0, index)
                    self.arrays.append(array)
                    self.indices.append(swap.index)
                    self.shapes.append(swap.shape)
                use.append(known[key])
            self.uses.append(use)
        self.added = [a for job in jobs for tile in job.add or () for a in tile if not isinstance(a, int)]
        self.stage = (
            max([rows for job in jobs for _, rows, _, _ in job.tiles] or [0]),
            max([columns for job in jobs for _, _, _, columns in job.tiles] or [0]),
        )
        self.dtype = jobs[0].dtype if jobs else F32
        self.count = len(self.arrays) + 2 * sum(len(job.tiles) for job in jobs) + len(self.added)
        self.count += sum(isinstance(a, int) for job in jobs for tile in job.add or () for a in tile)

    def tasks(self, arrays, added, outs, swaps, swaps_out, held, staged, taken, sem):
        local = copier(sem)
        loads = [
            local(array.at[index] if index else array, target)
            for array, index, target in zip(arrays, self.indices, held)
        ]
        middle = len(loads) // 2
        tasks = [
            lambda: [load.start() for load in loads[:middle]],
            lambda: [load.start() for load in loads[middle:]],
        ]
        waited, stores = set(), []
        added = list(added)

        def work(job, use, out, tile, extra):
            for i in use:
                if i not in waited:
                    waited.add(i)
                    loads[i].wait()
            row, rows, column, columns = tile
            takes = []
            for i, source in enumerate(extra):
                if isinstance(source, int):
                    swaps[source].wait_recv()
                    source = swaps_out[source]
                takes.append(local(source, taken.at[pl.ds(0, rows), pl.ds(0, columns)]))
            for take in takes[:1]:
                take.start()
            left, right = held[use[0]], held[use[1]]
            if job.kind == "tn":
                value = dot_tn(left[:, pl.ds(row, rows)], right[:, pl.ds(column, columns)])
            else:
                value = dot_nn(left[pl.ds(row, rows), :], right[:, pl.ds(column, columns)])
                if len(use) > 2:
                    value = value * held[use[2]][pl.ds(row, rows), :1]
            slot = len(stores) % 2
            if len(stores) > 1:
                stores[-2].wait()
            spot = staged.at[slot, pl.ds(0, rows), pl.ds(0, columns)]
            for i, take in enumerate(takes):
                if i:
                    take.start()
                take.wait()
                value = value + taken[pl.ds(0, rows), pl.ds(0, columns)].astype(F32)
            spot[...] = value.astype(job.dtype)
            store = local(spot, out.at[pl.ds(row, rows), pl.ds(column, columns)])
            store.start()
            stores.append(store)

        for job, use, out in zip(self.jobs, self.uses, outs):
            for i, tile in enumerate(job.tiles):
                extra = [a if isinstance(a, int) else added.pop(0) for a in (job.add[i] if job.add else ())]
                tasks.append(functools.partial(work, job, use, out, tile, extra))
        return tasks, stores


def scatter_kernel(depth, n_row, parts, kinds, has_stat, has_extra, shifts, jobs, *refs):
    count = 2 * len(kinds) + has_stat + has_extra
    extra = refs[count - 1 - has_stat] if has_extra else None
    operands, stat = refs[: 2 * len(kinds)], refs[count - 1] if has_stat else None
    swaps_in, refs = refs[count : count + len(shifts)], refs[count + len(shifts) :]
    job_arrays, refs = refs[: len(jobs.arrays)], refs[len(jobs.arrays) :]
    job_added, refs = refs[: len(jobs.added)], refs[len(jobs.added) :]
    out = refs[0]
    extra_out = refs[1] if has_extra else None
    refs = refs[has_extra:]
    stats = refs[1] if has_stat else None
    swaps_out = refs[1 + has_stat : 1 + has_stat + len(shifts)]
    refs = refs[1 + has_stat + len(shifts) :]
    job_outs, rest = refs[: len(jobs.jobs)], refs[len(jobs.jobs) :]
    if jobs.jobs:
        held = rest[-len(jobs.arrays) - 3 : -3]
        job_staged, job_taken, job_sem = rest[-3:]
        rest = rest[: -len(jobs.arrays) - 3]
    mine, core_send, core_recv, side_send, side_recv, line_send, line_recv = rest[:7]
    cs, cr, ss, sr, ls, lr = rest[7:13]
    extra_core, extra_side_send, extra_side, extra_line_send, extra_line = rest[-7:-2] if has_extra else [None] * 5
    row, z, y, c = place()
    me, n = col_of(z, y, c), 4 * depth
    pairs = 2 * depth
    rows = out.shape[0]
    size = rows // parts
    tile = min(256, size)
    if has_stat:
        stat_held, stat_send, stat_recv = rest[13:16]
        greet_all(row, me, n, n_row if shifts else 1)

        def stat_copy(step):
            target = lax.rem(me + step, n)
            return pltpu.make_async_remote_copy(
                src_ref=stat,
                dst_ref=stat_held.at[me],
                send_sem=stat_send.at[step],
                recv_sem=stat_recv.at[me],
                device_id=(row, target),
                device_id_type=MESH,
            )

        for step in range(1, n):
            stat_copy(step).start()
    else:
        greet_neighbours(row, z, y, c, depth, n_row if shifts else 1)
    swaps = swap_start(row, me, n_row, shifts, swaps_in, swaps_out, rest[-2], rest[-1])
    up, down = col_of(z + 1, y, c), col_of(z - 1, y, c)
    side, core = col_of(z, 1 - y, c), col_of(z, y, 1 - c)

    def remote(src, dst, send, recv, target):
        return pltpu.make_async_remote_copy(
            src_ref=src, dst_ref=dst, send_sem=send, recv_sem=recv,
            device_id=(row, target), device_id_type=MESH,
        )

    def span(h):
        return pl.ds(h * size, size)

    def block_of(s, cc):
        return col_of(order(s % depth), 1 - y if s < depth else y, cc)

    def extra_rows(s, cc):
        size = extra.shape[0] // n
        return extra.at[pl.ds(pl.multiple_of(block_of(s, cc) * size, 16), size)]

    def mine_at(s, h):
        return mine.at[s, span(h)] if h < parts else extra_rows(s, c)

    def core_recv_at(s, h):
        return core_recv.at[s, span(h)] if h < parts else extra_core.at[s]

    def side_send_at(k, h):
        return side_send.at[k, span(h)] if h < parts else extra_side_send.at[k]

    def side_recv_at(k, h):
        return side_recv.at[k, span(h)] if h < parts else extra_side.at[k]

    def line_send_at(zz, h):
        return line_send.at[zz, span(h)] if h < parts else extra_line_send.at[zz]

    def line_recv_at(way, zz, h):
        slot = zz + 1 - way
        return line_recv.at[slot, span(h)] if h < parts else extra_line.at[slot]

    def out_at(h):
        return out.at[span(h)] if h < parts else extra_out

    def core_copy(s, h):
        source = core_send.at[s % depth, span(h)] if h < parts else extra_rows(s, 1 - c)
        return remote(source, core_recv_at(s, h), cs.at[s, h], cr.at[s, h], core)

    def side_copy(k, h):
        return remote(side_send_at(k, h), side_recv_at(k, h), ss.at[k, h], sr.at[k, h], side)

    def line_copy(way, zz, h, target):
        return remote(
            line_send_at(zz, h), line_recv_at(way, zz, h), ls.at[zz, h], lr.at[way, zz, h], target
        )

    low_half = z < depth // 2

    def order(k):
        if k == depth - 1:
            return z
        from_top = depth - 1 - k
        from_top = from_top - (from_top <= z).astype(jnp.int32)
        from_low = k + (k >= z).astype(jnp.int32)
        return jnp.where(low_half, from_top, from_low)

    def tiles(body):
        def step(i, carry):
            body(i)
            return carry

        lax.fori_loop(0, size // tile, step, 0)

    def multiply(s, h):
        if h == parts:
            core_copy(s, h).start()
            return
        yy = 1 - y if s < depth else y
        pair = rolled(order(s % depth) * 2 + yy, row, n_row, pairs)
        cols = pl.ds(pl.multiple_of(pair * 2 * LANES, 2 * LANES), 2 * LANES)

        def body(i):
            at = pl.ds(pl.multiple_of(h * size + i * tile, tile), tile)
            total = None
            for j, kind in enumerate(kinds):
                left, right = operands[2 * j], operands[2 * j + 1]
                if kind == "nn":
                    term = dot_nn(left[at, :], right[:, cols])
                elif kind == "tn":
                    term = dot_tn(left[:, at], right[:, cols])
                else:
                    term = dot_nt(left[at, :], right[cols, :])
                total = term if total is None else total + term
            first, second = total[:, :LANES], total[:, LANES:]
            mine[s, at, :] = jnp.where(c == 0, first, second).astype(BF16)
            core_send[s % depth, at, :] = jnp.where(c == 0, second, first).astype(BF16)

        tiles(body)
        core_copy(s, h).start()

    def add_up(target, sources):
        step = min(tile, target.shape[0])

        def body(i, carry):
            at = pl.ds(pl.multiple_of(i * step, step), step)
            total = sources[0][at, :].astype(F32)
            for source in sources[1:]:
                total = total + source[at, :].astype(F32)
            target[at, :] = total.astype(target.dtype)
            return carry

        lax.fori_loop(0, target.shape[0] // step, body, 0)

    def fold(s, h):
        core_copy(s, h).wait_recv()
        k = s % depth
        sources = [mine_at(s, h), core_recv_at(s, h)]
        if s < depth:
            add_up(side_send_at(k, h), sources)
            side_copy(k, h).start()
            return
        side_copy(k, h).wait_recv()
        sources.append(side_recv_at(k, h))
        zz = order(k)
        if k < depth - 1:

            @pl.when(zz > z)
            def _():
                @pl.when(z > 0)
                def _():
                    line_copy(0, zz, h, up).wait_recv()
                    add_up(line_send_at(zz, h), sources + [line_recv_at(0, zz, h)])

                @pl.when(z == 0)
                def _():
                    add_up(line_send_at(zz, h), sources)

                line_copy(0, zz, h, up).start()

            @pl.when(zz < z)
            def _():
                @pl.when(z < depth - 1)
                def _():
                    line_copy(1, zz, h, down).wait_recv()
                    add_up(line_send_at(zz, h), sources + [line_recv_at(1, zz, h)])

                @pl.when(z == depth - 1)
                def _():
                    add_up(line_send_at(zz, h), sources)

                line_copy(1, zz, h, down).start()

            return

        @pl.when((z > 0) & (z < depth - 1))
        def _():
            line_copy(0, z, h, me).wait_recv()
            line_copy(1, z, h, me).wait_recv()
            add_up(out_at(h), sources + [line_recv_at(0, z, h), line_recv_at(1, z, h)])

        @pl.when(z == 0)
        def _():
            line_copy(1, z, h, me).wait_recv()
            add_up(out_at(h), sources + [line_recv_at(1, z, h)])

        @pl.when(z == depth - 1)
        def _():
            line_copy(0, z, h, me).wait_recv()
            add_up(out_at(h), sources + [line_recv_at(0, z, h)])

    chunks = parts + has_extra
    steps = [(s, h) for s in range(2 * depth) for h in range(chunks)]
    tasks, stores = [], []
    if jobs.jobs:
        tasks, stores = jobs.tasks(
            job_arrays, job_added, job_outs, swaps, swaps_out, held, job_staged, job_taken, job_sem
        )
    first = depth * chunks
    for i, (s, h) in enumerate(steps):
        if s >= depth and h < parts:
            core_copy(s - depth, h).wait_send()
        multiply(s, h)
        if 0 < i <= first:
            fold(*steps[i - 1])
        if i > first + 1:
            fold(*steps[i - 2])
        if i >= first:
            for _ in range(-(-len(tasks) // (len(steps) - i + 1))):
                tasks.pop(0)()
    for step in steps[-2:]:
        fold(*step)
        for _ in range(-(-len(tasks) // 2)):
            tasks.pop(0)()
    for task in tasks:
        task()
    for store in stores[-2:]:
        store.wait()
    for s, h in steps:
        if s >= depth or h == parts:
            core_copy(s, h).wait_send()
    for k in range(depth):
        for h in range(chunks):
            side_copy(k, h).wait_send()
    for k in range(depth - 1):
        zz = order(k)
        for h in range(chunks):
            line_copy(0, zz, h, me).wait_send()
    if has_stat:
        stat_held[me] = stat[...]
        for step in range(1, n):
            stat_copy(step).wait_send()
            source = lax.rem(me + step, n)
            remote(stat, stat_held.at[source], stat_send.at[step], stat_recv.at[source], me).wait_recv()
        stats[...] = stat_held[...]
    taken = {a for job in jobs.jobs for tile in job.add or () for a in tile if isinstance(a, int)}
    for i, swap in enumerate(swaps):
        swap.wait_send()
        if i not in taken:
            swap.wait_recv()


def scatter_cols(products, stat, parts, collective_id, swaps=(), extra=None, jobs=()):
    n, n_row = lax.axis_size("col"), lax.axis_size("row")
    depth = n // 4
    chunks = parts + (extra is not None)
    kinds = tuple(kind for kind, _, _ in products)
    operands = [x for _, a, b in products for x in (a, b)]
    rows = operands[0].shape[kinds[0] == "tn"]
    in_vmem = pl.BlockSpec(memory_space=pltpu.VMEM)
    out_shape = [jax.ShapeDtypeStruct((rows, LANES), F32)]
    dma = pltpu.SemaphoreType.DMA
    scratch = [
        pltpu.VMEM((2 * depth, rows, LANES), BF16),
        pltpu.VMEM((depth, rows, LANES), BF16),
        pltpu.VMEM((2 * depth, rows, LANES), BF16),
        pltpu.VMEM((depth, rows, LANES), BF16),
        pltpu.VMEM((depth, rows, LANES), BF16),
        pltpu.VMEM((depth, rows, LANES), BF16),
        pltpu.VMEM((depth + 1, rows, LANES), BF16),
        dma((2 * depth, chunks)),
        dma((2 * depth, chunks)),
        dma((depth, chunks)),
        dma((depth, chunks)),
        dma((depth, chunks)),
        dma((2, depth, chunks)),
    ]
    if extra is not None:
        operands.append(extra)
        block = (extra.shape[0] // n, extra.shape[1])
        out_shape.append(jax.ShapeDtypeStruct(block, F32))
    if stat is not None:
        operands.append(stat)
        out_shape.append(jax.ShapeDtypeStruct((n,) + stat.shape, F32))
        scratch += [pltpu.VMEM((n,) + stat.shape, F32), dma((n,)), dma((n,))]
    held = [in_vmem] * len(operands)
    kept = [in_vmem] * len(out_shape)
    anywhere = pl.BlockSpec(memory_space=pl.ANY)
    if extra is not None:
        scratch += [
            pltpu.VMEM((2 * depth,) + block, BF16),
            pltpu.VMEM((depth,) + block, BF16),
            pltpu.VMEM((depth,) + block, BF16),
            pltpu.VMEM((depth,) + block, BF16),
            pltpu.VMEM((depth + 1,) + block, BF16),
        ]
    if swaps:
        operands += [swap.array for swap in swaps]
        held += [anywhere] * len(swaps)
        kept += [anywhere] * len(swaps)
        out_shape += [swap.shape for swap in swaps]
    scratch += [dma((max(1, len(swaps)),)), dma((max(1, len(swaps)),))]
    jobs = Jobs(list(jobs))
    if jobs.jobs:
        operands += jobs.arrays + jobs.added
        held += [anywhere] * (len(jobs.arrays) + len(jobs.added))
        kept += [anywhere] * len(jobs.jobs)
        out_shape += [job.shape for job in jobs.jobs]
        scratch += [pltpu.VMEM(a.shape, a.dtype) for a in jobs.shapes]
        scratch += [
            pltpu.VMEM((2,) + jobs.stage, jobs.dtype),
            pltpu.VMEM(jobs.stage if jobs.dtype == F32 else (16, LANES), BF16),
            dma((jobs.count,)),
        ]
    shifts = tuple((swap.t, swap.index) for swap in swaps)
    return pl.pallas_call(
        functools.partial(scatter_kernel, depth, n_row, parts, kinds, stat is not None, extra is not None, shifts, jobs),
        out_shape=out_shape,
        in_specs=held,
        out_specs=kept,
        scratch_shapes=scratch,
        compiler_params=pltpu.CompilerParams(
            collective_id=collective_id, has_side_effects=True, vmem_limit_bytes=63 << 20
        ),
        name="scatter_cols",
    )(*operands)


class Piece:
    def __init__(self, source, spot, prepare=None, side_first=False):
        self.source, self.spot, self.prepare, self.side_first = source, spot, prepare, side_first


def gather_steps(row, z, y, c, depth, pieces, send_sem, recv_sem):
    me = col_of(z, y, c)
    up, down = col_of(z + 1, y, c), col_of(z - 1, y, c)
    side, core = col_of(z, 1 - y, c), col_of(z, y, 1 - c)

    def copy(way, block, p, target, own=False):
        piece = pieces[p]
        return pltpu.make_async_remote_copy(
            src_ref=piece.source if own else piece.spot(block),
            dst_ref=piece.spot(block),
            send_sem=send_sem.at[p, way * 2 * depth + block // 2],
            recv_sem=recv_sem.at[p, block],
            device_id=(row, target),
            device_id_type=MESH,
        )

    def start(way, block, p, target, own=False):
        copy(way, block, p, target, own).start()

    def finish(way, block, p, target, own=False):
        copy(way, block, p, target, own).wait_send()

    def arrive(block, p):
        copy(CORE, block, p, me).wait_recv()

    def own(p, act):
        act(SIDE, me, p, side, True)

        @pl.when(z + 1 < depth)
        def _():
            act(UP, me, p, up, True)

        @pl.when(z > 0)
        def _():
            act(DOWN, me, p, down, True)

        act(CORE, me, p, core, True)

    def onward(at, yy, p, act, along, across):
        block = col_of(at, yy, c)
        if act is start:
            arrive(block, p)
        if along:

            @pl.when((at <= z) & (z + 1 < depth))
            def _():
                act(UP, block, p, up)

            @pl.when((at >= z) & (z > 0))
            def _():
                act(DOWN, block, p, down)

        if across:
            act(SIDE, block, p, side)
        act(CORE, block, p, core)

    def line(d, p, act):
        if d == 0:
            own(p, act)
            return
        for at in (z - d, z + d):

            @pl.when((at >= 0) & (at < depth))
            def _():
                onward(at, y, p, act, True, not pieces[p].side_first)

    def sides(d, p, act):
        for at in (z - d, z + d) if d else (z,):

            @pl.when((at >= 0) & (at < depth))
            def _():
                onward(at, 1 - y, p, act, pieces[p].side_first, False)

    def begin(p):
        if pieces[p].prepare is not None:
            pieces[p].prepare()
        line(0, p, start)

    count = len(pieces)
    begin(0)
    for wave in range(count + depth + 1):
        done = []
        for p in range(count):
            k = wave - p
            if k == -1:
                begin(p)
            if 1 <= k < depth:
                line(k, p, start)
                sides(k - 1, p, start)
            if k == depth:
                sides(depth - 1, p, start)
            if k == depth + 1:
                for zz in range(depth):
                    for yy in range(2):
                        arrive(col_of(zz, yy, 1 - c), p)
                done.append(p)
        yield done
    for p in range(count):
        for d in range(depth):
            line(d, p, finish)
            sides(d, p, finish)


def row_pieces(source, rows, spot):
    count = rows // PIECE
    return [
        Piece(
            source.at[span_of(i, PIECE)],
            functools.partial(spot, span_of(i, PIECE)),
            side_first=i % 4 == 2,
        )
        for i in range(count)
    ]


def span_of(i, size):
    return pl.ds(i * size, size)


COSTS = {
    "project": 1.2, "project_latent": 1.6, "project_keys": 0.8, "project_queries": 0.7, "attend": 2.0, "norm": 0.5,
    "route": 0.8, "pick": 1.2, "forward": 1.6, "shared": 1.4, "weigh": 0.7, "expand": 1.5,
}


def work_through(steps, ready, tasks=(), budget=8.0):
    tasks = list(tasks)
    for done in steps:
        for p in done:
            tasks += ready(p)
        spent = 0.0
        while tasks and spent < budget:
            task = tasks.pop(0)
            spent += COSTS.get(getattr(getattr(task, "func", task), "__name__", ""), 0.3)
            task()
    for task in tasks:
        task()


def rotary_tables():
    frequency = 10000.0 ** (-np.arange(ROPE // 2, dtype=np.float32) * 2.0 / ROPE)
    angles = np.arange(LEN, dtype=np.float32)[:, None] * frequency[None, :].astype(np.float32)
    cosines, sines = np.cos(angles), np.sin(angles)
    return (
        jnp.asarray(np.concatenate([cosines] * 4, 1)),
        jnp.asarray(np.concatenate([-sines, sines, sines, -sines], 1)),
    )


def with_exchanged(array):
    half = ROPE // 2
    return jnp.concatenate([array, array[-half:], array[-ROPE:-half]], 0)


def turn(tile, cosines, sines):
    return tile * cosines + pltpu.roll(tile, ROPE, 1) * sines


def spread(columns, like):
    return jnp.broadcast_to(columns, like.shape)


SCALE = (NOPE + ROPE) ** (-0.5)
QK = NOPE + ROPE


def masked_scores(q, k, seg_col, seg_row, base, first, length):
    scores = dot_nt(q[pl.ds(base + first, TILE), :QK], k[pl.ds(base, length), :QK]) * SCALE
    here = first + lax.broadcasted_iota(jnp.int32, (TILE, length), 0)
    there = lax.broadcasted_iota(jnp.int32, (TILE, length), 1)
    allowed = (here >= there) & (
        seg_col[pl.ds(base + first, TILE), :1] == seg_row[:1, pl.ds(base, length)]
    )
    if WINDOW < LEN:
        allowed = allowed & (here - there < WINDOW)
    return jnp.where(allowed, scores, -1e30)


def forward_kernel(depth, n_row, sizes, shifts, *refs):
    (tokens, gain, query_own, down_own, up_own), loads_in = refs[:5], refs[5:11]
    swaps_in, refs = refs[11 : 11 + len(shifts)], refs[11 + len(shifts) :]
    outs, swaps_out, refs = refs[:13], refs[13 : 13 + len(shifts)], refs[13 + len(shifts) :]
    (full, gains, held, query_full, down_mine, down_full, up_full) = refs[:7]
    (q, k, v, latent, low, first_root, latent_root, mixed, lse) = refs[7:16]
    loads_to, refs = refs[16:22], refs[22:]
    (choose, latent_gain, cosines, sines, seg_col, seg_row) = loads_to
    (send_sem, recv_sem, swap_send, swap_recv, local_sem, out_sem, weight_sem, late_send, late_recv, load_sem) = refs
    results = (held, q, k, v, latent, low, first_root, latent_root, mixed, lse)
    rows, width, seqs = sizes
    row, z, y, c = place()
    me, n = col_of(z, y, c), 4 * depth
    greet_neighbours(row, z, y, c, depth, n_row)
    share = width // n_row
    up_rows = up_own.shape[0]
    down_rows = down_own.shape[0]

    def part(s):
        return pl.ds(s * share, share)

    swaps = []
    for i, (source, spot) in enumerate(
        [
            (down_own, lambda slot: down_mine.at[:, part(slot)]),
            (query_own, lambda slot: query_full.at[:, part(slot)]),
        ]
    ):
        swaps.append(
            [
                swap_copy(row, me, n_row, source, spot(n_row - t), t, swap_send.at[i, t], swap_recv.at[i, t])
                for t in range(1, n_row)
            ]
        )
    own_up = pl.ds(pl.multiple_of(row * up_rows, up_rows), up_rows)
    swaps.append(
        [
            swap_copy(row, me, n_row, up_own, up_full.at[own_up], t, swap_send.at[2, t], swap_recv.at[2, t])
            for t in range(1, n_row)
        ]
    )
    for group in swaps:
        for swap in group:
            swap.start()
    late = swap_start(row, me, n_row, shifts, swaps_in, swaps_out, late_send, late_recv)

    def lanes(block):
        return pl.ds(pl.multiple_of(rolled(block, row, n_row, n) * LANES, LANES), LANES)

    locals_ = [
        pltpu.make_async_copy(down_own, down_mine.at[:, part(0)], local_sem.at[0]),
        pltpu.make_async_copy(query_own, query_full.at[:, part(0)], local_sem.at[1]),
        pltpu.make_async_copy(up_own, up_full.at[own_up], local_sem.at[2]),
        pltpu.make_async_copy(gain, gains.at[:, lanes(me)], local_sem.at[3]),
        pltpu.make_async_copy(tokens, full.at[:, lanes(me)], local_sem.at[4]),
    ]
    for copy in locals_:
        copy.start()
    keep_down = pltpu.make_async_copy(
        down_mine, down_full.at[pl.ds(pl.multiple_of(me * down_rows, 16), down_rows)], local_sem.at[5]
    )

    def down_ready():
        locals_[0].wait()
        for swap in swaps[0]:
            swap.wait_recv()
        keep_down.start()

    pieces = [Piece(gain, lambda block: gains.at[:, lanes(block)])]
    pieces += row_pieces(tokens, rows, lambda span, block: full.at[span, lanes(block)])
    down_piece = 2
    pieces.insert(
        down_piece,
        Piece(
            down_mine,
            lambda block: down_full.at[pl.ds(pl.multiple_of(block * down_rows, 16), down_rows)],
            down_ready,
        ),
    )
    token_pieces = [p for p in range(1, len(pieces)) if p != down_piece]

    def keep(array, seq):
        span = pl.ds(seq * LEN, LEN)
        return pltpu.make_async_copy(results[array].at[span], outs[array].at[span], out_sem.at[array, seq])

    def keep_some(arrays, seq):
        for array in arrays:
            keep(array, seq).start()

    weights_out = [
        pltpu.make_async_copy(source, target, weight_sem.at[i])
        for i, (source, target) in enumerate(zip((query_full, down_full, up_full), outs[10:]))
    ]

    def project(i):
        span = pl.ds(i * TILE, TILE)
        x = full[span, :].astype(F32)
        root = lax.rsqrt(jnp.sum(x * x, 1, keepdims=True) / width + EPSILON)
        first_root[span, :] = jnp.broadcast_to(root, (TILE, LANES))
        held[span, :] = (x * root * gains[:1, :]).astype(BF16)

    def project_queries(i):
        span = span_of(i, TILE)
        at = pl.ds((i * TILE) % LEN, TILE)
        pre = dot_nt(held[span, :], query_full[...])
        q[span, :NOPE] = pre[:, :NOPE].astype(BF16)
        q[span, NOPE:] = turn(pre[:, NOPE:], cosines[at, :], sines[at, :]).astype(BF16)

    def project_latent(i):
        span = span_of(i, TILE)
        wide = dot_nt(held[span, :], down_full[...]).astype(BF16)
        low[span, :] = dot_nn(wide, choose[...]).astype(BF16)

    def project_keys(i):
        span = span_of(i, TILE)
        at = pl.ds((i * TILE) % LEN, TILE)
        compressed = low[span, :LATENT].astype(F32)
        root = lax.rsqrt(jnp.mean(compressed * compressed, 1, keepdims=True) + EPSILON)
        latent_root[span, :] = jnp.broadcast_to(root, (TILE, LANES))
        lat = (compressed * root * latent_gain[:1, :]).astype(BF16)
        latent[span, :] = lat
        expanded = dot_nn(lat, up_full[...]).astype(BF16)
        k[span, :NOPE] = expanded[:, :NOPE]
        tile = low[span, LATENT:].astype(F32)
        k[span, NOPE:] = turn(tile, cosines[at, :], sines[at, :]).astype(BF16)
        v[span, :] = expanded[:, NOPE:]

    def attend(seq, block):
        base, first = seq * LEN, block * TILE
        length = first + TILE
        scores = masked_scores(q, k, seg_col, seg_row, base, first, length)
        top = jnp.max(scores, -1, keepdims=True)
        weights = jnp.exp(scores - top)
        total = jnp.sum(weights, -1, keepdims=True)
        probs = (weights / total).astype(BF16)
        span = pl.ds(base + first, TILE)
        mixed[span, :] = dot_nn(probs, v[pl.ds(base, length), :]).astype(BF16)
        lse[span, :] = jnp.broadcast_to(top + jnp.log(total), (TILE, LANES))

    state = {"weights": False}
    per_seq = LEN // TILE
    waiting = []

    def weights_here():
        keep_down.wait()
        for copy in locals_[1:3]:
            copy.wait()
        for group in swaps[1:]:
            for swap in group:
                swap.wait_recv()
        for copy in weights_out:
            copy.start()

    local = copier(load_sem)
    loads = [local(a, b) for a, b in zip(loads_in, loads_to)]

    def ready(p):
        tasks = []
        if p == 0:
            tasks.append(lambda: [copy.wait() for copy in locals_[3:] + loads])
        if p == down_piece:
            tasks.append(weights_here)
            state["weights"] = True
        if p in token_pieces:
            for i in (2 * token_pieces.index(p), 2 * token_pieces.index(p) + 1):
                tasks.append(functools.partial(project, i))
                waiting.append(i)
        if state["weights"]:
            for i in waiting:
                seq, b = divmod(i, per_seq)
                tasks += [
                    functools.partial(project_latent, i),
                    functools.partial(project_keys, i),
                    functools.partial(project_queries, i),
                    functools.partial(attend, seq, b),
                ]
                if b == per_seq - 1:
                    tasks.append(functools.partial(keep_some, range(10), seq))
            waiting.clear()
        return tasks

    first_tasks = [lambda: [copy.start() for copy in loads]]
    work_through(gather_steps(row, z, y, c, depth, pieces, send_sem, recv_sem), ready, first_tasks)
    for group in swaps:
        for swap in group:
            swap.wait_send()
    for copy in weights_out:
        copy.wait()
    for seq in range(seqs):
        for array in range(10):
            keep(array, seq).wait()
    for swap in late:
        swap.wait()


def attention_forward(
    tokens, gain, query_own, down_own, up_own, choose, latent_gain, tables, seg_col, seg_row, collective_id, swaps=()
):
    n, n_row = lax.axis_size("col"), lax.axis_size("row")
    depth, rows = n // 4, tokens.shape[0]
    width, seqs = n * tokens.shape[1], rows // LEN
    padded = n * down_own.shape[0]
    in_vmem = pl.BlockSpec(memory_space=pltpu.VMEM)
    anywhere = pl.BlockSpec(memory_space=pl.ANY)
    count = 2 + rows // PIECE
    dma = pltpu.SemaphoreType.DMA
    shape = jax.ShapeDtypeStruct
    kept = [
        shape((rows, 2 * LANES), BF16),
        shape((rows, 2 * LANES), BF16),
        shape((rows, VD), BF16),
        shape((rows, LATENT), BF16),
        shape((rows, LATENT + LANES), BF16),
        shape((rows, LANES), F32),
        shape((rows, LANES), F32),
        shape((rows, VD), BF16),
        shape((rows, LANES), F32),
    ]
    loads = [choose, latent_gain, *tables, seg_col, seg_row]
    swapped = [swap.array for swap in swaps]
    return pl.pallas_call(
        functools.partial(
            forward_kernel, depth, n_row, (rows, width, seqs), tuple((swap.t, swap.index) for swap in swaps)
        ),
        out_shape=[shape((rows, width), BF16)]
        + kept
        + [
            shape((2 * LANES, width), BF16),
            shape((padded, width), BF16),
            shape((LATENT, 2 * LANES), BF16),
        ]
        + [swap.shape for swap in swaps],
        in_specs=[anywhere] * (11 + len(swapped)),
        out_specs=[anywhere] * (13 + len(swapped)),
        scratch_shapes=[
            pltpu.VMEM((rows, width), BF16),
            pltpu.VMEM((gain.shape[0], width), F32),
            pltpu.VMEM((rows, width), BF16),
            pltpu.VMEM((2 * LANES, width), BF16),
            pltpu.VMEM((down_own.shape[0], width), BF16),
            pltpu.VMEM((padded, width), BF16),
            pltpu.VMEM((LATENT, 2 * LANES), BF16),
        ]
        + [pltpu.VMEM(a.shape, a.dtype) for a in [*kept, *loads]]
        + [
            dma((count, 8 * depth)),
            dma((count, n)),
            dma((3, n_row)),
            dma((3, n_row)),
            dma((6,)),
            dma((10, seqs)),
            dma((3,)),
            dma((max(1, len(swapped)),)),
            dma((max(1, len(swapped)),)),
            dma((len(loads),)),
        ],
        compiler_params=pltpu.CompilerParams(
            collective_id=collective_id, has_side_effects=True, vmem_limit_bytes=60 << 20
        ),
        name="attention_forward",
    )(tokens, gain, query_own, down_own, up_own, *loads, *swapped)


def sigmoid_parts(values):
    sigmoid = jax.nn.sigmoid(values)
    return values * sigmoid, sigmoid * (1.0 + values * (1.0 - sigmoid))


def three_terms(column, width, first):
    high = column.astype(BF16).astype(F32)
    middle = (column - high).astype(BF16).astype(F32)
    lane = lax.broadcasted_iota(jnp.int32, (column.shape[0], width), 1)
    out = jnp.where(lane == first, high, 0.0)
    out = jnp.where(lane == first + 1, middle, out)
    return jnp.where(lane == first + 2, column - high - middle, out)


def copier(sem):
    count = itertools.count()
    return lambda source, target: pltpu.make_async_copy(source, target, sem.at[next(count)])


def hidden_kernel(depth, n_row, sizes, shifts, *refs):
    rows, width, capacity, narrow, experts = sizes
    block, squares, slot_row = refs[:3]
    parts, refs = refs[3 : 3 + 3 * n_row], refs[3 + 3 * n_row :]
    swaps_in, refs = refs[: len(shifts)], refs[len(shifts) :]
    outs, swaps_out, refs = refs[:11], refs[11 : 11 + len(shifts)], refs[11 + len(shifts) :]
    held, refs = refs[:11], refs[11:]
    (full, full_squares, gate_terms, send_sem, recv_sem, local_sem, swap_send, swap_recv) = refs
    (normed, picked, gate_in, up_in, act, logits, root, slot_gate, gate_weight, up_weight, router) = held
    row, z, y, c = place()
    me, n = col_of(z, y, c), 4 * depth
    greet_neighbours(row, z, y, c, depth, n_row)
    swaps = swap_start(row, me, n_row, shifts, swaps_in, swaps_out, swap_send, swap_recv)
    local = copier(local_sem)

    def lanes(block):
        return pl.ds(pl.multiple_of(rolled(block, row, n_row, n) * LANES, LANES), LANES)

    own = [
        local(block, full.at[:, lanes(me)]),
        local(squares, full_squares.at[:, lanes(me)]),
    ]
    share = width // n_row
    for i, target in enumerate((gate_weight, up_weight, router)):
        own += [local(parts[i * n_row + p], target.at[:, span_of(p, share)]) for p in range(n_row)]
    for copy in own:
        copy.start()
    pieces = [Piece(squares, lambda block: full_squares.at[:, lanes(block)])]
    pieces += row_pieces(block, rows, lambda span, block: full.at[span, lanes(block)])
    results = {}

    def store(name, index=slice(None)):
        copy = local(held[name].at[index], outs[name].at[index])
        results[len(results)] = copy
        copy.start()

    def roots():
        for copy in own:
            copy.wait()
        total = sum(full_squares[:, j * LANES : (j + 1) * LANES] for j in range(n))
        columns = jnp.transpose(lax.rsqrt(total / width + EPSILON))
        for i in range(rows // LANES):
            root[span_of(i, LANES), :] = jnp.broadcast_to(columns[:, i : i + 1], (LANES, LANES))
        for name in (6, 8, 9, 10):
            store(name)

    def norm(i):
        span = span_of(i, TILE)
        normed[span, :] = (full[span, :].astype(F32) * root[span, :1]).astype(BF16)

    def project(i):
        span = span_of(i, TILE)
        gate = dot_nt(normed[span, :], gate_weight[...])
        up = dot_nt(normed[span, :], up_weight[...])
        gate_in[span, :] = gate.astype(BF16)
        up_in[span, :] = up.astype(BF16)
        act[span, :] = (gate * jax.nn.sigmoid(gate) * up).astype(BF16)

    def route(i):
        span = span_of(i, TILE)
        scores = dot_nt(normed[span, :], router[...])
        logits[span, :] = scores
        weights = jnp.exp(scores - jnp.max(scores, -1, keepdims=True))
        mine = lax.broadcasted_iota(jnp.int32, scores.shape, 1) == me
        own_gate = jnp.sum(jnp.where(mine, weights, 0.0), -1, keepdims=True) / jnp.sum(
            weights, -1, keepdims=True
        )
        gate_terms[span, :] = three_terms(own_gate, LANES, 0).astype(BF16)

    def pick(q, t):
        tokens, span = span_of(q, 2 * TILE), span_of(t, TILE)
        here = lax.broadcasted_iota(jnp.int32, (TILE, 2 * TILE), 0) + t * TILE
        chosen = jnp.where(here == slot_row[:1, tokens], 1.0, 0.0).astype(BF16)
        term = dot_nn(chosen, normed[tokens, :])
        gates = dot_nn(chosen, gate_terms[tokens, :])
        if q == 0:
            picked[span, :] = term.astype(BF16)
            slot_gate[span, :] = gates
        else:
            picked[span, :] = (picked[span, :].astype(F32) + term).astype(BF16)
            slot_gate[span, :] += gates

    def finish():
        total = jnp.sum(slot_gate[...], 1, keepdims=True)
        slot_gate[...] = jnp.broadcast_to(total, slot_gate.shape)
        for name in (1, 2, 3, 4, 5, 7):
            store(name)

    def ready(p):
        if p == 0:
            return [roots]
        q = p - 1
        tasks = [functools.partial(norm, i) for i in (2 * q, 2 * q + 1)]
        tasks += [functools.partial(route, i) for i in (2 * q, 2 * q + 1)]
        tasks += [functools.partial(pick, q, t) for t in range(capacity // TILE)]
        tasks += [functools.partial(project, i) for i in (2 * q, 2 * q + 1)]
        tasks.append(functools.partial(store, 0, span_of(q, PIECE)))
        if p == len(pieces) - 1:
            tasks.append(finish)
        return tasks

    work_through(gather_steps(row, z, y, c, depth, pieces, send_sem, recv_sem), ready)
    for copy in results.values():
        copy.wait()
    for swap in swaps:
        swap.wait()


def hidden_rows(block, squares, slot_row, parts, capacity, collective_id, swaps=()):
    n, n_row = lax.axis_size("col"), lax.axis_size("row")
    depth, rows = n // 4, block.shape[0]
    width, narrow, experts = n * block.shape[1], parts[0].shape[0], parts[-1].shape[0]
    anywhere = pl.BlockSpec(memory_space=pl.ANY)
    dma, shape = pltpu.SemaphoreType.DMA, jax.ShapeDtypeStruct
    swapped = [swap.array for swap in swaps]
    count = 1 + rows // PIECE
    kept = [
        shape((rows, width), BF16),
        shape((capacity, width), BF16),
        shape((rows, narrow), BF16),
        shape((rows, narrow), BF16),
        shape((rows, narrow), BF16),
        shape((rows, experts), F32),
        shape((rows, LANES), F32),
        shape((capacity, LANES), F32),
        shape((narrow, width), BF16),
        shape((narrow, width), BF16),
        shape((experts, width), BF16),
    ]
    return pl.pallas_call(
        functools.partial(
            hidden_kernel,
            depth,
            n_row,
            (rows, width, capacity, narrow, experts),
            tuple((swap.t, swap.index) for swap in swaps),
        ),
        out_shape=kept + [swap.shape for swap in swaps],
        in_specs=[anywhere] * 2
        + [pl.BlockSpec(memory_space=pltpu.VMEM)]
        + [anywhere] * (len(parts) + len(swapped)),
        out_specs=[anywhere] * (len(kept) + len(swapped)),
        scratch_shapes=[pltpu.VMEM(a.shape, a.dtype) for a in kept]
        + [
            pltpu.VMEM((rows, width), BF16),
            pltpu.VMEM((squares.shape[0], width), F32),
            pltpu.VMEM((rows, LANES), BF16),
            dma((count, 8 * depth)),
            dma((count, n)),
            dma((2 + 3 * n_row + 10 + rows // TILE,)),
            dma((max(1, len(swapped)),)),
            dma((max(1, len(swapped)),)),
        ],
        compiler_params=pltpu.CompilerParams(
            collective_id=collective_id, has_side_effects=True, vmem_limit_bytes=60 << 20
        ),
        name="hidden_rows",
    )(block, squares, slot_row, *parts, *swapped)


def mixture_kernel(depth, n_row, sizes, falls, *refs):
    rows, width, capacity, hidden_units, narrow, experts = sizes
    block, picked_in, slot_row, slot_col, logits_in, slot_gate_in, gate_in, up_in = refs[:8]
    refs = refs[8:]
    each = 2 * n_row - 1
    gate_parts, up_parts, refs = refs[:each], refs[each : 2 * each], refs[2 * each :]
    fall_own, fall_got, refs = refs[0], refs[1:n_row], refs[n_row:]
    shared_parts, refs = refs[:n_row], refs[n_row:]
    outs, refs = refs[:9], refs[9:]
    (fall_out, rows_out, act_out, dgate_out, dup_out, grad_out, sgate_out, sup_out, coef_out) = outs
    (stat_out, full_out, shared_out), refs = refs[:3], refs[3:]
    (full, gate_weight, up_weight, fall_weight, picked, gate, up, act, grads, shared_weight) = refs[:10]
    (shared_gate, shared_up, logits, slot_cols, slot_gates, values, inner, coefs, stats), refs = refs[10:19], refs[19:]
    (staged, send_sem, recv_sem, local_sem, swap_send, swap_recv) = refs
    row, z, y, c = place()
    me, n = col_of(z, y, c), 4 * depth
    greet_neighbours(row, z, y, c, depth, n_row)
    share = width // n_row
    first = falls
    swaps = [
        swap_copy(
            row, me, n_row, fall_own.at[0, pl.ds(first, hidden_units - first)],
            fall_weight.at[pl.ds(first, hidden_units - first), span_of(n_row - t, share)],
            t, swap_send.at[t], swap_recv.at[t],
        )
        for t in range(1, n_row)
    ]
    for swap in swaps:
        swap.start()
    local = copier(local_sem)

    def lanes(block):
        return pl.ds(pl.multiple_of(rolled(block, row, n_row, n) * LANES, LANES), LANES)

    loads = [local(picked_in, picked)]
    for weight, pieces in ((gate_weight, gate_parts), (up_weight, up_parts)):
        loads.append(local(pieces[0].at[0], weight.at[span_of(0, share)]))
        at = share
        for piece in pieces[1:]:
            loads.append(local(piece, weight.at[pl.ds(at, piece.shape[0])]))
            at += piece.shape[0]
    later = [
        local(block, full.at[:, lanes(me)]),
        local(slot_gate_in, slot_gates),
        local(logits_in, logits),
        local(slot_col, slot_cols),
        local(gate_in, shared_gate),
        local(up_in, shared_up),
        local(fall_own.at[0], fall_weight.at[:, span_of(0, share)]),
    ]
    for p in range(n_row):
        later.append(local(shared_parts[p], shared_weight.at[:, span_of(p, share)]))
        if p:
            later.append(local(fall_got[p - 1], fall_weight.at[pl.ds(0, first), span_of(p, share)]))
    later[0].start()
    pieces = row_pieces(block, rows, lambda span, block: full.at[span, lanes(block)])
    chunk = 4 * LANES
    chunks = [(at, min(chunk, hidden_units - at)) for at in range(0, hidden_units, chunk)]
    results = []

    def store(source, target):
        copy = local(source, target)
        copy.start()
        results.append(copy)

    def begin():
        for copy in loads:
            copy.wait()

    def begin_more():
        for copy in later:
            copy.wait()
        store(shared_weight, shared_out)

    def fetch(copies):
        for copy in copies:
            copy.start()

    def forward(t, at, size):
        span, cols = span_of(t, TILE), pl.ds(at, size)
        g = dot_nn(picked[span, :], gate_weight[:, cols])
        u = dot_nn(picked[span, :], up_weight[:, cols])
        gate[span, cols] = g.astype(BF16)
        up[span, cols] = u.astype(BF16)
        act[span, cols] = (g * jax.nn.sigmoid(g) * u).astype(BF16)
        if at + size == hidden_units:
            store(act.at[span], act_out.at[span])

    def shared(i):
        span = span_of(i, TILE)
        raw = dot_nt(full[span, :], shared_weight[...])
        g, u = shared_gate[span, :].astype(F32), shared_up[span, :].astype(F32)
        silu, slope = sigmoid_parts(g)
        dg, du = (raw * u * slope).astype(BF16), (raw * silu).astype(BF16)
        inner[span, :] = jnp.broadcast_to(
            jnp.sum(g * dg.astype(F32) + u * du.astype(F32), 1, keepdims=True), (TILE, LANES)
        )
        shared_gate[span, :] = dg
        shared_up[span, :] = du

    def pick(q, t):
        tokens, span = span_of(q, 2 * TILE), span_of(t, TILE)
        here = lax.broadcasted_iota(jnp.int32, (TILE, 2 * TILE), 0) + t * TILE
        chosen = jnp.where(here == slot_row[:1, tokens], 1.0, 0.0).astype(BF16)
        term = dot_nn(chosen, full[tokens, :])
        if q == 0:
            grads[span, :] = term.astype(BF16)
        else:
            grads[span, :] = (grads[span, :].astype(F32) + term).astype(BF16)

    def fall_here():
        for swap in swaps:
            swap.wait()
        store(fall_weight, fall_out)

    staging = []

    def stage(value, target):
        slot = len(staging) % 2
        if len(staging) > 1:
            staging[-2].wait()
        staged[slot] = value
        copy = local(staged.at[slot], target)
        copy.start()
        staging.append(copy)

    def backward(t):
        span = span_of(t, TILE)
        scale = slot_gates[span, :1]
        raw_left = grads[span, :]
        gate_dot = jnp.zeros((TILE, 1), F32)
        slot_dot = jnp.zeros((TILE, 1), F32)
        for at, size in chunks:
            cols = pl.ds(at, size)
            raw = dot_nt(raw_left, fall_weight[cols, :])
            g, u = gate[span, cols].astype(F32), up[span, cols].astype(F32)
            gate_dot += jnp.sum(act[span, cols].astype(F32) * raw, 1, keepdims=True)
            silu, slope = sigmoid_parts(g)
            scaled = raw * scale
            dg, du = (scaled * u * slope).astype(BF16), (scaled * silu).astype(BF16)
            slot_dot += jnp.sum(g * dg.astype(F32) + u * du.astype(F32), 1, keepdims=True)
            gate[span, cols] = dg
            up[span, cols] = du
        values[span, :] = (
            three_terms(gate_dot, LANES, 0) + three_terms(slot_dot, LANES, 3)
        ).astype(BF16)
        grads[span, :] = (raw_left.astype(F32) * scale).astype(BF16)
        store(grads.at[span], grad_out.at[span])
        store(gate.at[span], dgate_out.at[span])
        store(up.at[span], dup_out.at[span])

    def to_rows(t):
        span = span_of(t, TILE)
        back = dot_nt(gate[span, :], gate_weight[...]) + dot_nt(up[span, :], up_weight[...])
        stage(back.astype(BF16), rows_out.at[span])

    def settle(i):
        span = span_of(i, TILE)
        here = lax.broadcasted_iota(jnp.int32, (TILE, capacity), 1)
        chosen = jnp.where(here == slot_cols[span, :1], 1.0, 0.0).astype(BF16)
        terms = dot_nn(chosen, values[...])
        lane = lax.broadcasted_iota(jnp.int32, terms.shape, 1)
        token_dot = jnp.sum(jnp.where(lane < 3, terms, 0.0), 1, keepdims=True)
        slot_dot = jnp.sum(jnp.where(lane >= 3, terms, 0.0), 1, keepdims=True)
        scores = logits[span, :]
        weights = jnp.exp(scores - jnp.max(scores, -1, keepdims=True))
        probs = weights / jnp.sum(weights, -1, keepdims=True)
        mine = jnp.where(lax.broadcasted_iota(jnp.int32, scores.shape, 1) == me, 1.0, 0.0)
        part = jnp.sum(probs * mine, -1, keepdims=True) * token_dot
        coef = (part * (mine - probs)).astype(BF16)
        coefs[span, :] = coef
        total = (
            inner[span, :1] + slot_dot + jnp.sum(coef.astype(F32) * scores, -1, keepdims=True)
        )
        stats[span, :] = jnp.where(lane == 0, total, jnp.where(lane == 1, part, 0.0))

    slots = range(capacity // TILE)

    def ready(p):
        tasks = [begin_more] if p == 0 else []
        tasks += [functools.partial(pick, p, t) for t in slots]
        tasks += [functools.partial(shared, i) for i in (2 * p, 2 * p + 1)]
        tasks.append(functools.partial(store, full.at[span_of(p, PIECE)], full_out.at[span_of(p, PIECE)]))
        if p == len(pieces) - 1:
            tasks.append(lambda: [store(shared_gate, sgate_out), store(shared_up, sup_out)])
            tasks.append(fall_here)
            for t in slots:
                tasks += [functools.partial(backward, t), functools.partial(to_rows, t)]
            tasks += [functools.partial(settle, i) for i in range(rows // TILE)]
        return tasks

    first_tasks = [
        functools.partial(fetch, loads[: len(loads) // 2 + 1]),
        functools.partial(fetch, loads[len(loads) // 2 + 1 :]),
        functools.partial(fetch, later[1:]),
        begin,
    ] + [
        functools.partial(forward, t, at, size) for t in slots for at, size in chunks
    ]
    work_through(gather_steps(row, z, y, c, depth, pieces, send_sem, recv_sem), ready, first_tasks)
    store(coefs, coef_out)
    store(stats, stat_out)
    for copy in results + staging[-2:]:
        copy.wait()


def mixture(
    block, picked, slot_row, slot_col, logits, slot_gate, gate_in, up_in,
    gate_pieces, up_pieces, fall, fall_got, shared_parts, collective_id,
):
    n, n_row = lax.axis_size("col"), lax.axis_size("row")
    depth, rows = n // 4, block.shape[0]
    width = n * block.shape[1]
    capacity, hidden_units = picked.shape[0], fall.shape[1]
    narrow, experts = gate_in.shape[1], logits.shape[1]
    anywhere = pl.BlockSpec(memory_space=pl.ANY)
    dma, shape = pltpu.SemaphoreType.DMA, jax.ShapeDtypeStruct
    count = rows // PIECE
    first = fall_got[0].shape[0] if fall_got else 0
    operands = [block, picked, slot_row, slot_col, logits, slot_gate, gate_in, up_in]
    operands += [*gate_pieces, *up_pieces, fall, *fall_got, *shared_parts]
    out_shape = [
        shape((hidden_units, width), BF16),
        shape((capacity, width), BF16),
        shape((capacity, hidden_units), BF16),
        shape((capacity, hidden_units), BF16),
        shape((capacity, hidden_units), BF16),
        shape((capacity, width), BF16),
        shape((rows, narrow), BF16),
        shape((rows, narrow), BF16),
        shape((rows, experts), BF16),
        shape((rows, LANES), F32),
        shape((rows, width), BF16),
        shape((narrow, width), BF16),
    ]
    return pl.pallas_call(
        functools.partial(
            mixture_kernel, depth, n_row, (rows, width, capacity, hidden_units, narrow, experts), first
        ),
        out_shape=out_shape,
        in_specs=[anywhere] * 2
        + [pl.BlockSpec(memory_space=pltpu.VMEM)]
        + [anywhere] * (len(operands) - 3),
        out_specs=[anywhere] * len(out_shape),
        scratch_shapes=[
            pltpu.VMEM((rows, width), BF16),
            pltpu.VMEM((width, hidden_units), BF16),
            pltpu.VMEM((width, hidden_units), BF16),
            pltpu.VMEM((hidden_units, width), BF16),
            pltpu.VMEM((capacity, width), BF16),
            pltpu.VMEM((capacity, hidden_units), BF16),
            pltpu.VMEM((capacity, hidden_units), BF16),
            pltpu.VMEM((capacity, hidden_units), BF16),
            pltpu.VMEM((capacity, width), BF16),
            pltpu.VMEM((narrow, width), BF16),
            pltpu.VMEM((rows, narrow), BF16),
            pltpu.VMEM((rows, narrow), BF16),
            pltpu.VMEM((rows, experts), F32),
            pltpu.VMEM((rows, LANES), jnp.int32),
            pltpu.VMEM((capacity, LANES), F32),
            pltpu.VMEM((capacity, LANES), BF16),
            pltpu.VMEM((rows, LANES), F32),
            pltpu.VMEM((rows, experts), BF16),
            pltpu.VMEM((rows, LANES), F32),
            pltpu.VMEM((2, TILE, width), BF16),
            dma((count, 8 * depth)),
            dma((count, n)),
            dma((96,)),
            dma((n_row,)),
            dma((n_row,)),
        ],
        compiler_params=pltpu.CompilerParams(
            collective_id=collective_id, has_side_effects=True, vmem_limit_bytes=63 << 20
        ),
        name="mixture",
    )(*operands)


def backward_kernel(depth, n_row, sizes, shifts, *refs):
    grad, loads, refs = refs[0], refs[1:18], refs[18:]
    swaps_in, refs = refs[: len(shifts)], refs[len(shifts) :]
    (gain_back, out_back, query_weight_back, up_weight_back), outs, refs = refs[:4], refs[4:8], refs[8:]
    swaps_out, refs = refs[: len(shifts)], refs[len(shifts) :]
    held, refs = refs[:17], refs[17:]
    (out_full, q, k, v, latent, low, latent_root, mixed, lse, up_full, choose, latent_gain) = held[:12]
    (cosines, sines, seg_col, seg_row, normed) = held[12:]
    (query_back, low_back, low_wide, inner), refs = refs[:4], refs[4:]
    results = (query_back, low_back, low_wide, inner)
    (full, keys_back, values_back, mixed_back), refs = refs[:4], refs[4:]
    (send_sem, recv_sem, local_sem, load_sem, out_sem, swap_send, swap_recv) = refs
    rows, width, seqs = sizes
    row, z, y, c = place()
    me, n = col_of(z, y, c), 4 * depth
    greet_neighbours(row, z, y, c, depth, n_row if shifts else 1)
    def lanes(block):
        return pl.ds(pl.multiple_of(rolled(block, row, n_row, n) * LANES, LANES), LANES)

    keep = pltpu.make_async_copy(grad, full.at[:, lanes(me)], local_sem)
    keep.start()
    fetches = [
        pltpu.make_async_copy(a, b, load_sem.at[i]) for i, (a, b) in enumerate(zip(loads, held))
    ]

    def result(array, seq):
        span = pl.ds(seq * LEN, LEN)
        span = (slice(None), span) if array == 2 else (span,)
        return pltpu.make_async_copy(results[array].at[span], outs[array].at[span], out_sem.at[array, seq])

    def store(seq):
        for array in range(4):
            result(array, seq).start()

    pieces = row_pieces(grad, rows, lambda span, block: full.at[span, lanes(block)])
    per_seq = LEN // TILE
    lower = lax.broadcasted_iota(jnp.int32, (TILE, LANES), 1) < ROPE

    def begin():
        keep.wait()
        for fetch in fetches:
            fetch.wait()
        for total in (gain_back, out_back, query_weight_back, up_weight_back):
            total[...] = jnp.zeros_like(total)

    def project(i):
        span = span_of(i, TILE)
        out_back[...] += dot_tn(mixed[span, :], full[span, :])
        mixed_back[...] = dot_nt(full[span, :], out_full[...]).astype(BF16)

    def attend(seq, block):
        base, first = seq * LEN, block * TILE
        length = first + TILE
        span, keys = pl.ds(base + first, TILE), pl.ds(base, length)
        at = pl.ds(first, TILE)
        grad_mixed = mixed_back[...]
        scores = masked_scores(q, k, seg_col, seg_row, base, first, length)
        probs = jnp.exp(scores - lse[span, :1])
        grad_probs = dot_nt(grad_mixed, v[keys, :])
        grad_scores = (
            probs * (grad_probs - jnp.sum(probs * grad_probs, -1, keepdims=True))
        ).astype(BF16)
        back = dot_nn(grad_scores, k[keys, :]) * SCALE
        nope, tile = back[:, :NOPE], back[:, NOPE:]
        inner[span, :] = jnp.broadcast_to(
            jnp.sum(nope * q[span, :NOPE].astype(F32), 1, keepdims=True)
            + 0.5 * jnp.sum(tile * q[span, NOPE:].astype(F32), 1, keepdims=True),
            (TILE, LANES),
        )
        query_back[span, :NOPE] = nope.astype(BF16)
        turned = turn(tile, cosines[at, :], -sines[at, :])
        query_back[span, NOPE:] = jnp.where(lower, turned, 0.0).astype(BF16)
        keys_term = dot_tn(grad_scores, q[span, :])
        values_term = dot_tn(probs.astype(BF16), grad_mixed)
        keys_back[first:length, :] = keys_term[first:, :]
        values_back[first:length, :] = values_term[first:, :]
        if first:
            keys_back[:first, :] += keys_term[:first, :]
            values_back[:first, :] += values_term[:first, :]

    def weigh(i):
        span = span_of(i, TILE)
        query_weight_back[...] += dot_tn(query_back[span, :], normed[span, :])

    def expand(seq, block):
        first = block * TILE
        span, at = pl.ds(seq * LEN + first, TILE), pl.ds(first, TILE)
        back = keys_back[at, :] * SCALE
        expanded = jnp.concatenate([back[:, :NOPE], values_back[at, :]], 1).astype(BF16)
        up_weight_back[...] += dot_tn(expanded, latent[span, :])
        latent_grad = dot_nt(expanded, up_full[...])
        compressed = low[span, :LATENT].astype(F32)
        root = latent_root[span, :1]
        dots = jnp.sum(latent_grad * latent[span, :].astype(F32), 1, keepdims=True)
        gain_back[...] += jnp.broadcast_to(
            jnp.sum(latent_grad * compressed * root, 0, keepdims=True), gain_back.shape
        )
        compressed_grad = root * latent_grad * latent_gain[:1, :] - compressed * (
            root * root * dots / LATENT
        )
        turned = turn(back[:, NOPE:], cosines[at, :], -sines[at, :])
        low_grad = jnp.concatenate([compressed_grad, jnp.where(lower, turned, 0.0)], 1).astype(BF16)
        low_back[span, :] = low_grad
        low_wide[:, span] = dot_nt(choose[...], low_grad).astype(BF16)
        inner[span, :] += jnp.broadcast_to(
            jnp.sum(low_grad.astype(F32) * low[span, :].astype(F32), 1, keepdims=True),
            (TILE, LANES),
        )

    def ready(p):
        tasks = [begin] if p == 0 else []
        for i in (2 * p, 2 * p + 1):
            seq, block = divmod(i, per_seq)
            tasks += [functools.partial(project, i), functools.partial(attend, seq, block)]
            tasks.append(functools.partial(weigh, i))
            if block == per_seq - 1:
                tasks += [functools.partial(expand, seq, b) for b in range(per_seq)]
                tasks.append(functools.partial(store, seq))
        return tasks

    swaps = swap_start(row, me, n_row, shifts, swaps_in, swaps_out, swap_send, swap_recv)
    first_tasks = [
        lambda: [fetch.start() for fetch in fetches[:8]],
        lambda: [fetch.start() for fetch in fetches[8:]],
    ]
    work_through(gather_steps(row, z, y, c, depth, pieces, send_sem, recv_sem), ready, first_tasks)
    for seq in range(seqs):
        for array in range(4):
            result(array, seq).wait()
    for swap in swaps:
        swap.wait()


def attention_backward(grad, operands, collective_id, swaps=()):
    n, n_row = lax.axis_size("col"), lax.axis_size("row")
    depth, rows = n // 4, grad.shape[0]
    width, seqs = n * grad.shape[1], rows // LEN
    in_vmem = pl.BlockSpec(memory_space=pltpu.VMEM)
    anywhere = pl.BlockSpec(memory_space=pl.ANY)
    count = rows // PIECE
    dma = pltpu.SemaphoreType.DMA
    shape = jax.ShapeDtypeStruct
    swapped = [swap.array for swap in swaps]
    kept = [
        shape((rows, 2 * LANES), BF16),
        shape((rows, LATENT + LANES), BF16),
        shape((operands[10].shape[0], rows), BF16),
        shape((rows, LANES), F32),
    ]
    return pl.pallas_call(
        functools.partial(
            backward_kernel, depth, n_row, (rows, width, seqs), tuple((swap.t, swap.index) for swap in swaps)
        ),
        out_shape=[
            shape((8, LATENT), F32),
            shape((VD, width), F32),
            shape((2 * LANES, width), F32),
            shape((2 * LANES, LATENT), F32),
        ]
        + kept
        + [swap.shape for swap in swaps],
        in_specs=[anywhere] * (18 + len(swapped)),
        out_specs=[in_vmem] * 4 + [anywhere] * (4 + len(swapped)),
        scratch_shapes=[pltpu.VMEM(a.shape, a.dtype) for a in [*operands, *kept]]
        + [
            pltpu.VMEM((rows, width), BF16),
            pltpu.VMEM((LEN, 2 * LANES), F32),
            pltpu.VMEM((LEN, VD), F32),
            pltpu.VMEM((TILE, VD), BF16),
            dma((count, 8 * depth)),
            dma((count, n)),
            dma,
            dma((17,)),
            dma((4, seqs)),
            dma((max(1, len(swapped)),)),
            dma((max(1, len(swapped)),)),
        ],
        compiler_params=pltpu.CompilerParams(
            collective_id=collective_id, has_side_effects=True, vmem_limit_bytes=60 << 20
        ),
        name="attention_backward",
    )(grad, *operands, *swapped)


def row_shift(array, step):
    n = lax.axis_size("row")
    return lax.ppermute(array, "row", [(i, (i - step) % n) for i in range(n)])


def to_others(*arrays):
    pairs = [array if isinstance(array, tuple) else (array, ()) for array in arrays]
    return [Swap(array, t, index) for array, index in pairs for t in range(1, lax.axis_size("row"))]


def from_others(got, index):
    others = lax.axis_size("row") - 1
    return got[index * others : (index + 1) * others][::-1]


def row_parts(array):
    return [array] + [row_shift(array, s) for s in range(1, lax.axis_size("row"))]


def row_sum(parts):
    return row_add(parts[0], [part.astype(BF16) for part in parts[1:]])


def row_add(total, parts):
    n = lax.axis_size("row")
    return row_sum_of(total, [row_shift(part, n - s) for s, part in enumerate(parts, 1)])


def row_sum_of(total, received):
    for part in received:
        total = total + part.astype(F32)
    return total


def unroll_parts(parts, axis):
    n = len(parts)
    size = parts[0].shape[axis]
    doubled = jnp.concatenate(parts + parts[:-1], axis)
    start = lax.rem(n - lax.axis_index("row"), n) * size
    return lax.dynamic_slice_in_dim(doubled, start, n * size, axis)


def own_parts(array, axis):
    n = lax.axis_size("row")
    size = array.shape[axis] // n
    row = lax.axis_index("row")
    return [
        lax.dynamic_slice_in_dim(array, lax.rem(row + s, n) * size, size, axis) for s in range(n)
    ]


def interleave(first, second):
    return [array for pair in zip(first, second) for array in pair]


def cut(array, axis):
    return jnp.split(array, lax.axis_size("row"), axis)


def as_stat(*vectors):
    return jnp.concatenate([v.reshape(-1, LANES) for v in vectors], 0)


def per_device(
    tokens,
    cotangent,
    segments,
    routes,
    first_gain,
    query_proj,
    latent_down,
    latent_gain,
    latent_up,
    output_proj,
    second_gain,
    router_weight,
    expert_gate,
    expert_up,
    expert_down,
    shared_gate,
    shared_up,
    shared_down,
):
    row_count, share = tokens.shape
    n = lax.axis_size("col")
    width = share * n
    column = lax.axis_index("col")
    seqs = segments.shape[0]
    narrow = latent_down.shape[1]
    padding = -narrow % 16
    tables = rotary_tables()
    seg_flat = segments.reshape(-1)
    seg_col = jnp.broadcast_to(seg_flat[:, None], (row_count, LANES))
    seg_row = jnp.broadcast_to(seg_flat[None, :], (8, row_count))
    column_of = np.arange(n * narrow)
    turned_of = np.concatenate([column_of, column_of[LATENT + 32 :], column_of[LATENT : LATENT + 32]])
    wide_of = turned_of // narrow * (narrow + padding) + turned_of % narrow
    choose = jnp.asarray((np.arange(n * (narrow + padding))[:, None] == wide_of[None, :]).astype(BF16))

    experts = router_weight.shape[1]
    capacity = row_count * routes.shape[1] * 4 // (3 * experts)
    member = jnp.any(routes == column, 1)
    slot_number = jnp.where(member, jnp.cumsum(member.astype(jnp.int32)) - 1, -1)
    slot_row = jnp.broadcast_to(slot_number[None, :], (8, row_count))
    slot_col = jnp.broadcast_to(slot_number[:, None], (row_count, LANES))
    part = expert_gate.shape[1]
    gate_cut, up_cut, fall_first = part * 11 // 16, part // 2, 2 * LANES
    gate_low, gate_high = (0, (0, gate_cut)), (0, (gate_cut, part - gate_cut))
    up_low, up_high = (0, (0, up_cut)), (0, (up_cut, part - up_cut))
    pick_back = (slot_number[:, None] == jnp.arange(capacity)[None, :]).astype(BF16)

    latent_gains = jnp.broadcast_to(latent_gain[None, :], (8, LATENT))
    (
        normed,
        queries,
        keys,
        values,
        latent,
        low,
        first_root,
        latent_root,
        mixed,
        log_total,
        query_full,
        down_full,
        up_full,
        *got,
    ) = attention_forward(
        tokens,
        jnp.broadcast_to(first_gain[None, :], (8, share)),
        with_exchanged(query_proj.T),
        jnp.pad(latent_down.T, ((0, padding), (0, 0))),
        latent_up,
        choose,
        latent_gains,
        tables,
        seg_col,
        seg_row,
        1,
        to_others(
            output_proj, shared_gate.T, shared_up.T, router_weight.T, (expert_gate, gate_low)
        ),
    )
    out_full = jnp.concatenate([output_proj] + from_others(got, 0), 1)
    shared_gate_parts = [shared_gate.T] + from_others(got, 1)
    shared_up_parts = [shared_up.T] + from_others(got, 2)
    router_parts = [router_weight.T] + from_others(got, 3)
    gate_first = from_others(got, 4)
    first_root = first_root[:, :1]
    branch, *got = scatter_cols(
        [("nn", mixed, out_full)], None, 2, 2, to_others((expert_gate, gate_high), (expert_up, up_low))
    )
    gate_pieces = [expert_gate] + interleave(gate_first, from_others(got, 0))
    up_first = from_others(got, 1)
    hidden = tokens.astype(F32) + branch
    (
        normed_two,
        picked,
        shared_in,
        shared_lift,
        shared_act,
        logits,
        second_root,
        slot_gate,
        shared_gate_full,
        shared_up_full,
        router_full,
        *got,
    ) = hidden_rows(
        (hidden * second_gain).astype(BF16),
        as_stat(jnp.sum(hidden * hidden, 1)),
        slot_row,
        shared_gate_parts + shared_up_parts + router_parts,
        capacity,
        3,
        to_others((expert_up, up_high), shared_down, (expert_down, (0, (0, fall_first)))),
    )
    second_root = second_root[:, :1]
    up_pieces = [expert_up] + interleave(up_first, from_others(got, 0))
    (
        fall_full,
        picked_back,
        activation,
        grad_gate_in,
        grad_up_in,
        slot_grad,
        shared_gin,
        shared_gup,
        coefficient,
        stat,
        grad_full,
        shared_down_full,
    ) = mixture(
        cotangent,
        picked,
        slot_row,
        slot_col,
        logits,
        slot_gate,
        shared_in,
        shared_lift,
        gate_pieces,
        up_pieces,
        expert_down,
        from_others(got, 2),
        [shared_down] + from_others(got, 1),
        4,
    )
    n_row = lax.axis_size("row")
    units = activation.shape[1]
    other = range(1, n_row)

    def part_of(array, p):
        return (array, ((0, array.shape[0]), (p * part, part)))

    part_tiles = [(at, min(TILE, part - at), 0, units) for at in range(0, part, TILE)]
    fall_tiles = [(at, min(3 * LANES, units - at), 0, part) for at in range(0, units, 3 * LANES)]

    def sent_rows(arrays, tiles, some):
        return [
            Swap(array, t, ((tiles[i][0], tiles[i][1]),))
            for i in some
            for t, array in enumerate(arrays, 1)
        ]

    fall_sent = [
        dot_tn(activation, slot_grad[:, p * part : (p + 1) * part]).astype(BF16) for p in other
    ]
    fall_split = max(1, len(fall_tiles) * 3 // 4)
    fall_now, fall_late = range(fall_split), range(fall_split, len(fall_tiles))
    part_split = max(1, len(part_tiles) // 2)
    part_now, part_late = range(part_split), range(part_split, len(part_tiles))
    rows_all = (0, row_count)
    expert_tiles = [(at, TILE, 0, width) for at in range(0, capacity, TILE)]

    grad_normed_two, stats, *got = scatter_cols(
        [
            ("nn", pick_back, picked_back),
            ("nn", shared_gin, shared_gate_full),
            ("nn", shared_gup, shared_up_full),
            ("nn", coefficient, router_full),
        ],
        as_stat(stat[:, 0], stat[:, 1]),
        2,
        5,
        sent_rows(fall_sent, fall_tiles, fall_now),
        jobs=[Job("tn", part_of(picked, p), (grad_gate_in, ()), part_tiles, BF16) for p in other]
        + [Job("tn", part_of(picked, p), (grad_up_in, ()), part_tiles, BF16) for p in other]
        + [Job("nn", (activation, ()), (fall_full, ()), expert_tiles, BF16, scale=(slot_gate, ()))],
    )
    fall_got, got = got[: len(fall_now) * len(other)], got[len(fall_now) * len(other) :]
    gate_sent, up_sent, (expert_out,) = got[: len(other)], got[len(other) : 2 * len(other)], got[-1:]

    wide_tiles = [(0, shared_act.shape[1], at, 4 * LANES) for at in range(0, width, 4 * LANES)]
    branch, *got = scatter_cols(
        [("nn", pick_back, expert_out), ("nn", shared_act, shared_down_full)],
        None,
        2,
        7,
        sent_rows(fall_sent, fall_tiles, fall_late) + sent_rows(gate_sent, part_tiles, part_now),
        jobs=[
            Job("tn", (shared_gin, ()), (normed_two, ()), wide_tiles, F32),
            Job("tn", (shared_gup, ()), (normed_two, ()), wide_tiles, F32),
            Job("tn", (shared_act, ()), (grad_full, ()), wide_tiles, F32),
        ],
    )
    fall_got += got[: len(fall_late) * len(other)]
    gate_got = got[len(fall_late) * len(other) : -3]
    shared_grads = [cut(array, 1) for array in got[-3:]]
    shared_sent = [[array.astype(BF16) for array in arrays[1:]] for arrays in shared_grads]
    output = (hidden + branch).astype(BF16)
    grad_normed_two, output = lax.optimization_barrier((grad_normed_two, output))
    stats = stats.reshape(n, 2, row_count)
    inner_total = jnp.sum(stats[:, 0], 0)[:, None]
    shares = stats[:, 1].T
    logit_grad = shares - jax.nn.softmax(logits, -1) * jnp.sum(shares, 1, keepdims=True)
    grad_stream = cotangent.astype(F32)
    grad_hidden = (
        grad_stream
        + second_root * (grad_normed_two * second_gain)
        - hidden * (second_root * second_root * inner_total / width)
    )
    second_gain_grad = jnp.sum(grad_normed_two * hidden * second_root, 0)
    def whole(arrays):
        return [Swap(array, t) for t, array in enumerate(arrays, 1)]

    (
        latent_gain_grad,
        output_grad,
        query_grad,
        up_grad,
        query_back,
        low_back,
        low_wide,
        inner,
        *got,
    ) = attention_backward(
        grad_hidden.astype(BF16),
        (
            out_full,
            queries,
            keys,
            values,
            latent,
            low,
            latent_root,
            mixed,
            log_total,
            up_full,
            choose,
            latent_gains,
            *tables,
            seg_col,
            seg_row,
            normed,
        ),
        6,
        sent_rows(gate_sent, part_tiles, part_late)
        + sent_rows(up_sent, part_tiles, part_tiles and [0])
        + whole(shared_sent[0]),
    )
    gate_count = len(part_late) * len(other)
    gate_got += got[:gate_count]
    up_got = got[gate_count : gate_count + len(other)]
    shared_got = [got[gate_count + len(other) :]]

    attn_grads = [
        cut(query_grad[:QK], 1),
        cut(output_grad, 1),
        own_parts(up_grad, 1),
    ]
    attn_sent = [[array.astype(BF16) for array in arrays[1:]] for arrays in attn_grads]
    swaps = sent_rows(up_sent, part_tiles, range(1, len(part_tiles)))
    in_flight = len(swaps)

    def by_tile(got, count):
        return [list(got[i * len(other) : (i + 1) * len(other)]) for i in range(count)]

    grad_normed, low_own, stats, *got = scatter_cols(
        [("nn", query_back, query_full), ("tn", low_wide, down_full)],
        as_stat(inner[:, 0], latent_gain_grad[0], jnp.zeros((-LATENT % 1024,), F32)),
        2,
        8,
        swaps
        + whole(shared_sent[1])
        + whole(shared_sent[2])
        + [swap for arrays in attn_sent for swap in whole(arrays)],
        low_wide,
        jobs=[
            Job(
                "tn", (activation, ()), part_of(slot_grad, 0), fall_tiles, F32,
                add=by_tile(fall_got, len(fall_tiles)),
            ),
            Job(
                "tn", part_of(picked, 0), (grad_gate_in, ()), part_tiles, F32,
                add=by_tile(gate_got, len(part_tiles)),
            ),
            Job(
                "tn", part_of(picked, 0), (grad_up_in, ()), part_tiles, F32,
                add=by_tile(up_got + list(range(in_flight)), len(part_tiles)),
            ),
        ],
    )
    fall_grad, gate_grad, up_proj_grad = got[-3:]
    got = by_tile(got[in_flight:-3], 2 + len(attn_sent))
    shared_got += got[:2]
    stats = jnp.sum(stats, 0).reshape(-1)
    inner_total = stats[:row_count, None]
    latent_gain_sum = stats[row_count : row_count + LATENT]
    stream = tokens.astype(F32)
    grad_input = (
        grad_hidden
        + first_root * (grad_normed * first_gain)
        - stream * (first_root * first_root * inner_total / width)
    )
    first_gain_grad = jnp.sum(grad_normed * stream * first_root, 0)
    shared_total = [row_sum_of(a[0], b) for a, b in zip(shared_grads, shared_got)]
    query_total, out_total, up_total = [row_sum_of(a[0], b) for a, b in zip(attn_grads, got[2:])]
    gain_grads = lax.psum((first_gain_grad, second_gain_grad, latent_gain_sum), "row")
    return (
        output,
        grad_input.astype(BF16),
        gain_grads[0],
        query_total.T,
        row_sum(cut(dot_nn(low_own.astype(BF16), normed)[:narrow].T, 0)),
        gain_grads[2],
        up_total.T,
        out_total,
        gain_grads[1],
        row_sum(cut(dot_tn(normed_two, logit_grad.astype(BF16)), 0)),
        gate_grad[None],
        up_proj_grad[None],
        fall_grad[None],
        shared_total[0].T,
        shared_total[1].T,
        shared_total[2],
    )


def solution(mesh):
    return jax.shard_map(
        per_device,
        mesh=mesh,
        in_specs=(
            P("row", "col"),
            P("row", "col"),
            P("row", None),
            P("row", None),
            P("col"),
            P("row", "col"),
            P("row", "col"),
            P(),
            P("row", "col"),
            P("col", "row"),
            P("col"),
            P("row", None),
            P("col", "row", None),
            P("col", "row", None),
            P("col", None, "row"),
            P("row", "col"),
            P("row", "col"),
            P("col", "row"),
        ),
        out_specs=(
            P("row", "col"),
            P("row", "col"),
            P("col"),
            P("row", "col"),
            P("row", "col"),
            P(),
            P("row", "col"),
            P("col", "row"),
            P("col"),
            P("row", None),
            P("col", "row", None),
            P("col", "row", None),
            P("col", None, "row"),
            P("row", "col"),
            P("row", "col"),
            P("col", "row"),
        ),
        check_vma=False,
    )
```

```python
import functools
import itertools

import jax
import jax.numpy as jnp
import numpy as np
from jax import lax
from jax.experimental import pallas as pl
from jax.experimental.pallas import tpu as pltpu
from jax.sharding import PartitionSpec as P

NOPE = 128
ROPE = 64
VD = 128
LATENT = 512
LEN = 1024
WINDOW = 1024
EPSILON = 1e-06
LANES = 128
MESH = pl.DeviceIdType.MESH
BF16 = jnp.bfloat16
F32 = jnp.float32
UP, DOWN, SIDE, CORE = range(4)
TILE = 256
PIECE = 2 * TILE


def dot_nn(a, b):
    return jnp.dot(a, b, preferred_element_type=F32)


def dot_nt(a, b):
    return lax.dot_general(a, b, (((1,), (1,)), ((), ())), preferred_element_type=F32)


def dot_tn(a, b):
    return lax.dot_general(a, b, (((0,), (0,)), ((), ())), preferred_element_type=F32)


def place():
    me = lax.axis_index("col")
    return lax.axis_index("row"), me // 4, (me // 2) % 2, me % 2


def col_of(z, y, c):
    return z * 4 + y * 2 + c


def rolled(index, row, n_row, count):
    return lax.rem(index + count - row * (count // n_row), count)


def signal(row, target):
    pl.semaphore_signal(
        pltpu.get_barrier_semaphore(), inc=1, device_id=(row, target), device_id_type=MESH
    )


def greet_row(row, me, n_row):
    for t in range(1, n_row):
        signal(lax.rem(row + t, n_row), me)
    pl.semaphore_wait(pltpu.get_barrier_semaphore(), n_row - 1)


def greet_neighbours(row, z, y, c, depth, n_row=1):
    for t in range(1, n_row):
        signal(lax.rem(row + t, n_row), col_of(z, y, c))
    signal(row, col_of(z, 1 - y, c))
    signal(row, col_of(z, y, 1 - c))

    @pl.when(z > 0)
    def _():
        signal(row, col_of(z - 1, y, c))

    @pl.when(z < depth - 1)
    def _():
        signal(row, col_of(z + 1, y, c))

    count = 1 + n_row + (z > 0).astype(jnp.int32) + (z < depth - 1).astype(jnp.int32)
    pl.semaphore_wait(pltpu.get_barrier_semaphore(), count)


class Swap:
    def __init__(self, array, t, index=()):
        self.array, self.t = array, t
        self.index = tuple(i if isinstance(i, int) else pl.ds(*i) for i in index)
        shape = [i[1] for i in index if not isinstance(i, int)] + list(array.shape[len(index) :])
        self.shape = jax.ShapeDtypeStruct(shape, array.dtype)


def swap_start(row, me, n_row, swaps, sources, targets, send_sem, recv_sem):
    copies = [
        swap_copy(
            row, me, n_row, source.at[index] if index else source, target, t,
            send_sem.at[i], recv_sem.at[i],
        )
        for i, ((t, index), source, target) in enumerate(zip(swaps, sources, targets))
    ]
    for copy in copies:
        copy.start()
    return copies


def swap_copy(row, me, n_row, source, target, t, send_sem, recv_sem):
    return pltpu.make_async_remote_copy(
        src_ref=source, dst_ref=target, send_sem=send_sem, recv_sem=recv_sem,
        device_id=(lax.rem(row + t, n_row), me), device_id_type=MESH,
    )


def greet_all(row, me, n, n_row=1):
    for t in range(1, n_row):
        signal(lax.rem(row + t, n_row), me)

    def hello(step, carry):
        signal(row, lax.rem(me + step, n))
        return carry

    lax.fori_loop(1, n, hello, 0)
    pl.semaphore_wait(pltpu.get_barrier_semaphore(), n + n_row - 2)


class Job:
    def __init__(self, kind, left, right, tiles, dtype, scale=None, add=None):
        self.kind, self.tiles, self.dtype, self.add = kind, tiles, dtype, add
        self.operands = [left, right] + ([scale] if scale is not None else [])
        shapes = [Swap(array, 0, index).shape.shape for array, index in (left, right)]
        self.shape = jax.ShapeDtypeStruct((shapes[0][kind == "tn"], shapes[1][1]), dtype)


class Jobs:
    def __init__(self, jobs):
        self.jobs, self.arrays, self.indices, self.shapes, self.uses = jobs, [], [], [], []
        known = {}
        for job in jobs:
            use = []
            for array, index in job.operands:
                key = (id(array), index)
                if key not in known:
                    known[key] = len(self.arrays)
                    swap = Swap(array, 0, index)
                    self.arrays.append(array)
                    self.indices.append(swap.index)
                    self.shapes.append(swap.shape)
                use.append(known[key])
            self.uses.append(use)
        self.added = [a for job in jobs for tile in job.add or () for a in tile if not isinstance(a, int)]
        self.stage = (
            max([rows for job in jobs for _, rows, _, _ in job.tiles] or [0]),
            max([columns for job in jobs for _, _, _, columns in job.tiles] or [0]),
        )
        self.dtype = jobs[0].dtype if jobs else F32
        self.count = len(self.arrays) + 2 * sum(len(job.tiles) for job in jobs) + len(self.added)
        self.count += sum(isinstance(a, int) for job in jobs for tile in job.add or () for a in tile)

    def tasks(self, arrays, added, outs, swaps, swaps_out, held, staged, taken, sem):
        local = copier(sem)
        loads = [
            local(array.at[index] if index else array, target)
            for array, index, target in zip(arrays, self.indices, held)
        ]
        middle = len(loads) // 2
        tasks = [
            lambda: [load.start() for load in loads[:middle]],
            lambda: [load.start() for load in loads[middle:]],
        ]
        waited, stores = set(), []
        added = list(added)

        def work(job, use, out, tile, extra):
            for i in use:
                if i not in waited:
                    waited.add(i)
                    loads[i].wait()
            row, rows, column, columns = tile
            takes = []
            for i, source in enumerate(extra):
                if isinstance(source, int):
                    swaps[source].wait_recv()
                    source = swaps_out[source]
                takes.append(local(source, taken.at[pl.ds(0, rows), pl.ds(0, columns)]))
            for take in takes[:1]:
                take.start()
            left, right = held[use[0]], held[use[1]]
            if job.kind == "tn":
                value = dot_tn(left[:, pl.ds(row, rows)], right[:, pl.ds(column, columns)])
            else:
                value = dot_nn(left[pl.ds(row, rows), :], right[:, pl.ds(column, columns)])
                if len(use) > 2:
                    value = value * held[use[2]][pl.ds(row, rows), :1]
            slot = len(stores) % 2
            if len(stores) > 1:
                stores[-2].wait()
            spot = staged.at[slot, pl.ds(0, rows), pl.ds(0, columns)]
            for i, take in enumerate(takes):
                if i:
                    take.start()
                take.wait()
                value = value + taken[pl.ds(0, rows), pl.ds(0, columns)].astype(F32)
            spot[...] = value.astype(job.dtype)
            store = local(spot, out.at[pl.ds(row, rows), pl.ds(column, columns)])
            store.start()
            stores.append(store)

        for job, use, out in zip(self.jobs, self.uses, outs):
            for i, tile in enumerate(job.tiles):
                extra = [a if isinstance(a, int) else added.pop(0) for a in (job.add[i] if job.add else ())]
                tasks.append(functools.partial(work, job, use, out, tile, extra))
        return tasks, stores


def scatter_kernel(depth, n_row, parts, kinds, has_stat, has_extra, shifts, jobs, *refs):
    count = 2 * len(kinds) + has_stat + has_extra
    extra = refs[count - 1 - has_stat] if has_extra else None
    operands, stat = refs[: 2 * len(kinds)], refs[count - 1] if has_stat else None
    swaps_in, refs = refs[count : count + len(shifts)], refs[count + len(shifts) :]
    job_arrays, refs = refs[: len(jobs.arrays)], refs[len(jobs.arrays) :]
    job_added, refs = refs[: len(jobs.added)], refs[len(jobs.added) :]
    out = refs[0]
    extra_out = refs[1] if has_extra else None
    refs = refs[has_extra:]
    stats = refs[1] if has_stat else None
    swaps_out = refs[1 + has_stat : 1 + has_stat + len(shifts)]
    refs = refs[1 + has_stat + len(shifts) :]
    job_outs, rest = refs[: len(jobs.jobs)], refs[len(jobs.jobs) :]
    if jobs.jobs:
        held = rest[-len(jobs.arrays) - 3 : -3]
        job_staged, job_taken, job_sem = rest[-3:]
        rest = rest[: -len(jobs.arrays) - 3]
    (load_sem, *loaded), rest = rest[: 1 + len(operands)], rest[1 + len(operands) :]
    local = copier(load_sem)
    loads = [local(a, b) for a, b in zip(operands, loaded)]
    for load in loads:
        load.start()
    operands = loaded
    mine, core_send, core_recv, side_send, side_recv, line_send, line_recv = rest[:7]
    cs, cr, ss, sr, ls, lr = rest[7:13]
    extra_core, extra_side_send, extra_side, extra_line_send, extra_line = rest[-7:-2] if has_extra else [None] * 5
    row, z, y, c = place()
    me, n = col_of(z, y, c), 4 * depth
    pairs = 2 * depth
    rows = out.shape[0]
    size = rows // parts
    tile = min(256, size)
    if has_stat:
        stat_held, stat_send, stat_recv = rest[13:16]
        greet_all(row, me, n, n_row if shifts else 1)

        def stat_copy(step):
            target = lax.rem(me + step, n)
            return pltpu.make_async_remote_copy(
                src_ref=stat,
                dst_ref=stat_held.at[me],
                send_sem=stat_send.at[step],
                recv_sem=stat_recv.at[me],
                device_id=(row, target),
                device_id_type=MESH,
            )

        for step in range(1, n):
            stat_copy(step).start()
    else:
        greet_neighbours(row, z, y, c, depth, n_row if shifts else 1)
    swaps = swap_start(row, me, n_row, shifts, swaps_in, swaps_out, rest[-2], rest[-1])
    up, down = col_of(z + 1, y, c), col_of(z - 1, y, c)
    side, core = col_of(z, 1 - y, c), col_of(z, y, 1 - c)

    def remote(src, dst, send, recv, target):
        return pltpu.make_async_remote_copy(
            src_ref=src, dst_ref=dst, send_sem=send, recv_sem=recv,
            device_id=(row, target), device_id_type=MESH,
        )

    def span(h):
        return pl.ds(h * size, size)

    def block_of(s, cc):
        return col_of(order(s % depth), 1 - y if s < depth else y, cc)

    def extra_rows(s, cc):
        size = extra.shape[0] // n
        return extra.at[pl.ds(pl.multiple_of(block_of(s, cc) * size, 16), size)]

    def mine_at(s, h):
        return mine.at[s, span(h)] if h < parts else extra_rows(s, c)

    def core_recv_at(s, h):
        return core_recv.at[s, span(h)] if h < parts else extra_core.at[s]

    def side_send_at(k, h):
        return side_send.at[k, span(h)] if h < parts else extra_side_send.at[k]

    def side_recv_at(k, h):
        return side_recv.at[k, span(h)] if h < parts else extra_side.at[k]

    def line_send_at(zz, h):
        return line_send.at[zz, span(h)] if h < parts else extra_line_send.at[zz]

    def line_recv_at(way, zz, h):
        slot = zz + 1 - way
        return line_recv.at[slot, span(h)] if h < parts else extra_line.at[slot]

    def out_at(h):
        return out.at[span(h)] if h < parts else extra_out

    def core_copy(s, h):
        source = core_send.at[s % depth, span(h)] if h < parts else extra_rows(s, 1 - c)
        return remote(source, core_recv_at(s, h), cs.at[s, h], cr.at[s, h], core)

    def side_copy(k, h):
        return remote(side_send_at(k, h), side_recv_at(k, h), ss.at[k, h], sr.at[k, h], side)

    def line_copy(way, zz, h, target):
        return remote(
            line_send_at(zz, h), line_recv_at(way, zz, h), ls.at[zz, h], lr.at[way, zz, h], target
        )

    low_half = z < depth // 2

    def order(k):
        if k == depth - 1:
            return z
        from_top = depth - 1 - k
        from_top = from_top - (from_top <= z).astype(jnp.int32)
        from_low = k + (k >= z).astype(jnp.int32)
        return jnp.where(low_half, from_top, from_low)

    def tiles(body):
        def step(i, carry):
            body(i)
            return carry

        lax.fori_loop(0, size // tile, step, 0)

    def multiply(s, h):
        if h == parts:
            core_copy(s, h).start()
            return
        yy = 1 - y if s < depth else y
        pair = rolled(order(s % depth) * 2 + yy, row, n_row, pairs)
        cols = pl.ds(pl.multiple_of(pair * 2 * LANES, 2 * LANES), 2 * LANES)

        def body(i):
            at = pl.ds(pl.multiple_of(h * size + i * tile, tile), tile)
            total = None
            for j, kind in enumerate(kinds):
                left, right = operands[2 * j], operands[2 * j + 1]
                if kind == "nn":
                    term = dot_nn(left[at, :], right[:, cols])
                elif kind == "tn":
                    term = dot_tn(left[:, at], right[:, cols])
                else:
                    term = dot_nt(left[at, :], right[cols, :])
                total = term if total is None else total + term
            first, second = total[:, :LANES], total[:, LANES:]
            mine[s, at, :] = jnp.where(c == 0, first, second).astype(BF16)
            core_send[s % depth, at, :] = jnp.where(c == 0, second, first).astype(BF16)

        tiles(body)
        core_copy(s, h).start()

    def add_up(target, sources):
        step = min(tile, target.shape[0])

        def body(i, carry):
            at = pl.ds(pl.multiple_of(i * step, step), step)
            total = sources[0][at, :].astype(F32)
            for source in sources[1:]:
                total = total + source[at, :].astype(F32)
            target[at, :] = total.astype(target.dtype)
            return carry

        lax.fori_loop(0, target.shape[0] // step, body, 0)

    def fold(s, h):
        core_copy(s, h).wait_recv()
        k = s % depth
        sources = [mine_at(s, h), core_recv_at(s, h)]
        if s < depth:
            add_up(side_send_at(k, h), sources)
            side_copy(k, h).start()
            return
        side_copy(k, h).wait_recv()
        sources.append(side_recv_at(k, h))
        zz = order(k)
        if k < depth - 1:

            @pl.when(zz > z)
            def _():
                @pl.when(z > 0)
                def _():
                    line_copy(0, zz, h, up).wait_recv()
                    add_up(line_send_at(zz, h), sources + [line_recv_at(0, zz, h)])

                @pl.when(z == 0)
                def _():
                    add_up(line_send_at(zz, h), sources)

                line_copy(0, zz, h, up).start()

            @pl.when(zz < z)
            def _():
                @pl.when(z < depth - 1)
                def _():
                    line_copy(1, zz, h, down).wait_recv()
                    add_up(line_send_at(zz, h), sources + [line_recv_at(1, zz, h)])

                @pl.when(z == depth - 1)
                def _():
                    add_up(line_send_at(zz, h), sources)

                line_copy(1, zz, h, down).start()

            return

        @pl.when((z > 0) & (z < depth - 1))
        def _():
            line_copy(0, z, h, me).wait_recv()
            line_copy(1, z, h, me).wait_recv()
            add_up(out_at(h), sources + [line_recv_at(0, z, h), line_recv_at(1, z, h)])

        @pl.when(z == 0)
        def _():
            line_copy(1, z, h, me).wait_recv()
            add_up(out_at(h), sources + [line_recv_at(1, z, h)])

        @pl.when(z == depth - 1)
        def _():
            line_copy(0, z, h, me).wait_recv()
            add_up(out_at(h), sources + [line_recv_at(0, z, h)])

    chunks = parts + has_extra
    steps = [(s, h) for s in range(2 * depth) for h in range(chunks)]
    tasks, stores = [], []
    if jobs.jobs:
        tasks, stores = jobs.tasks(
            job_arrays, job_added, job_outs, swaps, swaps_out, held, job_staged, job_taken, job_sem
        )
    for load in loads:
        load.wait()
    first = depth * chunks
    for i, (s, h) in enumerate(steps):
        if s >= depth and h < parts:
            core_copy(s - depth, h).wait_send()
        multiply(s, h)
        if 0 < i <= first:
            fold(*steps[i - 1])
        if i > first + 1:
            fold(*steps[i - 2])
        if i >= first:
            for _ in range(-(-len(tasks) // (len(steps) - i + 1))):
                tasks.pop(0)()
    for step in steps[-2:]:
        fold(*step)
        for _ in range(-(-len(tasks) // 2)):
            tasks.pop(0)()
    for task in tasks:
        task()
    for store in stores[-2:]:
        store.wait()
    for s, h in steps:
        if s >= depth or h == parts:
            core_copy(s, h).wait_send()
    for k in range(depth):
        for h in range(chunks):
            side_copy(k, h).wait_send()
    for k in range(depth - 1):
        zz = order(k)
        for h in range(chunks):
            line_copy(0, zz, h, me).wait_send()
    if has_stat:
        stat_held[me] = stat[...]
        for step in range(1, n):
            stat_copy(step).wait_send()
            source = lax.rem(me + step, n)
            remote(stat, stat_held.at[source], stat_send.at[step], stat_recv.at[source], me).wait_recv()
        stats[...] = stat_held[...]
    taken = {a for job in jobs.jobs for tile in job.add or () for a in tile if isinstance(a, int)}
    for i, swap in enumerate(swaps):
        swap.wait_send()
        if i not in taken:
            swap.wait_recv()


def scatter_cols(products, stat, parts, collective_id, swaps=(), extra=None, jobs=()):
    n, n_row = lax.axis_size("col"), lax.axis_size("row")
    depth = n // 4
    chunks = parts + (extra is not None)
    kinds = tuple(kind for kind, _, _ in products)
    operands = [x for _, a, b in products for x in (a, b)]
    rows = operands[0].shape[kinds[0] == "tn"]
    in_vmem = pl.BlockSpec(memory_space=pltpu.VMEM)
    out_shape = [jax.ShapeDtypeStruct((rows, LANES), F32)]
    dma = pltpu.SemaphoreType.DMA
    scratch = [dma((len(operands),))]
    scratch += [pltpu.VMEM(a.shape, a.dtype) for a in operands]
    factors = len(operands)
    scratch += [
        pltpu.VMEM((2 * depth, rows, LANES), BF16),
        pltpu.VMEM((depth, rows, LANES), BF16),
        pltpu.VMEM((2 * depth, rows, LANES), BF16),
        pltpu.VMEM((depth, rows, LANES), BF16),
        pltpu.VMEM((depth, rows, LANES), BF16),
        pltpu.VMEM((depth, rows, LANES), BF16),
        pltpu.VMEM((depth + 1, rows, LANES), BF16),
        dma((2 * depth, chunks)),
        dma((2 * depth, chunks)),
        dma((depth, chunks)),
        dma((depth, chunks)),
        dma((depth, chunks)),
        dma((2, depth, chunks)),
    ]
    if extra is not None:
        operands.append(extra)
        block = (extra.shape[0] // n, extra.shape[1])
        out_shape.append(jax.ShapeDtypeStruct(block, F32))
    if stat is not None:
        operands.append(stat)
        out_shape.append(jax.ShapeDtypeStruct((n,) + stat.shape, F32))
        scratch += [pltpu.VMEM((n,) + stat.shape, F32), dma((n,)), dma((n,))]
    anywhere = pl.BlockSpec(memory_space=pl.ANY)
    held = [anywhere] * factors + [in_vmem] * (len(operands) - factors)
    kept = [in_vmem] * len(out_shape)
    if extra is not None:
        scratch += [
            pltpu.VMEM((2 * depth,) + block, BF16),
            pltpu.VMEM((depth,) + block, BF16),
            pltpu.VMEM((depth,) + block, BF16),
            pltpu.VMEM((depth,) + block, BF16),
            pltpu.VMEM((depth + 1,) + block, BF16),
        ]
    if swaps:
        operands += [swap.array for swap in swaps]
        held += [anywhere] * len(swaps)
        kept += [anywhere] * len(swaps)
        out_shape += [swap.shape for swap in swaps]
    scratch += [dma((max(1, len(swaps)),)), dma((max(1, len(swaps)),))]
    jobs = Jobs(list(jobs))
    if jobs.jobs:
        operands += jobs.arrays + jobs.added
        held += [anywhere] * (len(jobs.arrays) + len(jobs.added))
        kept += [anywhere] * len(jobs.jobs)
        out_shape += [job.shape for job in jobs.jobs]
        scratch += [pltpu.VMEM(a.shape, a.dtype) for a in jobs.shapes]
        scratch += [
            pltpu.VMEM((2,) + jobs.stage, jobs.dtype),
            pltpu.VMEM(jobs.stage if jobs.dtype == F32 else (16, LANES), BF16),
            dma((jobs.count,)),
        ]
    shifts = tuple((swap.t, swap.index) for swap in swaps)
    return pl.pallas_call(
        functools.partial(scatter_kernel, depth, n_row, parts, kinds, stat is not None, extra is not None, shifts, jobs),
        out_shape=out_shape,
        in_specs=held,
        out_specs=kept,
        scratch_shapes=scratch,
        compiler_params=pltpu.CompilerParams(
            collective_id=collective_id, has_side_effects=True, vmem_limit_bytes=63 << 20
        ),
        name="scatter_cols",
    )(*operands)


class Piece:
    def __init__(self, source, spot, prepare=None, side_first=False):
        self.source, self.spot, self.prepare, self.side_first = source, spot, prepare, side_first


def gather_steps(row, z, y, c, depth, pieces, send_sem, recv_sem):
    me = col_of(z, y, c)
    up, down = col_of(z + 1, y, c), col_of(z - 1, y, c)
    side, core = col_of(z, 1 - y, c), col_of(z, y, 1 - c)

    def copy(way, block, p, target, own=False):
        piece = pieces[p]
        return pltpu.make_async_remote_copy(
            src_ref=piece.source if own else piece.spot(block),
            dst_ref=piece.spot(block),
            send_sem=send_sem.at[p, way * 2 * depth + block // 2],
            recv_sem=recv_sem.at[p, block],
            device_id=(row, target),
            device_id_type=MESH,
        )

    def start(way, block, p, target, own=False):
        copy(way, block, p, target, own).start()

    def finish(way, block, p, target, own=False):
        copy(way, block, p, target, own).wait_send()

    def arrive(block, p):
        copy(CORE, block, p, me).wait_recv()

    def own(p, act):
        act(SIDE, me, p, side, True)

        @pl.when(z + 1 < depth)
        def _():
            act(UP, me, p, up, True)

        @pl.when(z > 0)
        def _():
            act(DOWN, me, p, down, True)

        act(CORE, me, p, core, True)

    def onward(at, yy, p, act, along, across):
        block = col_of(at, yy, c)
        if act is start:
            arrive(block, p)
        if along:

            @pl.when((at <= z) & (z + 1 < depth))
            def _():
                act(UP, block, p, up)

            @pl.when((at >= z) & (z > 0))
            def _():
                act(DOWN, block, p, down)

        if across:
            act(SIDE, block, p, side)
        act(CORE, block, p, core)

    def line(d, p, act):
        if d == 0:
            own(p, act)
            return
        for at in (z - d, z + d):

            @pl.when((at >= 0) & (at < depth))
            def _():
                onward(at, y, p, act, True, not pieces[p].side_first)

    def sides(d, p, act):
        for at in (z - d, z + d) if d else (z,):

            @pl.when((at >= 0) & (at < depth))
            def _():
                onward(at, 1 - y, p, act, pieces[p].side_first, False)

    def begin(p):
        if pieces[p].prepare is not None:
            pieces[p].prepare()
        line(0, p, start)

    count = len(pieces)
    begin(0)
    for wave in range(count + depth + 1):
        done = []
        for p in range(count):
            k = wave - p
            if k == -1:
                begin(p)
            if 1 <= k < depth:
                line(k, p, start)
                sides(k - 1, p, start)
            if k == depth:
                sides(depth - 1, p, start)
            if k == depth + 1:
                for zz in range(depth):
                    for yy in range(2):
                        arrive(col_of(zz, yy, 1 - c), p)
                done.append(p)
        yield done
    for p in range(count):
        for d in range(depth):
            line(d, p, finish)
            sides(d, p, finish)


def row_pieces(source, rows, spot):
    count = rows // PIECE
    return [
        Piece(
            source.at[span_of(i, PIECE)],
            functools.partial(spot, span_of(i, PIECE)),
            side_first=i % 4 == 2,
        )
        for i in range(count)
    ]


def span_of(i, size):
    return pl.ds(i * size, size)


COSTS = {
    "project": 1.2, "project_latent": 1.6, "project_keys": 0.8, "project_queries": 0.7, "attend": 2.0, "norm": 0.5,
    "route": 0.8, "pick": 1.2, "forward": 1.6, "shared": 1.4, "weigh": 0.7, "expand": 1.5,
}


def work_through(steps, ready, tasks=(), budget=8.0):
    tasks = list(tasks)
    for done in steps:
        for p in done:
            tasks += ready(p)
        spent = 0.0
        while tasks and spent < budget:
            task = tasks.pop(0)
            spent += COSTS.get(getattr(getattr(task, "func", task), "__name__", ""), 0.3)
            task()
    for task in tasks:
        task()


def rotary_tables():
    frequency = 10000.0 ** (-np.arange(ROPE // 2, dtype=np.float32) * 2.0 / ROPE)
    angles = np.arange(LEN, dtype=np.float32)[:, None] * frequency[None, :].astype(np.float32)
    cosines, sines = np.cos(angles), np.sin(angles)
    return (
        jnp.asarray(np.concatenate([cosines] * 4, 1)),
        jnp.asarray(np.concatenate([-sines, sines, sines, -sines], 1)),
    )


def with_exchanged(array):
    half = ROPE // 2
    return jnp.concatenate([array, array[-half:], array[-ROPE:-half]], 0)


def turn(tile, cosines, sines):
    return tile * cosines + pltpu.roll(tile, ROPE, 1) * sines


def spread(columns, like):
    return jnp.broadcast_to(columns, like.shape)


SCALE = (NOPE + ROPE) ** (-0.5)
QK = NOPE + ROPE


def masked_scores(q, k, seg_col, seg_row, base, first, length):
    scores = dot_nt(q[pl.ds(base + first, TILE), :QK], k[pl.ds(base, length), :QK]) * SCALE
    here = first + lax.broadcasted_iota(jnp.int32, (TILE, length), 0)
    there = lax.broadcasted_iota(jnp.int32, (TILE, length), 1)
    allowed = (here >= there) & (
        seg_col[pl.ds(base + first, TILE), :1] == seg_row[:1, pl.ds(base, length)]
    )
    if WINDOW < LEN:
        allowed = allowed & (here - there < WINDOW)
    return jnp.where(allowed, scores, -1e30)


def forward_kernel(depth, n_row, sizes, shifts, *refs):
    (tokens, gain, query_own, down_own, up_own), loads_in = refs[:5], refs[5:11]
    swaps_in, refs = refs[11 : 11 + len(shifts)], refs[11 + len(shifts) :]
    outs, swaps_out, refs = refs[:13], refs[13 : 13 + len(shifts)], refs[13 + len(shifts) :]
    (full, gains, held, query_full, down_mine, down_full, up_full) = refs[:7]
    (q, k, v, latent, low, first_root, latent_root, mixed, lse) = refs[7:16]
    loads_to, refs = refs[16:22], refs[22:]
    (choose, latent_gain, cosines, sines, seg_col, seg_row) = loads_to
    (send_sem, recv_sem, swap_send, swap_recv, local_sem, out_sem, weight_sem, late_send, late_recv, load_sem) = refs
    results = (held, q, k, v, latent, low, first_root, latent_root, mixed, lse)
    rows, width, seqs = sizes
    row, z, y, c = place()
    me, n = col_of(z, y, c), 4 * depth
    greet_neighbours(row, z, y, c, depth, n_row)
    share = width // n_row
    up_rows = up_own.shape[0]
    down_rows = down_own.shape[0]

    def part(s):
        return pl.ds(s * share, share)

    swaps = []
    for i, (source, spot) in enumerate(
        [
            (down_own, lambda slot: down_mine.at[:, part(slot)]),
            (query_own, lambda slot: query_full.at[:, part(slot)]),
        ]
    ):
        swaps.append(
            [
                swap_copy(row, me, n_row, source, spot(n_row - t), t, swap_send.at[i, t], swap_recv.at[i, t])
                for t in range(1, n_row)
            ]
        )
    own_up = pl.ds(pl.multiple_of(row * up_rows, up_rows), up_rows)
    swaps.append(
        [
            swap_copy(row, me, n_row, up_own, up_full.at[own_up], t, swap_send.at[2, t], swap_recv.at[2, t])
            for t in range(1, n_row)
        ]
    )
    for group in swaps:
        for swap in group:
            swap.start()
    late = swap_start(row, me, n_row, shifts, swaps_in, swaps_out, late_send, late_recv)

    def lanes(block):
        return pl.ds(pl.multiple_of(rolled(block, row, n_row, n) * LANES, LANES), LANES)

    locals_ = [
        pltpu.make_async_copy(down_own, down_mine.at[:, part(0)], local_sem.at[0]),
        pltpu.make_async_copy(query_own, query_full.at[:, part(0)], local_sem.at[1]),
        pltpu.make_async_copy(up_own, up_full.at[own_up], local_sem.at[2]),
        pltpu.make_async_copy(gain, gains.at[:, lanes(me)], local_sem.at[3]),
        pltpu.make_async_copy(tokens, full.at[:, lanes(me)], local_sem.at[4]),
    ]
    for copy in locals_:
        copy.start()
    keep_down = pltpu.make_async_copy(
        down_mine, down_full.at[pl.ds(pl.multiple_of(me * down_rows, 16), down_rows)], local_sem.at[5]
    )

    def down_ready():
        locals_[0].wait()
        for swap in swaps[0]:
            swap.wait_recv()
        keep_down.start()

    pieces = [Piece(gain, lambda block: gains.at[:, lanes(block)])]
    pieces += row_pieces(tokens, rows, lambda span, block: full.at[span, lanes(block)])
    down_piece = 2
    pieces.insert(
        down_piece,
        Piece(
            down_mine,
            lambda block: down_full.at[pl.ds(pl.multiple_of(block * down_rows, 16), down_rows)],
            down_ready,
        ),
    )
    token_pieces = [p for p in range(1, len(pieces)) if p != down_piece]

    def keep(array, seq):
        span = pl.ds(seq * LEN, LEN)
        return pltpu.make_async_copy(results[array].at[span], outs[array].at[span], out_sem.at[array, seq])

    def keep_some(arrays, seq):
        for array in arrays:
            keep(array, seq).start()

    weights_out = [
        pltpu.make_async_copy(source, target, weight_sem.at[i])
        for i, (source, target) in enumerate(zip((query_full, down_full, up_full), outs[10:]))
    ]

    def project(i):
        span = pl.ds(i * TILE, TILE)
        x = full[span, :].astype(F32)
        root = lax.rsqrt(jnp.sum(x * x, 1, keepdims=True) / width + EPSILON)
        first_root[span, :] = jnp.broadcast_to(root, (TILE, LANES))
        held[span, :] = (x * root * gains[:1, :]).astype(BF16)

    def project_queries(i):
        span = span_of(i, TILE)
        at = pl.ds((i * TILE) % LEN, TILE)
        pre = dot_nt(held[span, :], query_full[...])
        q[span, :NOPE] = pre[:, :NOPE].astype(BF16)
        q[span, NOPE:] = turn(pre[:, NOPE:], cosines[at, :], sines[at, :]).astype(BF16)

    def project_latent(i):
        span = span_of(i, TILE)
        wide = dot_nt(held[span, :], down_full[...]).astype(BF16)
        low[span, :] = dot_nn(wide, choose[...]).astype(BF16)

    def project_keys(i):
        span = span_of(i, TILE)
        at = pl.ds((i * TILE) % LEN, TILE)
        compressed = low[span, :LATENT].astype(F32)
        root = lax.rsqrt(jnp.mean(compressed * compressed, 1, keepdims=True) + EPSILON)
        latent_root[span, :] = jnp.broadcast_to(root, (TILE, LANES))
        lat = (compressed * root * latent_gain[:1, :]).astype(BF16)
        latent[span, :] = lat
        expanded = dot_nn(lat, up_full[...]).astype(BF16)
        k[span, :NOPE] = expanded[:, :NOPE]
        tile = low[span, LATENT:].astype(F32)
        k[span, NOPE:] = turn(tile, cosines[at, :], sines[at, :]).astype(BF16)
        v[span, :] = expanded[:, NOPE:]

    def attend(seq, block):
        base, first = seq * LEN, block * TILE
        length = first + TILE
        scores = masked_scores(q, k, seg_col, seg_row, base, first, length)
        top = jnp.max(scores, -1, keepdims=True)
        weights = jnp.exp(scores - top)
        total = jnp.sum(weights, -1, keepdims=True)
        probs = (weights / total).astype(BF16)
        span = pl.ds(base + first, TILE)
        mixed[span, :] = dot_nn(probs, v[pl.ds(base, length), :]).astype(BF16)
        lse[span, :] = jnp.broadcast_to(top + jnp.log(total), (TILE, LANES))

    state = {"weights": False}
    per_seq = LEN // TILE
    waiting = []

    def weights_here():
        keep_down.wait()
        for copy in locals_[1:3]:
            copy.wait()
        for group in swaps[1:]:
            for swap in group:
                swap.wait_recv()
        for copy in weights_out:
            copy.start()

    local = copier(load_sem)
    loads = [local(a, b) for a, b in zip(loads_in, loads_to)]

    def ready(p):
        tasks = []
        if p == 0:
            tasks.append(lambda: [copy.wait() for copy in locals_[3:] + loads])
        if p == down_piece:
            tasks.append(weights_here)
            state["weights"] = True
        if p in token_pieces:
            for i in (2 * token_pieces.index(p), 2 * token_pieces.index(p) + 1):
                tasks.append(functools.partial(project, i))
                waiting.append(i)
        if state["weights"]:
            for i in waiting:
                seq, b = divmod(i, per_seq)
                tasks += [
                    functools.partial(project_latent, i),
                    functools.partial(project_keys, i),
                    functools.partial(project_queries, i),
                    functools.partial(attend, seq, b),
                ]
                if b == per_seq - 1:
                    tasks.append(functools.partial(keep_some, range(10), seq))
            waiting.clear()
        return tasks

    first_tasks = [lambda: [copy.start() for copy in loads]]
    work_through(gather_steps(row, z, y, c, depth, pieces, send_sem, recv_sem), ready, first_tasks)
    for group in swaps:
        for swap in group:
            swap.wait_send()
    for copy in weights_out:
        copy.wait()
    for seq in range(seqs):
        for array in range(10):
            keep(array, seq).wait()
    for swap in late:
        swap.wait()


def attention_forward(
    tokens, gain, query_own, down_own, up_own, choose, latent_gain, tables, seg_col, seg_row, collective_id, swaps=()
):
    n, n_row = lax.axis_size("col"), lax.axis_size("row")
    depth, rows = n // 4, tokens.shape[0]
    width, seqs = n * tokens.shape[1], rows // LEN
    padded = n * down_own.shape[0]
    in_vmem = pl.BlockSpec(memory_space=pltpu.VMEM)
    anywhere = pl.BlockSpec(memory_space=pl.ANY)
    count = 2 + rows // PIECE
    dma = pltpu.SemaphoreType.DMA
    shape = jax.ShapeDtypeStruct
    kept = [
        shape((rows, 2 * LANES), BF16),
        shape((rows, 2 * LANES), BF16),
        shape((rows, VD), BF16),
        shape((rows, LATENT), BF16),
        shape((rows, LATENT + LANES), BF16),
        shape((rows, LANES), F32),
        shape((rows, LANES), F32),
        shape((rows, VD), BF16),
        shape((rows, LANES), F32),
    ]
    loads = [choose, latent_gain, *tables, seg_col, seg_row]
    swapped = [swap.array for swap in swaps]
    return pl.pallas_call(
        functools.partial(
            forward_kernel, depth, n_row, (rows, width, seqs), tuple((swap.t, swap.index) for swap in swaps)
        ),
        out_shape=[shape((rows, width), BF16)]
        + kept
        + [
            shape((2 * LANES, width), BF16),
            shape((padded, width), BF16),
            shape((LATENT, 2 * LANES), BF16),
        ]
        + [swap.shape for swap in swaps],
        in_specs=[anywhere] * (11 + len(swapped)),
        out_specs=[anywhere] * (13 + len(swapped)),
        scratch_shapes=[
            pltpu.VMEM((rows, width), BF16),
            pltpu.VMEM((gain.shape[0], width), F32),
            pltpu.VMEM((rows, width), BF16),
            pltpu.VMEM((2 * LANES, width), BF16),
            pltpu.VMEM((down_own.shape[0], width), BF16),
            pltpu.VMEM((padded, width), BF16),
            pltpu.VMEM((LATENT, 2 * LANES), BF16),
        ]
        + [pltpu.VMEM(a.shape, a.dtype) for a in [*kept, *loads]]
        + [
            dma((count, 8 * depth)),
            dma((count, n)),
            dma((3, n_row)),
            dma((3, n_row)),
            dma((6,)),
            dma((10, seqs)),
            dma((3,)),
            dma((max(1, len(swapped)),)),
            dma((max(1, len(swapped)),)),
            dma((len(loads),)),
        ],
        compiler_params=pltpu.CompilerParams(
            collective_id=collective_id, has_side_effects=True, vmem_limit_bytes=60 << 20
        ),
        name="attention_forward",
    )(tokens, gain, query_own, down_own, up_own, *loads, *swapped)


def sigmoid_parts(values):
    sigmoid = jax.nn.sigmoid(values)
    return values * sigmoid, sigmoid * (1.0 + values * (1.0 - sigmoid))


def three_terms(column, width, first):
    high = column.astype(BF16).astype(F32)
    middle = (column - high).astype(BF16).astype(F32)
    lane = lax.broadcasted_iota(jnp.int32, (column.shape[0], width), 1)
    out = jnp.where(lane == first, high, 0.0)
    out = jnp.where(lane == first + 1, middle, out)
    return jnp.where(lane == first + 2, column - high - middle, out)


def copier(sem):
    count = itertools.count()
    return lambda source, target: pltpu.make_async_copy(source, target, sem.at[next(count)])


def hidden_kernel(depth, n_row, sizes, shifts, *refs):
    rows, width, capacity, narrow, experts = sizes
    block, squares, slot_row = refs[:3]
    parts, refs = refs[3 : 3 + 3 * n_row], refs[3 + 3 * n_row :]
    swaps_in, refs = refs[: len(shifts)], refs[len(shifts) :]
    outs, swaps_out, refs = refs[:11], refs[11 : 11 + len(shifts)], refs[11 + len(shifts) :]
    held, refs = refs[:11], refs[11:]
    (full, full_squares, gate_terms, send_sem, recv_sem, local_sem, swap_send, swap_recv) = refs
    (normed, picked, gate_in, up_in, act, logits, root, slot_gate, gate_weight, up_weight, router) = held
    row, z, y, c = place()
    me, n = col_of(z, y, c), 4 * depth
    greet_neighbours(row, z, y, c, depth, n_row)
    swaps = swap_start(row, me, n_row, shifts, swaps_in, swaps_out, swap_send, swap_recv)
    local = copier(local_sem)

    def lanes(block):
        return pl.ds(pl.multiple_of(rolled(block, row, n_row, n) * LANES, LANES), LANES)

    own = [
        local(block, full.at[:, lanes(me)]),
        local(squares, full_squares.at[:, lanes(me)]),
    ]
    share = width // n_row
    for i, target in enumerate((gate_weight, up_weight, router)):
        own += [local(parts[i * n_row + p], target.at[:, span_of(p, share)]) for p in range(n_row)]
    for copy in own:
        copy.start()
    pieces = [Piece(squares, lambda block: full_squares.at[:, lanes(block)])]
    pieces += row_pieces(block, rows, lambda span, block: full.at[span, lanes(block)])
    results = {}

    def store(name, index=slice(None)):
        copy = local(held[name].at[index], outs[name].at[index])
        results[len(results)] = copy
        copy.start()

    def roots():
        for copy in own:
            copy.wait()
        total = sum(full_squares[:, j * LANES : (j + 1) * LANES] for j in range(n))
        columns = jnp.transpose(lax.rsqrt(total / width + EPSILON))
        for i in range(rows // LANES):
            root[span_of(i, LANES), :] = jnp.broadcast_to(columns[:, i : i + 1], (LANES, LANES))
        for name in (6, 8, 9, 10):
            store(name)

    def norm(i):
        span = span_of(i, TILE)
        normed[span, :] = (full[span, :].astype(F32) * root[span, :1]).astype(BF16)

    def project(i):
        span = span_of(i, TILE)
        gate = dot_nt(normed[span, :], gate_weight[...])
        up = dot_nt(normed[span, :], up_weight[...])
        gate_in[span, :] = gate.astype(BF16)
        up_in[span, :] = up.astype(BF16)
        act[span, :] = (gate * jax.nn.sigmoid(gate) * up).astype(BF16)

    def route(i):
        span = span_of(i, TILE)
        scores = dot_nt(normed[span, :], router[...])
        logits[span, :] = scores
        weights = jnp.exp(scores - jnp.max(scores, -1, keepdims=True))
        mine = lax.broadcasted_iota(jnp.int32, scores.shape, 1) == me
        own_gate = jnp.sum(jnp.where(mine, weights, 0.0), -1, keepdims=True) / jnp.sum(
            weights, -1, keepdims=True
        )
        gate_terms[span, :] = three_terms(own_gate, LANES, 0).astype(BF16)

    def pick(q, t):
        tokens, span = span_of(q, 2 * TILE), span_of(t, TILE)
        here = lax.broadcasted_iota(jnp.int32, (TILE, 2 * TILE), 0) + t * TILE
        chosen = jnp.where(here == slot_row[:1, tokens], 1.0, 0.0).astype(BF16)
        term = dot_nn(chosen, normed[tokens, :])
        gates = dot_nn(chosen, gate_terms[tokens, :])
        if q == 0:
            picked[span, :] = term.astype(BF16)
            slot_gate[span, :] = gates
        else:
            picked[span, :] = (picked[span, :].astype(F32) + term).astype(BF16)
            slot_gate[span, :] += gates

    def finish():
        total = jnp.sum(slot_gate[...], 1, keepdims=True)
        slot_gate[...] = jnp.broadcast_to(total, slot_gate.shape)
        for name in (1, 2, 3, 4, 5, 7):
            store(name)

    def ready(p):
        if p == 0:
            return [roots]
        q = p - 1
        tasks = [functools.partial(norm, i) for i in (2 * q, 2 * q + 1)]
        tasks += [functools.partial(route, i) for i in (2 * q, 2 * q + 1)]
        tasks += [functools.partial(pick, q, t) for t in range(capacity // TILE)]
        tasks += [functools.partial(project, i) for i in (2 * q, 2 * q + 1)]
        tasks.append(functools.partial(store, 0, span_of(q, PIECE)))
        if p == len(pieces) - 1:
            tasks.append(finish)
        return tasks

    work_through(gather_steps(row, z, y, c, depth, pieces, send_sem, recv_sem), ready)
    for copy in results.values():
        copy.wait()
    for swap in swaps:
        swap.wait()


def hidden_rows(block, squares, slot_row, parts, capacity, collective_id, swaps=()):
    n, n_row = lax.axis_size("col"), lax.axis_size("row")
    depth, rows = n // 4, block.shape[0]
    width, narrow, experts = n * block.shape[1], parts[0].shape[0], parts[-1].shape[0]
    anywhere = pl.BlockSpec(memory_space=pl.ANY)
    dma, shape = pltpu.SemaphoreType.DMA, jax.ShapeDtypeStruct
    swapped = [swap.array for swap in swaps]
    count = 1 + rows // PIECE
    kept = [
        shape((rows, width), BF16),
        shape((capacity, width), BF16),
        shape((rows, narrow), BF16),
        shape((rows, narrow), BF16),
        shape((rows, narrow), BF16),
        shape((rows, experts), F32),
        shape((rows, LANES), F32),
        shape((capacity, LANES), F32),
        shape((narrow, width), BF16),
        shape((narrow, width), BF16),
        shape((experts, width), BF16),
    ]
    return pl.pallas_call(
        functools.partial(
            hidden_kernel,
            depth,
            n_row,
            (rows, width, capacity, narrow, experts),
            tuple((swap.t, swap.index) for swap in swaps),
        ),
        out_shape=kept + [swap.shape for swap in swaps],
        in_specs=[anywhere] * 2
        + [pl.BlockSpec(memory_space=pltpu.VMEM)]
        + [anywhere] * (len(parts) + len(swapped)),
        out_specs=[anywhere] * (len(kept) + len(swapped)),
        scratch_shapes=[pltpu.VMEM(a.shape, a.dtype) for a in kept]
        + [
            pltpu.VMEM((rows, width), BF16),
            pltpu.VMEM((squares.shape[0], width), F32),
            pltpu.VMEM((rows, LANES), BF16),
            dma((count, 8 * depth)),
            dma((count, n)),
            dma((2 + 3 * n_row + 10 + rows // TILE,)),
            dma((max(1, len(swapped)),)),
            dma((max(1, len(swapped)),)),
        ],
        compiler_params=pltpu.CompilerParams(
            collective_id=collective_id, has_side_effects=True, vmem_limit_bytes=60 << 20
        ),
        name="hidden_rows",
    )(block, squares, slot_row, *parts, *swapped)


def mixture_kernel(depth, n_row, sizes, falls, *refs):
    rows, width, capacity, hidden_units, narrow, experts = sizes
    block, picked_in, slot_row, slot_col, logits_in, slot_gate_in, gate_in, up_in = refs[:8]
    refs = refs[8:]
    each = 2 * n_row - 1
    gate_parts, up_parts, refs = refs[:each], refs[each : 2 * each], refs[2 * each :]
    fall_own, fall_got, refs = refs[0], refs[1:n_row], refs[n_row:]
    shared_parts, refs = refs[:n_row], refs[n_row:]
    outs, refs = refs[:9], refs[9:]
    (fall_out, rows_out, act_out, dgate_out, dup_out, grad_out, sgate_out, sup_out, coef_out) = outs
    (stat_out, full_out, shared_out, probs_out), refs = refs[:4], refs[4:]
    sent_out, refs = refs[: n_row - 1], refs[n_row - 1 :]
    (full, gate_weight, up_weight, fall_weight, picked, gate, up, act, grads, shared_weight) = refs[:10]
    (shared_gate, shared_up, logits, slot_cols, slot_gates, values, inner, coefs, stats, shares), refs = refs[10:20], refs[20:]
    (staged, send_sem, recv_sem, local_sem, swap_send, swap_recv) = refs
    row, z, y, c = place()
    me, n = col_of(z, y, c), 4 * depth
    greet_neighbours(row, z, y, c, depth, n_row)
    share = width // n_row
    first = falls
    swaps = [
        swap_copy(
            row, me, n_row, fall_own.at[0, pl.ds(first, hidden_units - first)],
            fall_weight.at[pl.ds(first, hidden_units - first), span_of(n_row - t, share)],
            t, swap_send.at[t], swap_recv.at[t],
        )
        for t in range(1, n_row)
    ]
    for swap in swaps:
        swap.start()
    local = copier(local_sem)

    def lanes(block):
        return pl.ds(pl.multiple_of(rolled(block, row, n_row, n) * LANES, LANES), LANES)

    loads = [local(picked_in, picked)]
    for weight, pieces in ((gate_weight, gate_parts), (up_weight, up_parts)):
        loads.append(local(pieces[0].at[0], weight.at[span_of(0, share)]))
        at = share
        for piece in pieces[1:]:
            loads.append(local(piece, weight.at[pl.ds(at, piece.shape[0])]))
            at += piece.shape[0]
    later = [
        local(block, full.at[:, lanes(me)]),
        local(slot_gate_in, slot_gates),
        local(logits_in, logits),
        local(slot_col, slot_cols),
        local(gate_in, shared_gate),
        local(up_in, shared_up),
        local(fall_own.at[0], fall_weight.at[:, span_of(0, share)]),
    ]
    for p in range(n_row):
        later.append(local(shared_parts[p], shared_weight.at[:, span_of(p, share)]))
        if p:
            later.append(local(fall_got[p - 1], fall_weight.at[pl.ds(0, first), span_of(p, share)]))
    later[0].start()
    pieces = row_pieces(block, rows, lambda span, block: full.at[span, lanes(block)])
    chunk = 4 * LANES
    chunks = [(at, min(chunk, hidden_units - at)) for at in range(0, hidden_units, chunk)]
    results = []

    def store(source, target):
        copy = local(source, target)
        copy.start()
        results.append(copy)

    def begin():
        for copy in loads:
            copy.wait()

    def begin_more():
        for copy in later:
            copy.wait()
        store(shared_weight, shared_out)

    def fetch(copies):
        for copy in copies:
            copy.start()

    def forward(t, at, size):
        span, cols = span_of(t, TILE), pl.ds(at, size)
        g = dot_nn(picked[span, :], gate_weight[:, cols])
        u = dot_nn(picked[span, :], up_weight[:, cols])
        gate[span, cols] = g.astype(BF16)
        up[span, cols] = u.astype(BF16)
        act[span, cols] = (g * jax.nn.sigmoid(g) * u).astype(BF16)
        if at + size == hidden_units:
            store(act.at[span], act_out.at[span])

    def shared(i):
        span = span_of(i, TILE)
        raw = dot_nt(full[span, :], shared_weight[...])
        g, u = shared_gate[span, :].astype(F32), shared_up[span, :].astype(F32)
        silu, slope = sigmoid_parts(g)
        dg, du = (raw * u * slope).astype(BF16), (raw * silu).astype(BF16)
        inner[span, :] = jnp.broadcast_to(
            jnp.sum(g * dg.astype(F32) + u * du.astype(F32), 1, keepdims=True), (TILE, LANES)
        )
        shared_gate[span, :] = dg
        shared_up[span, :] = du

    def pick(q, t):
        tokens, span = span_of(q, 2 * TILE), span_of(t, TILE)
        here = lax.broadcasted_iota(jnp.int32, (TILE, 2 * TILE), 0) + t * TILE
        chosen = jnp.where(here == slot_row[:1, tokens], 1.0, 0.0).astype(BF16)
        term = dot_nn(chosen, full[tokens, :])
        if q == 0:
            grads[span, :] = term.astype(BF16)
        else:
            grads[span, :] = (grads[span, :].astype(F32) + term).astype(BF16)

    def fall_here():
        for swap in swaps:
            swap.wait()
        store(fall_weight, fall_out)

    staging = []

    def stage(value, target):
        slot = len(staging) % 2
        if len(staging) > 1:
            staging[-2].wait()
        spot = staged.at[slot, pl.ds(0, value.shape[0]), pl.ds(0, value.shape[1])]
        spot[...] = value
        copy = local(spot, target)
        copy.start()
        staging.append(copy)

    def weigh_rows(t):
        span = span_of(t, TILE)
        picked[span, :] = (grads[span, :].astype(F32) * slot_gates[span, :1]).astype(BF16)

    def weigh(p, at, size):
        value = dot_tn(act[:, pl.ds(at, size)], picked[:, span_of(p, share)])
        stage(value.astype(BF16), sent_out[p - 1].at[pl.ds(at, size)])

    def backward(t):
        span = span_of(t, TILE)
        scale = slot_gates[span, :1]
        raw_left = grads[span, :]
        gate_dot = jnp.zeros((TILE, 1), F32)
        slot_dot = jnp.zeros((TILE, 1), F32)
        for at, size in chunks:
            cols = pl.ds(at, size)
            raw = dot_nt(raw_left, fall_weight[cols, :])
            g, u = gate[span, cols].astype(F32), up[span, cols].astype(F32)
            gate_dot += jnp.sum(act[span, cols].astype(F32) * raw, 1, keepdims=True)
            silu, slope = sigmoid_parts(g)
            scaled = raw * scale
            dg, du = (scaled * u * slope).astype(BF16), (scaled * silu).astype(BF16)
            slot_dot += jnp.sum(g * dg.astype(F32) + u * du.astype(F32), 1, keepdims=True)
            gate[span, cols] = dg
            up[span, cols] = du
        store(picked.at[span], grad_out.at[span])
        values[span, :] = (
            three_terms(gate_dot, LANES, 0) + three_terms(slot_dot, LANES, 3)
        ).astype(BF16)
        store(gate.at[span], dgate_out.at[span])
        store(up.at[span], dup_out.at[span])

    def to_rows(t):
        span = span_of(t, TILE)
        back = dot_nt(gate[span, :], gate_weight[...]) + dot_nt(up[span, :], up_weight[...])
        stage(back.astype(BF16), rows_out.at[span])

    def settle(i):
        span = span_of(i, TILE)
        here = lax.broadcasted_iota(jnp.int32, (TILE, capacity), 1)
        chosen = jnp.where(here == slot_cols[span, :1], 1.0, 0.0).astype(BF16)
        terms = dot_nn(chosen, values[...])
        lane = lax.broadcasted_iota(jnp.int32, terms.shape, 1)
        token_dot = jnp.sum(jnp.where(lane < 3, terms, 0.0), 1, keepdims=True)
        slot_dot = jnp.sum(jnp.where(lane >= 3, terms, 0.0), 1, keepdims=True)
        scores = logits[span, :]
        weights = jnp.exp(scores - jnp.max(scores, -1, keepdims=True))
        probs = weights / jnp.sum(weights, -1, keepdims=True)
        mine = jnp.where(lax.broadcasted_iota(jnp.int32, scores.shape, 1) == me, 1.0, 0.0)
        part = jnp.sum(probs * mine, -1, keepdims=True) * token_dot
        coef = (part * (mine - probs)).astype(BF16)
        coefs[span, :] = coef
        shares[span, :] = probs
        total = (
            inner[span, :1] + slot_dot + jnp.sum(coef.astype(F32) * scores, -1, keepdims=True)
        )
        stats[span, :] = jnp.where(lane == 0, total, jnp.where(lane == 1, part, 0.0))

    slots = range(capacity // TILE)

    def ready(p):
        tasks = [begin_more] if p == 0 else []
        tasks += [functools.partial(pick, p, t) for t in slots]
        tasks += [functools.partial(shared, i) for i in (2 * p, 2 * p + 1)]
        tasks.append(functools.partial(store, full.at[span_of(p, PIECE)], full_out.at[span_of(p, PIECE)]))
        if p == len(pieces) - 1:
            tasks.append(lambda: [store(shared_gate, sgate_out), store(shared_up, sup_out)])
            tasks += [functools.partial(weigh_rows, t) for t in slots]
            for q in range(1, n_row):
                for at in range(0, hidden_units, TILE):
                    tasks.append(functools.partial(weigh, q, at, min(TILE, hidden_units - at)))
            tasks.append(fall_here)
            for t in slots:
                tasks += [functools.partial(backward, t), functools.partial(to_rows, t)]
            tasks += [functools.partial(settle, i) for i in range(rows // TILE)]
        return tasks

    first_tasks = [
        functools.partial(fetch, loads[: len(loads) // 2 + 1]),
        functools.partial(fetch, loads[len(loads) // 2 + 1 :]),
        functools.partial(fetch, later[1:]),
        begin,
    ] + [
        functools.partial(forward, t, at, size) for t in slots for at, size in chunks
    ]
    work_through(gather_steps(row, z, y, c, depth, pieces, send_sem, recv_sem), ready, first_tasks)
    store(coefs, coef_out)
    store(stats, stat_out)
    store(shares, probs_out)
    for copy in results + staging[-2:]:
        copy.wait()


def mixture(
    block, picked, slot_row, slot_col, logits, slot_gate, gate_in, up_in,
    gate_pieces, up_pieces, fall, fall_got, shared_parts, collective_id,
):
    n, n_row = lax.axis_size("col"), lax.axis_size("row")
    depth, rows = n // 4, block.shape[0]
    width = n * block.shape[1]
    capacity, hidden_units = picked.shape[0], fall.shape[1]
    narrow, experts = gate_in.shape[1], logits.shape[1]
    anywhere = pl.BlockSpec(memory_space=pl.ANY)
    dma, shape = pltpu.SemaphoreType.DMA, jax.ShapeDtypeStruct
    count = rows // PIECE
    first = fall_got[0].shape[0] if fall_got else 0
    operands = [block, picked, slot_row, slot_col, logits, slot_gate, gate_in, up_in]
    operands += [*gate_pieces, *up_pieces, fall, *fall_got, *shared_parts]
    out_shape = [
        shape((hidden_units, width), BF16),
        shape((capacity, width), BF16),
        shape((capacity, hidden_units), BF16),
        shape((capacity, hidden_units), BF16),
        shape((capacity, hidden_units), BF16),
        shape((capacity, width), BF16),
        shape((rows, narrow), BF16),
        shape((rows, narrow), BF16),
        shape((rows, experts), BF16),
        shape((rows, LANES), F32),
        shape((rows, width), BF16),
        shape((narrow, width), BF16),
        shape((rows, experts), F32),
    ] + [shape((hidden_units, width // n_row), BF16)] * (n_row - 1)
    return pl.pallas_call(
        functools.partial(
            mixture_kernel, depth, n_row, (rows, width, capacity, hidden_units, narrow, experts), first
        ),
        out_shape=out_shape,
        in_specs=[anywhere] * 2
        + [pl.BlockSpec(memory_space=pltpu.VMEM)]
        + [anywhere] * (len(operands) - 3),
        out_specs=[anywhere] * len(out_shape),
        scratch_shapes=[
            pltpu.VMEM((rows, width), BF16),
            pltpu.VMEM((width, hidden_units), BF16),
            pltpu.VMEM((width, hidden_units), BF16),
            pltpu.VMEM((hidden_units, width), BF16),
            pltpu.VMEM((capacity, width), BF16),
            pltpu.VMEM((capacity, hidden_units), BF16),
            pltpu.VMEM((capacity, hidden_units), BF16),
            pltpu.VMEM((capacity, hidden_units), BF16),
            pltpu.VMEM((capacity, width), BF16),
            pltpu.VMEM((narrow, width), BF16),
            pltpu.VMEM((rows, narrow), BF16),
            pltpu.VMEM((rows, narrow), BF16),
            pltpu.VMEM((rows, experts), F32),
            pltpu.VMEM((rows, LANES), jnp.int32),
            pltpu.VMEM((capacity, LANES), F32),
            pltpu.VMEM((capacity, LANES), BF16),
            pltpu.VMEM((rows, LANES), F32),
            pltpu.VMEM((rows, experts), BF16),
            pltpu.VMEM((rows, LANES), F32),
            pltpu.VMEM((rows, experts), F32),
            pltpu.VMEM((2, TILE, width), BF16),
            dma((count, 8 * depth)),
            dma((count, n)),
            dma((96,)),
            dma((n_row,)),
            dma((n_row,)),
        ],
        compiler_params=pltpu.CompilerParams(
            collective_id=collective_id, has_side_effects=True, vmem_limit_bytes=63 << 20
        ),
        name="mixture",
    )(*operands)


def backward_kernel(depth, n_row, sizes, shifts, *refs):
    grad, loads, refs = refs[0], refs[1:18], refs[18:]
    swaps_in, refs = refs[: len(shifts)], refs[len(shifts) :]
    (gain_back, *rounded), outs, refs = refs[:4], refs[4:8], refs[8:]
    swaps_out, refs = refs[: len(shifts)], refs[len(shifts) :]
    held, refs = refs[:17], refs[17:]
    (out_full, q, k, v, latent, low, latent_root, mixed, lse, up_full, choose, latent_gain) = held[:12]
    (cosines, sines, seg_col, seg_row, normed) = held[12:]
    (query_back, low_long, low_wide, inner), refs = refs[:4], refs[4:]
    results = (query_back, low_long, low_wide, inner)
    (full, keys_back, values_back, mixed_back), refs = refs[:4], refs[4:]
    (out_back, query_weight_back, up_weight_back), refs = refs[:3], refs[3:]
    (send_sem, recv_sem, local_sem, load_sem, out_sem, swap_send, swap_recv) = refs
    rows, width, seqs = sizes
    row, z, y, c = place()
    me, n = col_of(z, y, c), 4 * depth
    greet_neighbours(row, z, y, c, depth, n_row if shifts else 1)
    def lanes(block):
        return pl.ds(pl.multiple_of(rolled(block, row, n_row, n) * LANES, LANES), LANES)

    keep = pltpu.make_async_copy(grad, full.at[:, lanes(me)], local_sem)
    keep.start()
    fetches = [
        pltpu.make_async_copy(a, b, load_sem.at[i]) for i, (a, b) in enumerate(zip(loads, held))
    ]

    def result(array, seq):
        span = pl.ds(seq * LEN, LEN)
        span = (slice(None), span) if array == 2 else (span,)
        return pltpu.make_async_copy(results[array].at[span], outs[array].at[span], out_sem.at[array, seq])

    def store(seq):
        for array in range(4):
            result(array, seq).start()

    pieces = row_pieces(grad, rows, lambda span, block: full.at[span, lanes(block)])
    per_seq = LEN // TILE
    lower = lax.broadcasted_iota(jnp.int32, (TILE, LANES), 1) < ROPE

    def begin():
        keep.wait()
        for fetch in fetches:
            fetch.wait()
        for total in (gain_back, out_back, query_weight_back, up_weight_back):
            total[...] = jnp.zeros_like(total)

    def project(i):
        span = span_of(i, TILE)
        out_back[...] += dot_tn(mixed[span, :], full[span, :])
        mixed_back[...] = dot_nt(full[span, :], out_full[...]).astype(BF16)

    def attend(seq, block):
        base, first = seq * LEN, block * TILE
        length = first + TILE
        span, keys = pl.ds(base + first, TILE), pl.ds(base, length)
        at = pl.ds(first, TILE)
        grad_mixed = mixed_back[...]
        scores = masked_scores(q, k, seg_col, seg_row, base, first, length)
        probs = jnp.exp(scores - lse[span, :1])
        grad_probs = dot_nt(grad_mixed, v[keys, :])
        grad_scores = (
            probs * (grad_probs - jnp.sum(probs * grad_probs, -1, keepdims=True))
        ).astype(BF16)
        back = dot_nn(grad_scores, k[keys, :]) * SCALE
        nope, tile = back[:, :NOPE], back[:, NOPE:]
        inner[span, :] = jnp.broadcast_to(
            jnp.sum(nope * q[span, :NOPE].astype(F32), 1, keepdims=True)
            + 0.5 * jnp.sum(tile * q[span, NOPE:].astype(F32), 1, keepdims=True),
            (TILE, LANES),
        )
        query_back[span, :NOPE] = nope.astype(BF16)
        turned = turn(tile, cosines[at, :], -sines[at, :])
        query_back[span, NOPE:] = jnp.where(lower, turned, 0.0).astype(BF16)
        keys_term = dot_tn(grad_scores, q[span, :])
        values_term = dot_tn(probs.astype(BF16), grad_mixed)
        keys_back[first:length, :] = keys_term[first:, :]
        values_back[first:length, :] = values_term[first:, :]
        if first:
            keys_back[:first, :] += keys_term[:first, :]
            values_back[:first, :] += values_term[:first, :]

    def weigh(i):
        span = span_of(i, TILE)
        query_weight_back[...] += dot_tn(query_back[span, :], normed[span, :])

    def expand(seq, block):
        first = block * TILE
        span, at = pl.ds(seq * LEN + first, TILE), pl.ds(first, TILE)
        back = keys_back[at, :] * SCALE
        expanded = jnp.concatenate([back[:, :NOPE], values_back[at, :]], 1).astype(BF16)
        up_weight_back[...] += dot_tn(expanded, latent[span, :])
        latent_grad = dot_nt(expanded, up_full[...])
        compressed = low[span, :LATENT].astype(F32)
        root = latent_root[span, :1]
        dots = jnp.sum(latent_grad * latent[span, :].astype(F32), 1, keepdims=True)
        gain_back[...] += jnp.broadcast_to(
            jnp.sum(latent_grad * compressed * root, 0, keepdims=True), gain_back.shape
        )
        compressed_grad = root * latent_grad * latent_gain[:1, :] - compressed * (
            root * root * dots / LATENT
        )
        turned = turn(back[:, NOPE:], cosines[at, :], -sines[at, :])
        low_grad = jnp.concatenate([compressed_grad, jnp.where(lower, turned, 0.0)], 1).astype(BF16)
        low_wide[:, span] = dot_nt(choose[...], low_grad).astype(BF16)
        low_long[span, :] = dot_nt(low_grad, choose[...]).astype(BF16)
        inner[span, :] += jnp.broadcast_to(
            jnp.sum(low_grad.astype(F32) * low[span, :].astype(F32), 1, keepdims=True),
            (TILE, LANES),
        )

    def ready(p):
        tasks = [begin] if p == 0 else []
        for i in (2 * p, 2 * p + 1):
            seq, block = divmod(i, per_seq)
            tasks += [functools.partial(project, i), functools.partial(attend, seq, block)]
            tasks.append(functools.partial(weigh, i))
            if block == per_seq - 1:
                tasks += [functools.partial(expand, seq, b) for b in range(per_seq)]
                tasks.append(functools.partial(store, seq))
        return tasks

    swaps = swap_start(row, me, n_row, shifts, swaps_in, swaps_out, swap_send, swap_recv)
    first_tasks = [
        lambda: [fetch.start() for fetch in fetches[:8]],
        lambda: [fetch.start() for fetch in fetches[8:]],
    ]
    work_through(gather_steps(row, z, y, c, depth, pieces, send_sem, recv_sem), ready, first_tasks)
    for total, target in zip((out_back, query_weight_back, up_weight_back), rounded):
        target[...] = total[...].astype(BF16)
    for seq in range(seqs):
        for array in range(4):
            result(array, seq).wait()
    for swap in swaps:
        swap.wait()


def attention_backward(grad, operands, collective_id, swaps=()):
    n, n_row = lax.axis_size("col"), lax.axis_size("row")
    depth, rows = n // 4, grad.shape[0]
    width, seqs = n * grad.shape[1], rows // LEN
    in_vmem = pl.BlockSpec(memory_space=pltpu.VMEM)
    anywhere = pl.BlockSpec(memory_space=pl.ANY)
    count = rows // PIECE
    dma = pltpu.SemaphoreType.DMA
    shape = jax.ShapeDtypeStruct
    swapped = [swap.array for swap in swaps]
    kept = [
        shape((rows, 2 * LANES), BF16),
        shape((rows, operands[10].shape[0]), BF16),
        shape((operands[10].shape[0], rows), BF16),
        shape((rows, LANES), F32),
    ]
    return pl.pallas_call(
        functools.partial(
            backward_kernel, depth, n_row, (rows, width, seqs), tuple((swap.t, swap.index) for swap in swaps)
        ),
        out_shape=[
            shape((8, LATENT), F32),
            shape((VD, width), BF16),
            shape((2 * LANES, width), BF16),
            shape((2 * LANES, LATENT), BF16),
        ]
        + kept
        + [swap.shape for swap in swaps],
        in_specs=[anywhere] * (18 + len(swapped)),
        out_specs=[in_vmem] * 4 + [anywhere] * (4 + len(swapped)),
        scratch_shapes=[pltpu.VMEM(a.shape, a.dtype) for a in [*operands, *kept]]
        + [
            pltpu.VMEM((rows, width), BF16),
            pltpu.VMEM((LEN, 2 * LANES), F32),
            pltpu.VMEM((LEN, VD), F32),
            pltpu.VMEM((TILE, VD), BF16),
            pltpu.VMEM((VD, width), F32),
            pltpu.VMEM((2 * LANES, width), F32),
            pltpu.VMEM((2 * LANES, LATENT), F32),
            dma((count, 8 * depth)),
            dma((count, n)),
            dma,
            dma((17,)),
            dma((4, seqs)),
            dma((max(1, len(swapped)),)),
            dma((max(1, len(swapped)),)),
        ],
        compiler_params=pltpu.CompilerParams(
            collective_id=collective_id, has_side_effects=True, vmem_limit_bytes=60 << 20
        ),
        name="attention_backward",
    )(grad, *operands, *swapped)


def row_shift(array, step):
    n = lax.axis_size("row")
    return lax.ppermute(array, "row", [(i, (i - step) % n) for i in range(n)])


def to_others(*arrays):
    pairs = [array if isinstance(array, tuple) else (array, ()) for array in arrays]
    return [Swap(array, t, index) for array, index in pairs for t in range(1, lax.axis_size("row"))]


def from_others(got, index):
    others = lax.axis_size("row") - 1
    return got[index * others : (index + 1) * others][::-1]


def row_parts(array):
    return [array] + [row_shift(array, s) for s in range(1, lax.axis_size("row"))]


def row_sum(parts):
    return row_add(parts[0], [part.astype(BF16) for part in parts[1:]])


def row_add(total, parts):
    n = lax.axis_size("row")
    return row_sum_of(total, [row_shift(part, n - s) for s, part in enumerate(parts, 1)])


def row_sum_of(total, received):
    for part in received:
        total = total + part.astype(F32)
    return total


def unroll_parts(parts, axis):
    n = len(parts)
    size = parts[0].shape[axis]
    doubled = jnp.concatenate(parts + parts[:-1], axis)
    start = lax.rem(n - lax.axis_index("row"), n) * size
    return lax.dynamic_slice_in_dim(doubled, start, n * size, axis)


def own_parts(array, axis):
    n = lax.axis_size("row")
    size = array.shape[axis] // n
    row = lax.axis_index("row")
    return [
        lax.dynamic_slice_in_dim(array, lax.rem(row + s, n) * size, size, axis) for s in range(n)
    ]


def interleave(first, second):
    return [array for pair in zip(first, second) for array in pair]


def cut(array, axis):
    return jnp.split(array, lax.axis_size("row"), axis)


def as_stat(*vectors):
    return jnp.concatenate([v.reshape(-1, LANES) for v in vectors], 0)


def per_device(
    tokens,
    cotangent,
    segments,
    routes,
    first_gain,
    query_proj,
    latent_down,
    latent_gain,
    latent_up,
    output_proj,
    second_gain,
    router_weight,
    expert_gate,
    expert_up,
    expert_down,
    shared_gate,
    shared_up,
    shared_down,
):
    row_count, share = tokens.shape
    n = lax.axis_size("col")
    width = share * n
    column = lax.axis_index("col")
    seqs = segments.shape[0]
    narrow = latent_down.shape[1]
    padding = -narrow % 16
    tables = rotary_tables()
    seg_flat = segments.reshape(-1)
    seg_col = jnp.broadcast_to(seg_flat[:, None], (row_count, LANES))
    seg_row = jnp.broadcast_to(seg_flat[None, :], (8, row_count))
    column_of = np.arange(n * narrow)
    turned_of = np.concatenate([column_of, column_of[LATENT + 32 :], column_of[LATENT : LATENT + 32]])
    wide_of = turned_of // narrow * (narrow + padding) + turned_of % narrow
    choose = jnp.asarray((np.arange(n * (narrow + padding))[:, None] == wide_of[None, :]).astype(BF16))

    experts = router_weight.shape[1]
    capacity = row_count * routes.shape[1] * 4 // (3 * experts)
    member = jnp.any(routes == column, 1)
    slot_number = jnp.where(member, jnp.cumsum(member.astype(jnp.int32)) - 1, -1)
    slot_row = jnp.broadcast_to(slot_number[None, :], (8, row_count))
    slot_col = jnp.broadcast_to(slot_number[:, None], (row_count, LANES))
    part = expert_gate.shape[1]
    gate_cut, up_cut, fall_first = part * 11 // 16, part // 2, 2 * LANES
    gate_low, gate_high = (0, (0, gate_cut)), (0, (gate_cut, part - gate_cut))
    up_low, up_high = (0, (0, up_cut)), (0, (up_cut, part - up_cut))
    pick_back = (slot_number[:, None] == jnp.arange(capacity)[None, :]).astype(BF16)

    latent_gains = jnp.broadcast_to(latent_gain[None, :], (8, LATENT))
    (
        normed,
        queries,
        keys,
        values,
        latent,
        low,
        first_root,
        latent_root,
        mixed,
        log_total,
        query_full,
        down_full,
        up_full,
        *got,
    ) = attention_forward(
        tokens,
        jnp.broadcast_to(first_gain[None, :], (8, share)),
        with_exchanged(query_proj.T),
        jnp.pad(latent_down.T, ((0, padding), (0, 0))),
        latent_up,
        choose,
        latent_gains,
        tables,
        seg_col,
        seg_row,
        1,
        to_others(
            output_proj, shared_gate.T, shared_up.T, router_weight.T, (expert_gate, gate_low)
        ),
    )
    out_full = jnp.concatenate([output_proj] + from_others(got, 0), 1)
    shared_gate_parts = [shared_gate.T] + from_others(got, 1)
    shared_up_parts = [shared_up.T] + from_others(got, 2)
    router_parts = [router_weight.T] + from_others(got, 3)
    gate_first = from_others(got, 4)
    first_root = first_root[:, :1]
    branch, *got = scatter_cols(
        [("nn", mixed, out_full)], None, 2, 2, to_others((expert_gate, gate_high), (expert_up, up_low))
    )
    gate_pieces = [expert_gate] + interleave(gate_first, from_others(got, 0))
    up_first = from_others(got, 1)
    hidden = tokens.astype(F32) + branch
    (
        normed_two,
        picked,
        shared_in,
        shared_lift,
        shared_act,
        logits,
        second_root,
        slot_gate,
        shared_gate_full,
        shared_up_full,
        router_full,
        *got,
    ) = hidden_rows(
        (hidden * second_gain).astype(BF16),
        as_stat(jnp.sum(hidden * hidden, 1)),
        slot_row,
        shared_gate_parts + shared_up_parts + router_parts,
        capacity,
        3,
        to_others((expert_up, up_high), shared_down, (expert_down, (0, (0, fall_first)))),
    )
    second_root = second_root[:, :1]
    up_pieces = [expert_up] + interleave(up_first, from_others(got, 0))
    (
        fall_full,
        picked_back,
        activation,
        grad_gate_in,
        grad_up_in,
        slot_grad,
        shared_gin,
        shared_gup,
        coefficient,
        stat,
        grad_full,
        shared_down_full,
        probs,
        *fall_sent,
    ) = mixture(
        cotangent,
        picked,
        slot_row,
        slot_col,
        logits,
        slot_gate,
        shared_in,
        shared_lift,
        gate_pieces,
        up_pieces,
        expert_down,
        from_others(got, 2),
        [shared_down] + from_others(got, 1),
        4,
    )
    n_row = lax.axis_size("row")
    units = activation.shape[1]
    other = range(1, n_row)

    def part_of(array, p):
        return (array, ((0, array.shape[0]), (p * part, part)))

    part_tiles = [(at, min(TILE, part - at), 0, units) for at in range(0, part, TILE)]
    fall_tiles = [(at, min(3 * LANES, units - at), 0, part) for at in range(0, units, 3 * LANES)]

    def sent_rows(arrays, tiles, some):
        return [
            Swap(array, t, ((tiles[i][0], tiles[i][1]),))
            for i in some
            for t, array in enumerate(arrays, 1)
        ]

    fall_split = max(1, len(fall_tiles) * 3 // 4)
    fall_now, fall_late = range(fall_split), range(fall_split, len(fall_tiles))
    part_split = max(1, len(part_tiles) * 3 // 4)
    part_now, part_late = range(part_split), range(part_split, len(part_tiles))
    rows_all = (0, row_count)
    expert_tiles = [(at, TILE, 0, width) for at in range(0, capacity, TILE)]

    grad_normed_two, stats, *got = scatter_cols(
        [
            ("nn", pick_back, picked_back),
            ("nn", shared_gin, shared_gate_full),
            ("nn", shared_gup, shared_up_full),
            ("nn", coefficient, router_full),
        ],
        as_stat(stat[:, 0], stat[:, 1]),
        2,
        5,
        sent_rows(fall_sent, fall_tiles, fall_now),
        jobs=[Job("tn", part_of(picked, p), (grad_gate_in, ()), part_tiles, BF16) for p in other]
        + [Job("tn", part_of(picked, p), (grad_up_in, ()), part_tiles, BF16) for p in other]
        + [Job("nn", (activation, ()), (fall_full, ()), expert_tiles, BF16, scale=(slot_gate, ()))],
    )
    fall_got, got = got[: len(fall_now) * len(other)], got[len(fall_now) * len(other) :]
    gate_sent, up_sent, (expert_out,) = got[: len(other)], got[len(other) : 2 * len(other)], got[-1:]

    stats = stats.reshape(n, 2, row_count)
    inner_total = jnp.sum(stats[:, 0], 0)[:, None]
    shares = stats[:, 1]
    logit_grad = (shares - probs.T * jnp.sum(shares, 0, keepdims=True)).astype(BF16)
    router_tiles = [(0, experts, at, 4 * LANES) for at in range(0, width, 4 * LANES)]
    wide_tiles = [(0, shared_act.shape[1], at, 4 * LANES) for at in range(0, width, 4 * LANES)]
    branch, *got = scatter_cols(
        [("nn", pick_back, expert_out), ("nn", shared_act, shared_down_full)],
        None,
        2,
        7,
        sent_rows(fall_sent, fall_tiles, fall_late) + sent_rows(gate_sent, part_tiles, part_now),
        jobs=[
            Job("tn", (shared_gin, ()), (normed_two, ()), wide_tiles, BF16),
            Job("tn", (shared_gup, ()), (normed_two, ()), wide_tiles, BF16),
            Job("tn", (shared_act, ()), (grad_full, ()), wide_tiles, BF16),
            Job("nn", (logit_grad, ()), (normed_two, ()), router_tiles, BF16),
        ],
    )
    fall_got += got[: len(fall_late) * len(other)]
    gate_got = got[len(fall_late) * len(other) : -4]
    shared_grads = got[-4:]
    output = (hidden + branch).astype(BF16)
    grad_stream = cotangent.astype(F32)
    grad_hidden = (
        grad_stream
        + second_root * (grad_normed_two * second_gain)
        - hidden * (second_root * second_root * inner_total / width)
    )
    second_gain_grad = jnp.sum(grad_normed_two * hidden * second_root, 0)
    up_now = range(len(part_tiles) // 2)

    def others_of(array):
        return [Swap(array, t, ((0, array.shape[0]), (t * part, part))) for t in other]

    (
        latent_gain_grad,
        output_grad,
        query_grad,
        up_grad,
        query_back,
        low_long,
        low_wide,
        inner,
        *got,
    ) = attention_backward(
        grad_hidden.astype(BF16),
        (
            out_full,
            queries,
            keys,
            values,
            latent,
            low,
            latent_root,
            mixed,
            log_total,
            up_full,
            choose,
            latent_gains,
            *tables,
            seg_col,
            seg_row,
            normed,
        ),
        6,
        sent_rows(gate_sent, part_tiles, part_late)
        + sent_rows(up_sent, part_tiles, up_now)
        + others_of(shared_grads[0]),
    )
    gate_count, up_count = len(part_late) * len(other), len(up_now) * len(other)
    gate_got += got[:gate_count]
    up_got = got[gate_count : gate_count + up_count]
    shared_got = [got[gate_count + up_count :]]

    up_grads = own_parts(up_grad, 1)
    query_grad = query_grad[:QK]
    swaps = sent_rows(up_sent, part_tiles, range(len(up_now), len(part_tiles)))
    in_flight = len(swaps)

    def by_tile(got, count):
        return [list(got[i * len(other) : (i + 1) * len(other)]) for i in range(count)]

    grad_normed, low_own, stats, *got = scatter_cols(
        [("nn", query_back, query_full), ("nn", low_long, down_full)],
        as_stat(inner[:, 0], latent_gain_grad[0], jnp.zeros((-LATENT % 1024,), F32)),
        2,
        8,
        swaps
        + [swap for array in [*shared_grads[1:], query_grad, output_grad] for swap in others_of(array)]
        + [Swap(array, t) for t, array in enumerate(up_grads[1:], 1)],
        low_wide,
        jobs=[
            Job(
                "tn", (activation, ()), part_of(slot_grad, 0), fall_tiles, F32,
                add=by_tile(fall_got, len(fall_tiles)),
            ),
            Job(
                "tn", part_of(picked, 0), (grad_gate_in, ()), part_tiles, F32,
                add=by_tile(gate_got, len(part_tiles)),
            ),
            Job(
                "tn", part_of(picked, 0), (grad_up_in, ()), part_tiles, F32,
                add=by_tile(up_got + list(range(in_flight)), len(part_tiles)),
            ),
        ],
    )
    fall_grad, gate_grad, up_proj_grad = got[-3:]
    got = [shared_got[0]] + by_tile(got[in_flight:-3], 6)
    stats = jnp.sum(stats, 0).reshape(-1)
    inner_total = stats[:row_count, None]
    latent_gain_sum = stats[row_count : row_count + LATENT]
    stream = tokens.astype(F32)
    grad_input = (
        grad_hidden
        + first_root * (grad_normed * first_gain)
        - stream * (first_root * first_root * inner_total / width)
    )
    first_gain_grad = jnp.sum(grad_normed * stream * first_root, 0)
    firsts = [array[:, :part] for array in [*shared_grads, query_grad, output_grad]] + [up_grads[0]]
    totals = [row_sum_of(a.astype(F32), b) for a, b in zip(firsts, got)]
    gains = jnp.concatenate([first_gain_grad, second_gain_grad, latent_gain_sum])
    gains = gains + sum(row_shift(gains, t) for t in other)
    gain_grads = jnp.split(gains, [share, 2 * share])
    return (
        output,
        grad_input.astype(BF16),
        gain_grads[0],
        totals[4].T,
        row_sum(cut(dot_nn(low_own.astype(BF16), normed)[:narrow].T, 0)),
        gain_grads[2],
        totals[6].T,
        totals[5],
        gain_grads[1],
        totals[3].T,
        gate_grad[None],
        up_proj_grad[None],
        fall_grad[None],
        totals[0].T,
        totals[1].T,
        totals[2],
    )


def solution(mesh):
    return jax.shard_map(
        per_device,
        mesh=mesh,
        in_specs=(
            P("row", "col"),
            P("row", "col"),
            P("row", None),
            P("row", None),
            P("col"),
            P("row", "col"),
            P("row", "col"),
            P(),
            P("row", "col"),
            P("col", "row"),
            P("col"),
            P("row", None),
            P("col", "row", None),
            P("col", "row", None),
            P("col", None, "row"),
            P("row", "col"),
            P("row", "col"),
            P("col", "row"),
        ),
        out_specs=(
            P("row", "col"),
            P("row", "col"),
            P("col"),
            P("row", "col"),
            P("row", "col"),
            P(),
            P("row", "col"),
            P("col", "row"),
            P("col"),
            P("row", None),
            P("col", "row", None),
            P("col", "row", None),
            P("col", None, "row"),
            P("row", "col"),
            P("row", "col"),
            P("col", "row"),
        ),
        check_vma=False,
    )
```

```python
import functools
import itertools

import jax
import jax.numpy as jnp
import numpy as np
from jax import lax
from jax.experimental import pallas as pl
from jax.experimental.pallas import tpu as pltpu
from jax.sharding import PartitionSpec as P

NOPE = 128
ROPE = 64
VD = 128
LATENT = 512
LEN = 1024
WINDOW = 1024
EPSILON = 1e-06
LANES = 128
MESH = pl.DeviceIdType.MESH
BF16 = jnp.bfloat16
F32 = jnp.float32
UP, DOWN, SIDE, CORE = range(4)
TILE = 256
PIECE = 2 * TILE


def dot_nn(a, b):
    return jnp.dot(a, b, preferred_element_type=F32)


def dot_nt(a, b):
    return lax.dot_general(a, b, (((1,), (1,)), ((), ())), preferred_element_type=F32)


def dot_tn(a, b):
    return lax.dot_general(a, b, (((0,), (0,)), ((), ())), preferred_element_type=F32)


def place():
    me = lax.axis_index("col")
    return lax.axis_index("row"), me // 4, (me // 2) % 2, me % 2


def col_of(z, y, c):
    return z * 4 + y * 2 + c


def rolled(index, row, n_row, count):
    return lax.rem(index + count - row * (count // n_row), count)


def signal(row, target):
    pl.semaphore_signal(
        pltpu.get_barrier_semaphore(), inc=1, device_id=(row, target), device_id_type=MESH
    )


def greet_row(row, me, n_row):
    for t in range(1, n_row):
        signal(lax.rem(row + t, n_row), me)
    pl.semaphore_wait(pltpu.get_barrier_semaphore(), n_row - 1)


def greet_neighbours(row, z, y, c, depth, n_row=1):
    for t in range(1, n_row):
        signal(lax.rem(row + t, n_row), col_of(z, y, c))
    signal(row, col_of(z, 1 - y, c))
    signal(row, col_of(z, y, 1 - c))

    @pl.when(z > 0)
    def _():
        signal(row, col_of(z - 1, y, c))

    @pl.when(z < depth - 1)
    def _():
        signal(row, col_of(z + 1, y, c))

    count = 1 + n_row + (z > 0).astype(jnp.int32) + (z < depth - 1).astype(jnp.int32)
    pl.semaphore_wait(pltpu.get_barrier_semaphore(), count)


class Swap:
    def __init__(self, array, t, index=()):
        self.array, self.t = array, t
        self.index = tuple(i if isinstance(i, int) else pl.ds(*i) for i in index)
        shape = [i[1] for i in index if not isinstance(i, int)] + list(array.shape[len(index) :])
        self.shape = jax.ShapeDtypeStruct(shape, array.dtype)


def swap_start(row, me, n_row, swaps, sources, targets, send_sem, recv_sem):
    copies = [
        swap_copy(
            row, me, n_row, source.at[index] if index else source, target, t,
            send_sem.at[i], recv_sem.at[i],
        )
        for i, ((t, index), source, target) in enumerate(zip(swaps, sources, targets))
    ]
    for copy in copies:
        copy.start()
    return copies


def swap_copy(row, me, n_row, source, target, t, send_sem, recv_sem):
    return pltpu.make_async_remote_copy(
        src_ref=source, dst_ref=target, send_sem=send_sem, recv_sem=recv_sem,
        device_id=(lax.rem(row + t, n_row), me), device_id_type=MESH,
    )


def greet_all(row, me, n, n_row=1):
    for t in range(1, n_row):
        signal(lax.rem(row + t, n_row), me)

    def hello(step, carry):
        signal(row, lax.rem(me + step, n))
        return carry

    lax.fori_loop(1, n, hello, 0)
    pl.semaphore_wait(pltpu.get_barrier_semaphore(), n + n_row - 2)


class Job:
    def __init__(self, kind, left, right, tiles, dtype, scale=None, add=None):
        self.kind, self.tiles, self.dtype, self.add = kind, tiles, dtype, add
        self.operands = [left, right] + ([scale] if scale is not None else [])
        shapes = [Swap(array, 0, index).shape.shape for array, index in (left, right)]
        self.shape = jax.ShapeDtypeStruct((shapes[0][kind == "tn"], shapes[1][1]), dtype)


class Jobs:
    def __init__(self, jobs):
        self.jobs, self.arrays, self.indices, self.shapes, self.uses = jobs, [], [], [], []
        known = {}
        for job in jobs:
            use = []
            for array, index in job.operands:
                key = (id(array), index)
                if key not in known:
                    known[key] = len(self.arrays)
                    swap = Swap(array, 0, index)
                    self.arrays.append(array)
                    self.indices.append(swap.index)
                    self.shapes.append(swap.shape)
                use.append(known[key])
            self.uses.append(use)
        self.added = [a for job in jobs for tile in job.add or () for a in tile if not isinstance(a, int)]
        self.stage = (
            max([rows for job in jobs for _, rows, _, _ in job.tiles] or [0]),
            max([columns for job in jobs for _, _, _, columns in job.tiles] or [0]),
        )
        self.dtype = jobs[0].dtype if jobs else F32
        self.count = len(self.arrays) + 2 * sum(len(job.tiles) for job in jobs) + len(self.added)
        self.count += sum(isinstance(a, int) for job in jobs for tile in job.add or () for a in tile)

    def tasks(self, arrays, added, outs, swaps, swaps_out, held, staged, taken, sem):
        local = copier(sem)
        loads = [
            local(array.at[index] if index else array, target)
            for array, index, target in zip(arrays, self.indices, held)
        ]
        middle = len(loads) // 2
        tasks = [
            lambda: [load.start() for load in loads[:middle]],
            lambda: [load.start() for load in loads[middle:]],
        ]
        waited, stores = set(), []
        added = list(added)

        def work(job, use, out, tile, extra):
            for i in use:
                if i not in waited:
                    waited.add(i)
                    loads[i].wait()
            row, rows, column, columns = tile
            takes = []
            for i, source in enumerate(extra):
                if isinstance(source, int):
                    swaps[source].wait_recv()
                    source = swaps_out[source]
                takes.append(local(source, taken.at[pl.ds(0, rows), pl.ds(0, columns)]))
            for take in takes[:1]:
                take.start()
            left, right = held[use[0]], held[use[1]]
            if job.kind == "tn":
                value = dot_tn(left[:, pl.ds(row, rows)], right[:, pl.ds(column, columns)])
            else:
                value = dot_nn(left[pl.ds(row, rows), :], right[:, pl.ds(column, columns)])
                if len(use) > 2:
                    value = value * held[use[2]][pl.ds(row, rows), :1]
            slot = len(stores) % 2
            if len(stores) > 1:
                stores[-2].wait()
            spot = staged.at[slot, pl.ds(0, rows), pl.ds(0, columns)]
            for i, take in enumerate(takes):
                if i:
                    take.start()
                take.wait()
                value = value + taken[pl.ds(0, rows), pl.ds(0, columns)].astype(F32)
            spot[...] = value.astype(job.dtype)
            store = local(spot, out.at[pl.ds(row, rows), pl.ds(column, columns)])
            store.start()
            stores.append(store)

        for job, use, out in zip(self.jobs, self.uses, outs):
            for i, tile in enumerate(job.tiles):
                extra = [a if isinstance(a, int) else added.pop(0) for a in (job.add[i] if job.add else ())]
                tasks.append(functools.partial(work, job, use, out, tile, extra))
        return tasks, stores


def scatter_kernel(depth, n_row, parts, kinds, has_stat, has_extra, shifts, jobs, *refs):
    count = 2 * len(kinds) + has_stat + has_extra
    extra = refs[count - 1 - has_stat] if has_extra else None
    operands, stat = refs[: 2 * len(kinds)], refs[count - 1] if has_stat else None
    swaps_in, refs = refs[count : count + len(shifts)], refs[count + len(shifts) :]
    job_arrays, refs = refs[: len(jobs.arrays)], refs[len(jobs.arrays) :]
    job_added, refs = refs[: len(jobs.added)], refs[len(jobs.added) :]
    out = refs[0]
    extra_out = refs[1] if has_extra else None
    refs = refs[has_extra:]
    stats = refs[1] if has_stat else None
    swaps_out = refs[1 + has_stat : 1 + has_stat + len(shifts)]
    refs = refs[1 + has_stat + len(shifts) :]
    job_outs, rest = refs[: len(jobs.jobs)], refs[len(jobs.jobs) :]
    if jobs.jobs:
        held = rest[-len(jobs.arrays) - 3 : -3]
        job_staged, job_taken, job_sem = rest[-3:]
        rest = rest[: -len(jobs.arrays) - 3]
    (load_sem, *loaded), rest = rest[: 1 + len(operands)], rest[1 + len(operands) :]
    local = copier(load_sem)
    loads = [local(a, b) for a, b in zip(operands, loaded)]
    for load in loads:
        load.start()
    operands = loaded
    mine, core_send, core_recv, side_send, side_recv, line_send, line_recv = rest[:7]
    cs, cr, ss, sr, ls, lr = rest[7:13]
    extra_core, extra_side_send, extra_side, extra_line_send, extra_line = rest[-7:-2] if has_extra else [None] * 5
    row, z, y, c = place()
    me, n = col_of(z, y, c), 4 * depth
    pairs = 2 * depth
    rows = out.shape[0]
    size = rows // parts
    tile = min(256, size)
    if has_stat:
        stat_held, stat_send, stat_recv = rest[13:16]
        greet_all(row, me, n, n_row if shifts else 1)

        def stat_copy(step):
            target = lax.rem(me + step, n)
            return pltpu.make_async_remote_copy(
                src_ref=stat,
                dst_ref=stat_held.at[me],
                send_sem=stat_send.at[step],
                recv_sem=stat_recv.at[me],
                device_id=(row, target),
                device_id_type=MESH,
            )

        for step in range(1, n):
            stat_copy(step).start()
    else:
        greet_neighbours(row, z, y, c, depth, n_row if shifts else 1)
    swaps = swap_start(row, me, n_row, shifts, swaps_in, swaps_out, rest[-2], rest[-1])
    up, down = col_of(z + 1, y, c), col_of(z - 1, y, c)
    side, core = col_of(z, 1 - y, c), col_of(z, y, 1 - c)

    def remote(src, dst, send, recv, target):
        return pltpu.make_async_remote_copy(
            src_ref=src, dst_ref=dst, send_sem=send, recv_sem=recv,
            device_id=(row, target), device_id_type=MESH,
        )

    def span(h):
        return pl.ds(h * size, size)

    def block_of(s, cc):
        return col_of(order(s % depth), 1 - y if s < depth else y, cc)

    def extra_rows(s, cc):
        size = extra.shape[0] // n
        return extra.at[pl.ds(pl.multiple_of(block_of(s, cc) * size, 16), size)]

    def mine_at(s, h):
        return mine.at[s, span(h)] if h < parts else extra_rows(s, c)

    def core_recv_at(s, h):
        return core_recv.at[s, span(h)] if h < parts else extra_core.at[s]

    def side_send_at(k, h):
        return side_send.at[k, span(h)] if h < parts else extra_side_send.at[k]

    def side_recv_at(k, h):
        return side_recv.at[k, span(h)] if h < parts else extra_side.at[k]

    def line_send_at(zz, h):
        return line_send.at[zz, span(h)] if h < parts else extra_line_send.at[zz]

    def line_recv_at(way, zz, h):
        slot = zz + 1 - way
        return line_recv.at[slot, span(h)] if h < parts else extra_line.at[slot]

    def out_at(h):
        return out.at[span(h)] if h < parts else extra_out

    def core_copy(s, h):
        source = core_send.at[s % depth, span(h)] if h < parts else extra_rows(s, 1 - c)
        return remote(source, core_recv_at(s, h), cs.at[s, h], cr.at[s, h], core)

    def side_copy(k, h):
        return remote(side_send_at(k, h), side_recv_at(k, h), ss.at[k, h], sr.at[k, h], side)

    def line_copy(way, zz, h, target):
        return remote(
            line_send_at(zz, h), line_recv_at(way, zz, h), ls.at[zz, h], lr.at[way, zz, h], target
        )

    low_half = z < depth // 2

    def order(k):
        if k == depth - 1:
            return z
        from_top = depth - 1 - k
        from_top = from_top - (from_top <= z).astype(jnp.int32)
        from_low = k + (k >= z).astype(jnp.int32)
        return jnp.where(low_half, from_top, from_low)

    def tiles(body):
        def step(i, carry):
            body(i)
            return carry

        lax.fori_loop(0, size // tile, step, 0)

    def multiply(s, h):
        if h == parts:
            core_copy(s, h).start()
            return
        yy = 1 - y if s < depth else y
        pair = rolled(order(s % depth) * 2 + yy, row, n_row, pairs)
        cols = pl.ds(pl.multiple_of(pair * 2 * LANES, 2 * LANES), 2 * LANES)

        def body(i):
            at = pl.ds(pl.multiple_of(h * size + i * tile, tile), tile)
            total = None
            for j, kind in enumerate(kinds):
                left, right = operands[2 * j], operands[2 * j + 1]
                if kind == "nn":
                    term = dot_nn(left[at, :], right[:, cols])
                elif kind == "tn":
                    term = dot_tn(left[:, at], right[:, cols])
                else:
                    term = dot_nt(left[at, :], right[cols, :])
                total = term if total is None else total + term
            first, second = total[:, :LANES], total[:, LANES:]
            mine[s, at, :] = jnp.where(c == 0, first, second).astype(BF16)
            core_send[s % depth, at, :] = jnp.where(c == 0, second, first).astype(BF16)

        tiles(body)
        core_copy(s, h).start()

    def add_up(target, sources):
        step = min(tile, target.shape[0])

        def body(i, carry):
            at = pl.ds(pl.multiple_of(i * step, step), step)
            total = sources[0][at, :].astype(F32)
            for source in sources[1:]:
                total = total + source[at, :].astype(F32)
            target[at, :] = total.astype(target.dtype)
            return carry

        lax.fori_loop(0, target.shape[0] // step, body, 0)

    def fold(s, h):
        core_copy(s, h).wait_recv()
        k = s % depth
        sources = [mine_at(s, h), core_recv_at(s, h)]
        if s < depth:
            add_up(side_send_at(k, h), sources)
            side_copy(k, h).start()
            return
        side_copy(k, h).wait_recv()
        sources.append(side_recv_at(k, h))
        zz = order(k)
        if k < depth - 1:

            @pl.when(zz > z)
            def _():
                @pl.when(z > 0)
                def _():
                    line_copy(0, zz, h, up).wait_recv()
                    add_up(line_send_at(zz, h), sources + [line_recv_at(0, zz, h)])

                @pl.when(z == 0)
                def _():
                    add_up(line_send_at(zz, h), sources)

                line_copy(0, zz, h, up).start()

            @pl.when(zz < z)
            def _():
                @pl.when(z < depth - 1)
                def _():
                    line_copy(1, zz, h, down).wait_recv()
                    add_up(line_send_at(zz, h), sources + [line_recv_at(1, zz, h)])

                @pl.when(z == depth - 1)
                def _():
                    add_up(line_send_at(zz, h), sources)

                line_copy(1, zz, h, down).start()

            return

        @pl.when((z > 0) & (z < depth - 1))
        def _():
            line_copy(0, z, h, me).wait_recv()
            line_copy(1, z, h, me).wait_recv()
            add_up(out_at(h), sources + [line_recv_at(0, z, h), line_recv_at(1, z, h)])

        @pl.when(z == 0)
        def _():
            line_copy(1, z, h, me).wait_recv()
            add_up(out_at(h), sources + [line_recv_at(1, z, h)])

        @pl.when(z == depth - 1)
        def _():
            line_copy(0, z, h, me).wait_recv()
            add_up(out_at(h), sources + [line_recv_at(0, z, h)])

    chunks = parts + has_extra
    steps = [(s, h) for s in range(2 * depth) for h in range(chunks)]
    tasks, stores = [], []
    if jobs.jobs:
        tasks, stores = jobs.tasks(
            job_arrays, job_added, job_outs, swaps, swaps_out, held, job_staged, job_taken, job_sem
        )
    for load in loads:
        load.wait()
    first = depth * chunks
    for i, (s, h) in enumerate(steps):
        if s >= depth and h < parts:
            core_copy(s - depth, h).wait_send()
        multiply(s, h)
        if 0 < i <= first:
            fold(*steps[i - 1])
        if i > first + 1:
            fold(*steps[i - 2])
        if i >= first:
            for _ in range(-(-len(tasks) // (len(steps) - i + 1))):
                tasks.pop(0)()
    for step in steps[-2:]:
        fold(*step)
        for _ in range(-(-len(tasks) // 2)):
            tasks.pop(0)()
    for task in tasks:
        task()
    for store in stores[-2:]:
        store.wait()
    for s, h in steps:
        if s >= depth or h == parts:
            core_copy(s, h).wait_send()
    for k in range(depth):
        for h in range(chunks):
            side_copy(k, h).wait_send()
    for k in range(depth - 1):
        zz = order(k)
        for h in range(chunks):
            line_copy(0, zz, h, me).wait_send()
    if has_stat:
        stat_held[me] = stat[...]
        for step in range(1, n):
            stat_copy(step).wait_send()
            source = lax.rem(me + step, n)
            remote(stat, stat_held.at[source], stat_send.at[step], stat_recv.at[source], me).wait_recv()
        stats[...] = stat_held[...]
    taken = {a for job in jobs.jobs for tile in job.add or () for a in tile if isinstance(a, int)}
    for i, swap in enumerate(swaps):
        swap.wait_send()
        if i not in taken:
            swap.wait_recv()


def scatter_cols(products, stat, parts, collective_id, swaps=(), extra=None, jobs=()):
    n, n_row = lax.axis_size("col"), lax.axis_size("row")
    depth = n // 4
    chunks = parts + (extra is not None)
    kinds = tuple(kind for kind, _, _ in products)
    operands = [x for _, a, b in products for x in (a, b)]
    rows = operands[0].shape[kinds[0] == "tn"]
    in_vmem = pl.BlockSpec(memory_space=pltpu.VMEM)
    out_shape = [jax.ShapeDtypeStruct((rows, LANES), F32)]
    dma = pltpu.SemaphoreType.DMA
    scratch = [dma((len(operands),))]
    scratch += [pltpu.VMEM(a.shape, a.dtype) for a in operands]
    factors = len(operands)
    scratch += [
        pltpu.VMEM((2 * depth, rows, LANES), BF16),
        pltpu.VMEM((depth, rows, LANES), BF16),
        pltpu.VMEM((2 * depth, rows, LANES), BF16),
        pltpu.VMEM((depth, rows, LANES), BF16),
        pltpu.VMEM((depth, rows, LANES), BF16),
        pltpu.VMEM((depth, rows, LANES), BF16),
        pltpu.VMEM((depth + 1, rows, LANES), BF16),
        dma((2 * depth, chunks)),
        dma((2 * depth, chunks)),
        dma((depth, chunks)),
        dma((depth, chunks)),
        dma((depth, chunks)),
        dma((2, depth, chunks)),
    ]
    if extra is not None:
        operands.append(extra)
        block = (extra.shape[0] // n, extra.shape[1])
        out_shape.append(jax.ShapeDtypeStruct(block, F32))
    if stat is not None:
        operands.append(stat)
        out_shape.append(jax.ShapeDtypeStruct((n,) + stat.shape, F32))
        scratch += [pltpu.VMEM((n,) + stat.shape, F32), dma((n,)), dma((n,))]
    anywhere = pl.BlockSpec(memory_space=pl.ANY)
    held = [anywhere] * factors + [in_vmem] * (len(operands) - factors)
    kept = [in_vmem] * len(out_shape)
    if extra is not None:
        scratch += [
            pltpu.VMEM((2 * depth,) + block, BF16),
            pltpu.VMEM((depth,) + block, BF16),
            pltpu.VMEM((depth,) + block, BF16),
            pltpu.VMEM((depth,) + block, BF16),
            pltpu.VMEM((depth + 1,) + block, BF16),
        ]
    if swaps:
        operands += [swap.array for swap in swaps]
        held += [anywhere] * len(swaps)
        kept += [anywhere] * len(swaps)
        out_shape += [swap.shape for swap in swaps]
    scratch += [dma((max(1, len(swaps)),)), dma((max(1, len(swaps)),))]
    jobs = Jobs(list(jobs))
    if jobs.jobs:
        operands += jobs.arrays + jobs.added
        held += [anywhere] * (len(jobs.arrays) + len(jobs.added))
        kept += [anywhere] * len(jobs.jobs)
        out_shape += [job.shape for job in jobs.jobs]
        scratch += [pltpu.VMEM(a.shape, a.dtype) for a in jobs.shapes]
        scratch += [
            pltpu.VMEM((2,) + jobs.stage, jobs.dtype),
            pltpu.VMEM(jobs.stage if jobs.dtype == F32 else (16, LANES), BF16),
            dma((jobs.count,)),
        ]
    shifts = tuple((swap.t, swap.index) for swap in swaps)
    return pl.pallas_call(
        functools.partial(scatter_kernel, depth, n_row, parts, kinds, stat is not None, extra is not None, shifts, jobs),
        out_shape=out_shape,
        in_specs=held,
        out_specs=kept,
        scratch_shapes=scratch,
        compiler_params=pltpu.CompilerParams(
            collective_id=collective_id, has_side_effects=True, vmem_limit_bytes=63 << 20
        ),
        name="scatter_cols",
    )(*operands)


class Piece:
    def __init__(self, source, spot, prepare=None, side_first=False):
        self.source, self.spot, self.prepare, self.side_first = source, spot, prepare, side_first


def gather_steps(row, z, y, c, depth, pieces, send_sem, recv_sem):
    me = col_of(z, y, c)
    up, down = col_of(z + 1, y, c), col_of(z - 1, y, c)
    side, core = col_of(z, 1 - y, c), col_of(z, y, 1 - c)

    def copy(way, block, p, target, own=False):
        piece = pieces[p]
        return pltpu.make_async_remote_copy(
            src_ref=piece.source if own else piece.spot(block),
            dst_ref=piece.spot(block),
            send_sem=send_sem.at[p, way * 2 * depth + block // 2],
            recv_sem=recv_sem.at[p, block],
            device_id=(row, target),
            device_id_type=MESH,
        )

    def start(way, block, p, target, own=False):
        copy(way, block, p, target, own).start()

    def finish(way, block, p, target, own=False):
        copy(way, block, p, target, own).wait_send()

    def arrive(block, p):
        copy(CORE, block, p, me).wait_recv()

    def own(p, act):
        act(SIDE, me, p, side, True)

        @pl.when(z + 1 < depth)
        def _():
            act(UP, me, p, up, True)

        @pl.when(z > 0)
        def _():
            act(DOWN, me, p, down, True)

        act(CORE, me, p, core, True)

    def onward(at, yy, p, act, along, across):
        block = col_of(at, yy, c)
        if act is start:
            arrive(block, p)
        if along:

            @pl.when((at <= z) & (z + 1 < depth))
            def _():
                act(UP, block, p, up)

            @pl.when((at >= z) & (z > 0))
            def _():
                act(DOWN, block, p, down)

        if across:
            act(SIDE, block, p, side)
        act(CORE, block, p, core)

    def line(d, p, act):
        if d == 0:
            own(p, act)
            return
        for at in (z - d, z + d):

            @pl.when((at >= 0) & (at < depth))
            def _():
                onward(at, y, p, act, True, not pieces[p].side_first)

    def sides(d, p, act):
        for at in (z - d, z + d) if d else (z,):

            @pl.when((at >= 0) & (at < depth))
            def _():
                onward(at, 1 - y, p, act, pieces[p].side_first, False)

    def begin(p):
        if pieces[p].prepare is not None:
            pieces[p].prepare()
        line(0, p, start)

    count = len(pieces)
    begin(0)
    for wave in range(count + depth + 1):
        done = []
        for p in range(count):
            k = wave - p
            if k == -1:
                begin(p)
            if 1 <= k < depth:
                line(k, p, start)
                sides(k - 1, p, start)
            if k == depth:
                sides(depth - 1, p, start)
            if k == depth + 1:
                for zz in range(depth):
                    for yy in range(2):
                        arrive(col_of(zz, yy, 1 - c), p)
                done.append(p)
        yield done
    for p in range(count):
        for d in range(depth):
            line(d, p, finish)
            sides(d, p, finish)


def row_pieces(source, rows, spot):
    count = rows // PIECE
    return [
        Piece(
            source.at[span_of(i, PIECE)],
            functools.partial(spot, span_of(i, PIECE)),
            side_first=i % 4 == 2,
        )
        for i in range(count)
    ]


def span_of(i, size):
    return pl.ds(i * size, size)


COSTS = {
    "project": 1.2, "project_latent": 1.6, "project_keys": 0.8, "project_queries": 0.7, "attend": 2.0, "norm": 0.5,
    "route": 0.8, "pick": 1.2, "forward": 1.6, "shared": 1.4, "weigh": 0.7, "expand": 1.5,
}


def work_through(steps, ready, tasks=(), budget=8.0):
    tasks = list(tasks)
    for done in steps:
        for p in done:
            tasks += ready(p)
        spent = 0.0
        while tasks and spent < budget:
            task = tasks.pop(0)
            spent += COSTS.get(getattr(getattr(task, "func", task), "__name__", ""), 0.3)
            task()
    for task in tasks:
        task()


def rotary_tables():
    frequency = 10000.0 ** (-np.arange(ROPE // 2, dtype=np.float32) * 2.0 / ROPE)
    angles = np.arange(LEN, dtype=np.float32)[:, None] * frequency[None, :].astype(np.float32)
    cosines, sines = np.cos(angles), np.sin(angles)
    return (
        jnp.asarray(np.concatenate([cosines] * 4, 1)),
        jnp.asarray(np.concatenate([-sines, sines, sines, -sines], 1)),
    )


def turn(tile, cosines, sines):
    return tile * cosines + pltpu.roll(tile, ROPE, 1) * sines


def spread(columns, like):
    return jnp.broadcast_to(columns, like.shape)


SCALE = (NOPE + ROPE) ** (-0.5)
QK = NOPE + ROPE


def masked_scores(q, k, seg_col, seg_row, base, first, length):
    scores = dot_nt(q[pl.ds(base + first, TILE), :QK], k[pl.ds(base, length), :QK]) * SCALE
    here = first + lax.broadcasted_iota(jnp.int32, (TILE, length), 0)
    there = lax.broadcasted_iota(jnp.int32, (TILE, length), 1)
    allowed = (here >= there) & (
        seg_col[pl.ds(base + first, TILE), :1] == seg_row[:1, pl.ds(base, length)]
    )
    if WINDOW < LEN:
        allowed = allowed & (here - there < WINDOW)
    return jnp.where(allowed, scores, -1e30)


def forward_kernel(depth, n_row, sizes, shifts, *refs):
    (tokens, gain, query_own, down_own, up_own), loads_in = refs[:5], refs[5:11]
    swaps_in, refs = refs[11 : 11 + len(shifts)], refs[11 + len(shifts) :]
    outs, swaps_out, refs = refs[:13], refs[13 : 13 + len(shifts)], refs[13 + len(shifts) :]
    (full, gains, held, query_full, down_mine, down_full, up_full) = refs[:7]
    (q, k, v, latent, low, first_root, latent_root, mixed, lse) = refs[7:16]
    loads_to, refs = refs[16:22], refs[22:]
    (choose, latent_gain, cosines, sines, seg_col, seg_row) = loads_to
    (send_sem, recv_sem, swap_send, swap_recv, local_sem, out_sem, weight_sem, late_send, late_recv, load_sem) = refs
    results = (held, q, k, v, latent, low, first_root, latent_root, mixed, lse)
    rows, width, seqs = sizes
    row, z, y, c = place()
    me, n = col_of(z, y, c), 4 * depth
    greet_neighbours(row, z, y, c, depth, n_row)
    share = width // n_row
    up_rows = up_own.shape[0]
    down_rows = down_own.shape[0]

    def part(s):
        return pl.ds(s * share, share)

    swaps = []
    for i, (source, spot) in enumerate(
        [
            (down_own, lambda slot: down_mine.at[:, part(slot)]),
            (query_own, lambda slot: query_full.at[pl.ds(0, QK), part(slot)]),
        ]
    ):
        swaps.append(
            [
                swap_copy(row, me, n_row, source, spot(n_row - t), t, swap_send.at[i, t], swap_recv.at[i, t])
                for t in range(1, n_row)
            ]
        )
    own_up = pl.ds(pl.multiple_of(row * up_rows, up_rows), up_rows)
    swaps.append(
        [
            swap_copy(row, me, n_row, up_own, up_full.at[own_up], t, swap_send.at[2, t], swap_recv.at[2, t])
            for t in range(1, n_row)
        ]
    )
    for group in swaps:
        for swap in group:
            swap.start()
    late = swap_start(row, me, n_row, shifts, swaps_in, swaps_out, late_send, late_recv)

    def lanes(block):
        return pl.ds(pl.multiple_of(rolled(block, row, n_row, n) * LANES, LANES), LANES)

    locals_ = [
        pltpu.make_async_copy(down_own, down_mine.at[:, part(0)], local_sem.at[0]),
        pltpu.make_async_copy(query_own, query_full.at[pl.ds(0, QK), part(0)], local_sem.at[1]),
        pltpu.make_async_copy(up_own, up_full.at[own_up], local_sem.at[2]),
        pltpu.make_async_copy(gain, gains.at[:, lanes(me)], local_sem.at[3]),
        pltpu.make_async_copy(tokens, full.at[:, lanes(me)], local_sem.at[4]),
    ]
    for copy in locals_:
        copy.start()
    keep_down = pltpu.make_async_copy(
        down_mine, down_full.at[pl.ds(pl.multiple_of(me * down_rows, 16), down_rows)], local_sem.at[5]
    )

    def down_ready():
        locals_[0].wait()
        for swap in swaps[0]:
            swap.wait_recv()
        keep_down.start()

    pieces = [Piece(gain, lambda block: gains.at[:, lanes(block)])]
    pieces += row_pieces(tokens, rows, lambda span, block: full.at[span, lanes(block)])
    down_piece = 2
    pieces.insert(
        down_piece,
        Piece(
            down_mine,
            lambda block: down_full.at[pl.ds(pl.multiple_of(block * down_rows, 16), down_rows)],
            down_ready,
        ),
    )
    token_pieces = [p for p in range(1, len(pieces)) if p != down_piece]

    def keep(array, seq):
        span = pl.ds(seq * LEN, LEN)
        return pltpu.make_async_copy(results[array].at[span], outs[array].at[span], out_sem.at[array, seq])

    def keep_some(arrays, seq):
        for array in arrays:
            keep(array, seq).start()

    weights_out = [
        pltpu.make_async_copy(source, target, weight_sem.at[i])
        for i, (source, target) in enumerate(zip((query_full, down_full, up_full), outs[10:]))
    ]

    def project(i):
        span = pl.ds(i * TILE, TILE)
        x = full[span, :].astype(F32)
        root = lax.rsqrt(jnp.sum(x * x, 1, keepdims=True) / width + EPSILON)
        first_root[span, :] = jnp.broadcast_to(root, (TILE, LANES))
        held[span, :] = (x * root * gains[:1, :]).astype(BF16)

    def project_queries(i):
        span = span_of(i, TILE)
        at = pl.ds((i * TILE) % LEN, TILE)
        pre = dot_nt(held[span, :], query_full[...])
        q[span, :NOPE] = pre[:, :NOPE].astype(BF16)
        q[span, NOPE:] = turn(pre[:, NOPE:], cosines[at, :], sines[at, :]).astype(BF16)

    def project_latent(i):
        span = span_of(i, TILE)
        wide = dot_nt(held[span, :], down_full[...]).astype(BF16)
        low[span, :] = dot_nn(wide, choose[...]).astype(BF16)

    def project_keys(i):
        span = span_of(i, TILE)
        at = pl.ds((i * TILE) % LEN, TILE)
        compressed = low[span, :LATENT].astype(F32)
        root = lax.rsqrt(jnp.mean(compressed * compressed, 1, keepdims=True) + EPSILON)
        latent_root[span, :] = jnp.broadcast_to(root, (TILE, LANES))
        lat = (compressed * root * latent_gain[:1, :]).astype(BF16)
        latent[span, :] = lat
        expanded = dot_nn(lat, up_full[...]).astype(BF16)
        k[span, :NOPE] = expanded[:, :NOPE]
        tile = low[span, LATENT:].astype(F32)
        k[span, NOPE:] = turn(tile, cosines[at, :], sines[at, :]).astype(BF16)
        v[span, :] = expanded[:, NOPE:]

    def attend(seq, block):
        base, first = seq * LEN, block * TILE
        length = first + TILE
        scores = masked_scores(q, k, seg_col, seg_row, base, first, length)
        top = jnp.max(scores, -1, keepdims=True)
        weights = jnp.exp(scores - top)
        total = jnp.sum(weights, -1, keepdims=True)
        probs = (weights / total).astype(BF16)
        span = pl.ds(base + first, TILE)
        mixed[span, :] = dot_nn(probs, v[pl.ds(base, length), :]).astype(BF16)
        lse[span, :] = jnp.broadcast_to(top + jnp.log(total), (TILE, LANES))

    state = {"weights": False}
    per_seq = LEN // TILE
    waiting = []

    def weights_here():
        keep_down.wait()
        for copy in locals_[1:3]:
            copy.wait()
        for group in swaps[1:]:
            for swap in group:
                swap.wait_recv()
        half = ROPE // 2
        query_full[QK : QK + half, :] = query_full[QK - half : QK, :]
        query_full[QK + half :, :] = query_full[QK - ROPE : QK - half, :]
        for copy in weights_out:
            copy.start()

    local = copier(load_sem)
    loads = [local(a, b) for a, b in zip(loads_in, loads_to)]

    def ready(p):
        tasks = []
        if p == 0:
            tasks.append(lambda: [copy.wait() for copy in locals_[3:] + loads])
        if p == down_piece:
            tasks.append(weights_here)
            state["weights"] = True
        if p in token_pieces:
            for i in (2 * token_pieces.index(p), 2 * token_pieces.index(p) + 1):
                tasks.append(functools.partial(project, i))
                waiting.append(i)
        if state["weights"]:
            for i in waiting:
                seq, b = divmod(i, per_seq)
                tasks += [
                    functools.partial(project_latent, i),
                    functools.partial(project_keys, i),
                    functools.partial(project_queries, i),
                    functools.partial(attend, seq, b),
                ]
                if b == per_seq - 1:
                    tasks.append(functools.partial(keep_some, range(10), seq))
            waiting.clear()
        return tasks

    first_tasks = [lambda: [copy.start() for copy in loads]]
    work_through(gather_steps(row, z, y, c, depth, pieces, send_sem, recv_sem), ready, first_tasks)
    for group in swaps:
        for swap in group:
            swap.wait_send()
    for copy in weights_out:
        copy.wait()
    for seq in range(seqs):
        for array in range(10):
            keep(array, seq).wait()
    for swap in late:
        swap.wait()


def attention_forward(
    tokens, gain, query_own, down_own, up_own, choose, latent_gain, tables, seg_col, seg_row, collective_id, swaps=()
):
    n, n_row = lax.axis_size("col"), lax.axis_size("row")
    depth, rows = n // 4, tokens.shape[0]
    width, seqs = n * tokens.shape[1], rows // LEN
    padded = n * down_own.shape[0]
    in_vmem = pl.BlockSpec(memory_space=pltpu.VMEM)
    anywhere = pl.BlockSpec(memory_space=pl.ANY)
    count = 2 + rows // PIECE
    dma = pltpu.SemaphoreType.DMA
    shape = jax.ShapeDtypeStruct
    kept = [
        shape((rows, 2 * LANES), BF16),
        shape((rows, 2 * LANES), BF16),
        shape((rows, VD), BF16),
        shape((rows, LATENT), BF16),
        shape((rows, LATENT + LANES), BF16),
        shape((rows, LANES), F32),
        shape((rows, LANES), F32),
        shape((rows, VD), BF16),
        shape((rows, LANES), F32),
    ]
    loads = [choose, latent_gain, *tables, seg_col, seg_row]
    swapped = [swap.array for swap in swaps]
    return pl.pallas_call(
        functools.partial(
            forward_kernel, depth, n_row, (rows, width, seqs), tuple((swap.t, swap.index) for swap in swaps)
        ),
        out_shape=[shape((rows, width), BF16)]
        + kept
        + [
            shape((2 * LANES, width), BF16),
            shape((padded, width), BF16),
            shape((LATENT, 2 * LANES), BF16),
        ]
        + [swap.shape for swap in swaps],
        in_specs=[anywhere] * (11 + len(swapped)),
        out_specs=[anywhere] * (13 + len(swapped)),
        scratch_shapes=[
            pltpu.VMEM((rows, width), BF16),
            pltpu.VMEM((gain.shape[0], width), F32),
            pltpu.VMEM((rows, width), BF16),
            pltpu.VMEM((2 * LANES, width), BF16),
            pltpu.VMEM((down_own.shape[0], width), BF16),
            pltpu.VMEM((padded, width), BF16),
            pltpu.VMEM((LATENT, 2 * LANES), BF16),
        ]
        + [pltpu.VMEM(a.shape, a.dtype) for a in [*kept, *loads]]
        + [
            dma((count, 8 * depth)),
            dma((count, n)),
            dma((3, n_row)),
            dma((3, n_row)),
            dma((6,)),
            dma((10, seqs)),
            dma((3,)),
            dma((max(1, len(swapped)),)),
            dma((max(1, len(swapped)),)),
            dma((len(loads),)),
        ],
        compiler_params=pltpu.CompilerParams(
            collective_id=collective_id, has_side_effects=True, vmem_limit_bytes=60 << 20
        ),
        name="attention_forward",
    )(tokens, gain, query_own, down_own, up_own, *loads, *swapped)


def sigmoid_parts(values):
    sigmoid = jax.nn.sigmoid(values)
    return values * sigmoid, sigmoid * (1.0 + values * (1.0 - sigmoid))


def three_terms(column, width, first):
    high = column.astype(BF16).astype(F32)
    middle = (column - high).astype(BF16).astype(F32)
    lane = lax.broadcasted_iota(jnp.int32, (column.shape[0], width), 1)
    out = jnp.where(lane == first, high, 0.0)
    out = jnp.where(lane == first + 1, middle, out)
    return jnp.where(lane == first + 2, column - high - middle, out)


def copier(sem):
    count = itertools.count()
    return lambda source, target: pltpu.make_async_copy(source, target, sem.at[next(count)])


def hidden_kernel(depth, n_row, sizes, shifts, *refs):
    rows, width, capacity, narrow, experts = sizes
    block, squares, slot_row = refs[:3]
    parts, refs = refs[3 : 3 + 3 * n_row], refs[3 + 3 * n_row :]
    swaps_in, refs = refs[: len(shifts)], refs[len(shifts) :]
    outs, swaps_out, refs = refs[:11], refs[11 : 11 + len(shifts)], refs[11 + len(shifts) :]
    held, refs = refs[:11], refs[11:]
    (full, full_squares, gate_terms, send_sem, recv_sem, local_sem, swap_send, swap_recv) = refs
    (normed, picked, gate_in, up_in, act, logits, root, slot_gate, gate_weight, up_weight, router) = held
    row, z, y, c = place()
    me, n = col_of(z, y, c), 4 * depth
    greet_neighbours(row, z, y, c, depth, n_row)
    swaps = swap_start(row, me, n_row, shifts, swaps_in, swaps_out, swap_send, swap_recv)
    local = copier(local_sem)

    def lanes(block):
        return pl.ds(pl.multiple_of(rolled(block, row, n_row, n) * LANES, LANES), LANES)

    own = [
        local(block, full.at[:, lanes(me)]),
        local(squares, full_squares.at[:, lanes(me)]),
    ]
    share = width // n_row
    for i, target in enumerate((gate_weight, up_weight, router)):
        own += [local(parts[i * n_row + p], target.at[:, span_of(p, share)]) for p in range(n_row)]
    for copy in own:
        copy.start()
    pieces = [Piece(squares, lambda block: full_squares.at[:, lanes(block)])]
    pieces += row_pieces(block, rows, lambda span, block: full.at[span, lanes(block)])
    results = {}

    def store(name, index=slice(None)):
        copy = local(held[name].at[index], outs[name].at[index])
        results[len(results)] = copy
        copy.start()

    def roots():
        for copy in own:
            copy.wait()
        total = sum(full_squares[:, j * LANES : (j + 1) * LANES] for j in range(n))
        columns = jnp.transpose(lax.rsqrt(total / width + EPSILON))
        for i in range(rows // LANES):
            root[span_of(i, LANES), :] = jnp.broadcast_to(columns[:, i : i + 1], (LANES, LANES))
        for name in (6, 8, 9, 10):
            store(name)

    def norm(i):
        span = span_of(i, TILE)
        normed[span, :] = (full[span, :].astype(F32) * root[span, :1]).astype(BF16)

    def project(i):
        span = span_of(i, TILE)
        gate = dot_nt(normed[span, :], gate_weight[...])
        up = dot_nt(normed[span, :], up_weight[...])
        gate_in[span, :] = gate.astype(BF16)
        up_in[span, :] = up.astype(BF16)
        act[span, :] = (gate * jax.nn.sigmoid(gate) * up).astype(BF16)

    def route(i):
        span = span_of(i, TILE)
        scores = dot_nt(normed[span, :], router[...])
        logits[span, :] = scores
        weights = jnp.exp(scores - jnp.max(scores, -1, keepdims=True))
        mine = lax.broadcasted_iota(jnp.int32, scores.shape, 1) == me
        own_gate = jnp.sum(jnp.where(mine, weights, 0.0), -1, keepdims=True) / jnp.sum(
            weights, -1, keepdims=True
        )
        gate_terms[span, :] = three_terms(own_gate, LANES, 0).astype(BF16)

    def pick(q, t):
        tokens, span = span_of(q, 2 * TILE), span_of(t, TILE)
        here = lax.broadcasted_iota(jnp.int32, (TILE, 2 * TILE), 0) + t * TILE
        chosen = jnp.where(here == slot_row[:1, tokens], 1.0, 0.0).astype(BF16)
        term = dot_nn(chosen, normed[tokens, :])
        gates = dot_nn(chosen, gate_terms[tokens, :])
        if q == 0:
            picked[span, :] = term.astype(BF16)
            slot_gate[span, :] = gates
        else:
            picked[span, :] = (picked[span, :].astype(F32) + term).astype(BF16)
            slot_gate[span, :] += gates

    def finish():
        total = jnp.sum(slot_gate[...], 1, keepdims=True)
        slot_gate[...] = jnp.broadcast_to(total, slot_gate.shape)
        for name in (1, 2, 3, 4, 5, 7):
            store(name)

    def ready(p):
        if p == 0:
            return [roots]
        q = p - 1
        tasks = [functools.partial(norm, i) for i in (2 * q, 2 * q + 1)]
        tasks += [functools.partial(route, i) for i in (2 * q, 2 * q + 1)]
        tasks += [functools.partial(pick, q, t) for t in range(capacity // TILE)]
        tasks += [functools.partial(project, i) for i in (2 * q, 2 * q + 1)]
        tasks.append(functools.partial(store, 0, span_of(q, PIECE)))
        if p == len(pieces) - 1:
            tasks.append(finish)
        return tasks

    work_through(gather_steps(row, z, y, c, depth, pieces, send_sem, recv_sem), ready)
    for copy in results.values():
        copy.wait()
    for swap in swaps:
        swap.wait()


def hidden_rows(block, squares, slot_row, parts, capacity, collective_id, swaps=()):
    n, n_row = lax.axis_size("col"), lax.axis_size("row")
    depth, rows = n // 4, block.shape[0]
    width, narrow, experts = n * block.shape[1], parts[0].shape[0], parts[-1].shape[0]
    anywhere = pl.BlockSpec(memory_space=pl.ANY)
    dma, shape = pltpu.SemaphoreType.DMA, jax.ShapeDtypeStruct
    swapped = [swap.array for swap in swaps]
    count = 1 + rows // PIECE
    kept = [
        shape((rows, width), BF16),
        shape((capacity, width), BF16),
        shape((rows, narrow), BF16),
        shape((rows, narrow), BF16),
        shape((rows, narrow), BF16),
        shape((rows, experts), F32),
        shape((rows, LANES), F32),
        shape((capacity, LANES), F32),
        shape((narrow, width), BF16),
        shape((narrow, width), BF16),
        shape((experts, width), BF16),
    ]
    return pl.pallas_call(
        functools.partial(
            hidden_kernel,
            depth,
            n_row,
            (rows, width, capacity, narrow, experts),
            tuple((swap.t, swap.index) for swap in swaps),
        ),
        out_shape=kept + [swap.shape for swap in swaps],
        in_specs=[anywhere] * 2
        + [pl.BlockSpec(memory_space=pltpu.VMEM)]
        + [anywhere] * (len(parts) + len(swapped)),
        out_specs=[anywhere] * (len(kept) + len(swapped)),
        scratch_shapes=[pltpu.VMEM(a.shape, a.dtype) for a in kept]
        + [
            pltpu.VMEM((rows, width), BF16),
            pltpu.VMEM((squares.shape[0], width), F32),
            pltpu.VMEM((rows, LANES), BF16),
            dma((count, 8 * depth)),
            dma((count, n)),
            dma((2 + 3 * n_row + 10 + rows // TILE,)),
            dma((max(1, len(swapped)),)),
            dma((max(1, len(swapped)),)),
        ],
        compiler_params=pltpu.CompilerParams(
            collective_id=collective_id, has_side_effects=True, vmem_limit_bytes=60 << 20
        ),
        name="hidden_rows",
    )(block, squares, slot_row, *parts, *swapped)


def mixture_kernel(depth, n_row, sizes, falls, *refs):
    rows, width, capacity, hidden_units, narrow, experts = sizes
    block, picked_in, slot_row, slot_col, logits_in, slot_gate_in, gate_in, up_in = refs[:8]
    refs = refs[8:]
    each = 2 * n_row - 1
    gate_parts, up_parts, refs = refs[:each], refs[each : 2 * each], refs[2 * each :]
    fall_own, fall_got, refs = refs[0], refs[1:n_row], refs[n_row:]
    shared_parts, refs = refs[:n_row], refs[n_row:]
    outs, refs = refs[:9], refs[9:]
    (fall_out, rows_out, act_out, dgate_out, dup_out, grad_out, sgate_out, sup_out, coef_out) = outs
    (stat_out, full_out, shared_out, probs_out), refs = refs[:4], refs[4:]
    sent_out, refs = refs[: n_row - 1], refs[n_row - 1 :]
    (full, gate_weight, up_weight, fall_weight, picked, gate, up, act, grads, shared_weight) = refs[:10]
    (shared_gate, shared_up, logits, slot_cols, slot_gates, values, inner, coefs, stats, shares), refs = refs[10:20], refs[20:]
    (staged, send_sem, recv_sem, local_sem, swap_send, swap_recv) = refs
    row, z, y, c = place()
    me, n = col_of(z, y, c), 4 * depth
    greet_neighbours(row, z, y, c, depth, n_row)
    share = width // n_row
    first = falls
    swaps = [
        swap_copy(
            row, me, n_row, fall_own.at[0, pl.ds(first, hidden_units - first)],
            fall_weight.at[pl.ds(first, hidden_units - first), span_of(n_row - t, share)],
            t, swap_send.at[t], swap_recv.at[t],
        )
        for t in range(1, n_row)
    ]
    for swap in swaps:
        swap.start()
    local = copier(local_sem)

    def lanes(block):
        return pl.ds(pl.multiple_of(rolled(block, row, n_row, n) * LANES, LANES), LANES)

    loads = [local(picked_in, picked)]
    for weight, pieces in ((gate_weight, gate_parts), (up_weight, up_parts)):
        loads.append(local(pieces[0].at[0], weight.at[span_of(0, share)]))
        at = share
        for piece in pieces[1:]:
            loads.append(local(piece, weight.at[pl.ds(at, piece.shape[0])]))
            at += piece.shape[0]
    later = [
        local(block, full.at[:, lanes(me)]),
        local(slot_gate_in, slot_gates),
        local(logits_in, logits),
        local(slot_col, slot_cols),
        local(gate_in, shared_gate),
        local(up_in, shared_up),
        local(fall_own.at[0], fall_weight.at[:, span_of(0, share)]),
    ]
    for p in range(n_row):
        later.append(local(shared_parts[p], shared_weight.at[:, span_of(p, share)]))
        if p:
            later.append(local(fall_got[p - 1], fall_weight.at[pl.ds(0, first), span_of(p, share)]))
    later[0].start()
    pieces = row_pieces(block, rows, lambda span, block: full.at[span, lanes(block)])
    chunk = 4 * LANES
    chunks = [(at, min(chunk, hidden_units - at)) for at in range(0, hidden_units, chunk)]
    results = []

    def store(source, target):
        copy = local(source, target)
        copy.start()
        results.append(copy)

    def begin():
        for copy in loads:
            copy.wait()

    def begin_more():
        for copy in later:
            copy.wait()
        store(shared_weight, shared_out)

    def fetch(copies):
        for copy in copies:
            copy.start()

    def forward(t, at, size):
        span, cols = span_of(t, TILE), pl.ds(at, size)
        g = dot_nn(picked[span, :], gate_weight[:, cols])
        u = dot_nn(picked[span, :], up_weight[:, cols])
        gate[span, cols] = g.astype(BF16)
        up[span, cols] = u.astype(BF16)
        act[span, cols] = (g * jax.nn.sigmoid(g) * u).astype(BF16)
        if at + size == hidden_units:
            store(act.at[span], act_out.at[span])

    def shared(i):
        span = span_of(i, TILE)
        raw = dot_nt(full[span, :], shared_weight[...])
        g, u = shared_gate[span, :].astype(F32), shared_up[span, :].astype(F32)
        silu, slope = sigmoid_parts(g)
        dg, du = (raw * u * slope).astype(BF16), (raw * silu).astype(BF16)
        inner[span, :] = jnp.broadcast_to(
            jnp.sum(g * dg.astype(F32) + u * du.astype(F32), 1, keepdims=True), (TILE, LANES)
        )
        shared_gate[span, :] = dg
        shared_up[span, :] = du

    def pick(q, t):
        tokens, span = span_of(q, 2 * TILE), span_of(t, TILE)
        here = lax.broadcasted_iota(jnp.int32, (TILE, 2 * TILE), 0) + t * TILE
        chosen = jnp.where(here == slot_row[:1, tokens], 1.0, 0.0).astype(BF16)
        term = dot_nn(chosen, full[tokens, :])
        if q == 0:
            grads[span, :] = term.astype(BF16)
        else:
            grads[span, :] = (grads[span, :].astype(F32) + term).astype(BF16)

    def fall_here():
        for swap in swaps:
            swap.wait()
        store(fall_weight, fall_out)

    staging = []

    def stage(value, target):
        slot = len(staging) % 2
        if len(staging) > 1:
            staging[-2].wait()
        spot = staged.at[slot, pl.ds(0, value.shape[0]), pl.ds(0, value.shape[1])]
        spot[...] = value
        copy = local(spot, target)
        copy.start()
        staging.append(copy)

    def weigh_rows(t):
        span = span_of(t, TILE)
        picked[span, :] = (grads[span, :].astype(F32) * slot_gates[span, :1]).astype(BF16)

    def weigh(p, at, size):
        value = dot_tn(act[:, pl.ds(at, size)], picked[:, span_of(p, share)])
        stage(value.astype(BF16), sent_out[p - 1].at[pl.ds(at, size)])

    def backward(t):
        span = span_of(t, TILE)
        scale = slot_gates[span, :1]
        raw_left = grads[span, :]
        gate_dot = jnp.zeros((TILE, 1), F32)
        slot_dot = jnp.zeros((TILE, 1), F32)
        for at, size in chunks:
            cols = pl.ds(at, size)
            raw = dot_nt(raw_left, fall_weight[cols, :])
            g, u = gate[span, cols].astype(F32), up[span, cols].astype(F32)
            gate_dot += jnp.sum(act[span, cols].astype(F32) * raw, 1, keepdims=True)
            silu, slope = sigmoid_parts(g)
            scaled = raw * scale
            dg, du = (scaled * u * slope).astype(BF16), (scaled * silu).astype(BF16)
            slot_dot += jnp.sum(g * dg.astype(F32) + u * du.astype(F32), 1, keepdims=True)
            gate[span, cols] = dg
            up[span, cols] = du
        store(picked.at[span], grad_out.at[span])
        values[span, :] = (
            three_terms(gate_dot, LANES, 0) + three_terms(slot_dot, LANES, 3)
        ).astype(BF16)
        store(gate.at[span], dgate_out.at[span])
        store(up.at[span], dup_out.at[span])

    def to_rows(t):
        span = span_of(t, TILE)
        back = dot_nt(gate[span, :], gate_weight[...]) + dot_nt(up[span, :], up_weight[...])
        stage(back.astype(BF16), rows_out.at[span])

    def settle(i):
        span = span_of(i, TILE)
        here = lax.broadcasted_iota(jnp.int32, (TILE, capacity), 1)
        chosen = jnp.where(here == slot_cols[span, :1], 1.0, 0.0).astype(BF16)
        terms = dot_nn(chosen, values[...])
        lane = lax.broadcasted_iota(jnp.int32, terms.shape, 1)
        token_dot = jnp.sum(jnp.where(lane < 3, terms, 0.0), 1, keepdims=True)
        slot_dot = jnp.sum(jnp.where(lane >= 3, terms, 0.0), 1, keepdims=True)
        scores = logits[span, :]
        weights = jnp.exp(scores - jnp.max(scores, -1, keepdims=True))
        probs = weights / jnp.sum(weights, -1, keepdims=True)
        mine = jnp.where(lax.broadcasted_iota(jnp.int32, scores.shape, 1) == me, 1.0, 0.0)
        part = jnp.sum(probs * mine, -1, keepdims=True) * token_dot
        coef = (part * (mine - probs)).astype(BF16)
        coefs[span, :] = coef
        shares[span, :] = probs
        total = (
            inner[span, :1] + slot_dot + jnp.sum(coef.astype(F32) * scores, -1, keepdims=True)
        )
        stats[span, :] = jnp.where(lane == 0, total, jnp.where(lane == 1, part, 0.0))

    slots = range(capacity // TILE)

    def ready(p):
        tasks = [begin_more] if p == 0 else []
        tasks += [functools.partial(pick, p, t) for t in slots]
        tasks += [functools.partial(shared, i) for i in (2 * p, 2 * p + 1)]
        tasks.append(functools.partial(store, full.at[span_of(p, PIECE)], full_out.at[span_of(p, PIECE)]))
        if p == len(pieces) - 1:
            tasks.append(lambda: [store(shared_gate, sgate_out), store(shared_up, sup_out)])
            tasks += [functools.partial(weigh_rows, t) for t in slots]
            for q in range(1, n_row):
                for at in range(0, hidden_units, TILE):
                    tasks.append(functools.partial(weigh, q, at, min(TILE, hidden_units - at)))
            tasks.append(fall_here)
            for t in slots:
                tasks += [functools.partial(backward, t), functools.partial(to_rows, t)]
            tasks += [functools.partial(settle, i) for i in range(rows // TILE)]
        return tasks

    first_tasks = [
        functools.partial(fetch, loads[: len(loads) // 2 + 1]),
        functools.partial(fetch, loads[len(loads) // 2 + 1 :]),
        functools.partial(fetch, later[1:]),
        begin,
    ] + [
        functools.partial(forward, t, at, size) for t in slots for at, size in chunks
    ]
    work_through(gather_steps(row, z, y, c, depth, pieces, send_sem, recv_sem), ready, first_tasks)
    store(coefs, coef_out)
    store(stats, stat_out)
    store(shares, probs_out)
    for copy in results + staging[-2:]:
        copy.wait()


def mixture(
    block, picked, slot_row, slot_col, logits, slot_gate, gate_in, up_in,
    gate_pieces, up_pieces, fall, fall_got, shared_parts, collective_id,
):
    n, n_row = lax.axis_size("col"), lax.axis_size("row")
    depth, rows = n // 4, block.shape[0]
    width = n * block.shape[1]
    capacity, hidden_units = picked.shape[0], fall.shape[1]
    narrow, experts = gate_in.shape[1], logits.shape[1]
    anywhere = pl.BlockSpec(memory_space=pl.ANY)
    dma, shape = pltpu.SemaphoreType.DMA, jax.ShapeDtypeStruct
    count = rows // PIECE
    first = fall_got[0].shape[0] if fall_got else 0
    operands = [block, picked, slot_row, slot_col, logits, slot_gate, gate_in, up_in]
    operands += [*gate_pieces, *up_pieces, fall, *fall_got, *shared_parts]
    out_shape = [
        shape((hidden_units, width), BF16),
        shape((capacity, width), BF16),
        shape((capacity, hidden_units), BF16),
        shape((capacity, hidden_units), BF16),
        shape((capacity, hidden_units), BF16),
        shape((capacity, width), BF16),
        shape((rows, narrow), BF16),
        shape((rows, narrow), BF16),
        shape((rows, experts), BF16),
        shape((rows, LANES), F32),
        shape((rows, width), BF16),
        shape((narrow, width), BF16),
        shape((rows, experts), F32),
    ] + [shape((hidden_units, width // n_row), BF16)] * (n_row - 1)
    return pl.pallas_call(
        functools.partial(
            mixture_kernel, depth, n_row, (rows, width, capacity, hidden_units, narrow, experts), first
        ),
        out_shape=out_shape,
        in_specs=[anywhere] * 2
        + [pl.BlockSpec(memory_space=pltpu.VMEM)]
        + [anywhere] * (len(operands) - 3),
        out_specs=[anywhere] * len(out_shape),
        scratch_shapes=[
            pltpu.VMEM((rows, width), BF16),
            pltpu.VMEM((width, hidden_units), BF16),
            pltpu.VMEM((width, hidden_units), BF16),
            pltpu.VMEM((hidden_units, width), BF16),
            pltpu.VMEM((capacity, width), BF16),
            pltpu.VMEM((capacity, hidden_units), BF16),
            pltpu.VMEM((capacity, hidden_units), BF16),
            pltpu.VMEM((capacity, hidden_units), BF16),
            pltpu.VMEM((capacity, width), BF16),
            pltpu.VMEM((narrow, width), BF16),
            pltpu.VMEM((rows, narrow), BF16),
            pltpu.VMEM((rows, narrow), BF16),
            pltpu.VMEM((rows, experts), F32),
            pltpu.VMEM((rows, LANES), jnp.int32),
            pltpu.VMEM((capacity, LANES), F32),
            pltpu.VMEM((capacity, LANES), BF16),
            pltpu.VMEM((rows, LANES), F32),
            pltpu.VMEM((rows, experts), BF16),
            pltpu.VMEM((rows, LANES), F32),
            pltpu.VMEM((rows, experts), F32),
            pltpu.VMEM((2, TILE, width), BF16),
            dma((count, 8 * depth)),
            dma((count, n)),
            dma((96,)),
            dma((n_row,)),
            dma((n_row,)),
        ],
        compiler_params=pltpu.CompilerParams(
            collective_id=collective_id, has_side_effects=True, vmem_limit_bytes=63 << 20
        ),
        name="mixture",
    )(*operands)


def backward_kernel(depth, n_row, sizes, shifts, *refs):
    grad, loads, refs = refs[0], refs[1:18], refs[18:]
    swaps_in, refs = refs[: len(shifts)], refs[len(shifts) :]
    (gain_back, *rounded), outs, refs = refs[:4], refs[4:8], refs[8:]
    swaps_out, refs = refs[: len(shifts)], refs[len(shifts) :]
    held, refs = refs[:17], refs[17:]
    (out_full, q, k, v, latent, low, latent_root, mixed, lse, up_full, choose, latent_gain) = held[:12]
    (cosines, sines, seg_col, seg_row, normed) = held[12:]
    (query_back, low_long, low_wide, inner), refs = refs[:4], refs[4:]
    results = (query_back, low_long, low_wide, inner)
    (full, keys_back, values_back, mixed_back), refs = refs[:4], refs[4:]
    (out_back, query_weight_back, up_weight_back), refs = refs[:3], refs[3:]
    (send_sem, recv_sem, local_sem, load_sem, out_sem, swap_send, swap_recv) = refs
    rows, width, seqs = sizes
    row, z, y, c = place()
    me, n = col_of(z, y, c), 4 * depth
    greet_neighbours(row, z, y, c, depth, n_row if shifts else 1)
    def lanes(block):
        return pl.ds(pl.multiple_of(rolled(block, row, n_row, n) * LANES, LANES), LANES)

    keep = pltpu.make_async_copy(grad, full.at[:, lanes(me)], local_sem)
    keep.start()
    fetches = [
        pltpu.make_async_copy(a, b, load_sem.at[i]) for i, (a, b) in enumerate(zip(loads, held))
    ]

    def result(array, seq):
        span = pl.ds(seq * LEN, LEN)
        span = (slice(None), span) if array == 2 else (span,)
        return pltpu.make_async_copy(results[array].at[span], outs[array].at[span], out_sem.at[array, seq])

    def store(seq):
        for array in range(4):
            result(array, seq).start()

    pieces = row_pieces(grad, rows, lambda span, block: full.at[span, lanes(block)])
    per_seq = LEN // TILE
    lower = lax.broadcasted_iota(jnp.int32, (TILE, LANES), 1) < ROPE

    def begin():
        keep.wait()
        for fetch in fetches:
            fetch.wait()
        for total in (gain_back, out_back, query_weight_back, up_weight_back):
            total[...] = jnp.zeros_like(total)

    def project(i):
        span = span_of(i, TILE)
        out_back[...] += dot_tn(mixed[span, :], full[span, :])
        mixed_back[...] = dot_nt(full[span, :], out_full[...]).astype(BF16)

    def attend(seq, block):
        base, first = seq * LEN, block * TILE
        length = first + TILE
        span, keys = pl.ds(base + first, TILE), pl.ds(base, length)
        at = pl.ds(first, TILE)
        grad_mixed = mixed_back[...]
        scores = masked_scores(q, k, seg_col, seg_row, base, first, length)
        probs = jnp.exp(scores - lse[span, :1])
        grad_probs = dot_nt(grad_mixed, v[keys, :])
        grad_scores = (
            probs * (grad_probs - jnp.sum(probs * grad_probs, -1, keepdims=True))
        ).astype(BF16)
        back = dot_nn(grad_scores, k[keys, :]) * SCALE
        nope, tile = back[:, :NOPE], back[:, NOPE:]
        inner[span, :] = jnp.broadcast_to(
            jnp.sum(nope * q[span, :NOPE].astype(F32), 1, keepdims=True)
            + 0.5 * jnp.sum(tile * q[span, NOPE:].astype(F32), 1, keepdims=True),
            (TILE, LANES),
        )
        query_back[span, :NOPE] = nope.astype(BF16)
        turned = turn(tile, cosines[at, :], -sines[at, :])
        query_back[span, NOPE:] = jnp.where(lower, turned, 0.0).astype(BF16)
        keys_term = dot_tn(grad_scores, q[span, :])
        values_term = dot_tn(probs.astype(BF16), grad_mixed)
        keys_back[first:length, :] = keys_term[first:, :]
        values_back[first:length, :] = values_term[first:, :]
        if first:
            keys_back[:first, :] += keys_term[:first, :]
            values_back[:first, :] += values_term[:first, :]

    def weigh(i):
        span = span_of(i, TILE)
        query_weight_back[...] += dot_tn(query_back[span, :], normed[span, :])

    def expand(seq, block):
        first = block * TILE
        span, at = pl.ds(seq * LEN + first, TILE), pl.ds(first, TILE)
        back = keys_back[at, :] * SCALE
        expanded = jnp.concatenate([back[:, :NOPE], values_back[at, :]], 1).astype(BF16)
        up_weight_back[...] += dot_tn(expanded, latent[span, :])
        latent_grad = dot_nt(expanded, up_full[...])
        compressed = low[span, :LATENT].astype(F32)
        root = latent_root[span, :1]
        dots = jnp.sum(latent_grad * latent[span, :].astype(F32), 1, keepdims=True)
        gain_back[...] += jnp.broadcast_to(
            jnp.sum(latent_grad * compressed * root, 0, keepdims=True), gain_back.shape
        )
        compressed_grad = root * latent_grad * latent_gain[:1, :] - compressed * (
            root * root * dots / LATENT
        )
        turned = turn(back[:, NOPE:], cosines[at, :], -sines[at, :])
        low_grad = jnp.concatenate([compressed_grad, jnp.where(lower, turned, 0.0)], 1).astype(BF16)
        low_wide[:, span] = dot_nt(choose[...], low_grad).astype(BF16)
        low_long[span, :] = dot_nt(low_grad, choose[...]).astype(BF16)
        inner[span, :] += jnp.broadcast_to(
            jnp.sum(low_grad.astype(F32) * low[span, :].astype(F32), 1, keepdims=True),
            (TILE, LANES),
        )

    def ready(p):
        tasks = [begin] if p == 0 else []
        for i in (2 * p, 2 * p + 1):
            seq, block = divmod(i, per_seq)
            tasks += [functools.partial(project, i), functools.partial(attend, seq, block)]
            tasks.append(functools.partial(weigh, i))
            if block == per_seq - 1:
                tasks += [functools.partial(expand, seq, b) for b in range(per_seq)]
                tasks.append(functools.partial(store, seq))
        return tasks

    swaps = swap_start(row, me, n_row, shifts, swaps_in, swaps_out, swap_send, swap_recv)
    first_tasks = [
        lambda: [fetch.start() for fetch in fetches[:8]],
        lambda: [fetch.start() for fetch in fetches[8:]],
    ]
    work_through(gather_steps(row, z, y, c, depth, pieces, send_sem, recv_sem), ready, first_tasks)
    for total, target in zip((out_back, query_weight_back, up_weight_back), rounded):
        target[...] = total[...].astype(BF16)
    for seq in range(seqs):
        for array in range(4):
            result(array, seq).wait()
    for swap in swaps:
        swap.wait()


def attention_backward(grad, operands, collective_id, swaps=()):
    n, n_row = lax.axis_size("col"), lax.axis_size("row")
    depth, rows = n // 4, grad.shape[0]
    width, seqs = n * grad.shape[1], rows // LEN
    in_vmem = pl.BlockSpec(memory_space=pltpu.VMEM)
    anywhere = pl.BlockSpec(memory_space=pl.ANY)
    count = rows // PIECE
    dma = pltpu.SemaphoreType.DMA
    shape = jax.ShapeDtypeStruct
    swapped = [swap.array for swap in swaps]
    kept = [
        shape((rows, 2 * LANES), BF16),
        shape((rows, operands[10].shape[0]), BF16),
        shape((operands[10].shape[0], rows), BF16),
        shape((rows, LANES), F32),
    ]
    return pl.pallas_call(
        functools.partial(
            backward_kernel, depth, n_row, (rows, width, seqs), tuple((swap.t, swap.index) for swap in swaps)
        ),
        out_shape=[
            shape((8, LATENT), F32),
            shape((VD, width), BF16),
            shape((2 * LANES, width), BF16),
            shape((2 * LANES, LATENT), BF16),
        ]
        + kept
        + [swap.shape for swap in swaps],
        in_specs=[anywhere] * (18 + len(swapped)),
        out_specs=[in_vmem] * 4 + [anywhere] * (4 + len(swapped)),
        scratch_shapes=[pltpu.VMEM(a.shape, a.dtype) for a in [*operands, *kept]]
        + [
            pltpu.VMEM((rows, width), BF16),
            pltpu.VMEM((LEN, 2 * LANES), F32),
            pltpu.VMEM((LEN, VD), F32),
            pltpu.VMEM((TILE, VD), BF16),
            pltpu.VMEM((VD, width), F32),
            pltpu.VMEM((2 * LANES, width), F32),
            pltpu.VMEM((2 * LANES, LATENT), F32),
            dma((count, 8 * depth)),
            dma((count, n)),
            dma,
            dma((17,)),
            dma((4, seqs)),
            dma((max(1, len(swapped)),)),
            dma((max(1, len(swapped)),)),
        ],
        compiler_params=pltpu.CompilerParams(
            collective_id=collective_id, has_side_effects=True, vmem_limit_bytes=60 << 20
        ),
        name="attention_backward",
    )(grad, *operands, *swapped)


def row_shift(array, step):
    n = lax.axis_size("row")
    return lax.ppermute(array, "row", [(i, (i - step) % n) for i in range(n)])


def to_others(*arrays):
    pairs = [array if isinstance(array, tuple) else (array, ()) for array in arrays]
    return [Swap(array, t, index) for array, index in pairs for t in range(1, lax.axis_size("row"))]


def from_others(got, index):
    others = lax.axis_size("row") - 1
    return got[index * others : (index + 1) * others][::-1]


def row_parts(array):
    return [array] + [row_shift(array, s) for s in range(1, lax.axis_size("row"))]


def row_sum(parts):
    return row_add(parts[0], [part.astype(BF16) for part in parts[1:]])


def row_add(total, parts):
    n = lax.axis_size("row")
    return row_sum_of(total, [row_shift(part, n - s) for s, part in enumerate(parts, 1)])


def row_sum_of(total, received):
    for part in received:
        total = total + part.astype(F32)
    return total


def unroll_parts(parts, axis):
    n = len(parts)
    size = parts[0].shape[axis]
    doubled = jnp.concatenate(parts + parts[:-1], axis)
    start = lax.rem(n - lax.axis_index("row"), n) * size
    return lax.dynamic_slice_in_dim(doubled, start, n * size, axis)


def own_parts(array, axis):
    n = lax.axis_size("row")
    size = array.shape[axis] // n
    row = lax.axis_index("row")
    return [
        lax.dynamic_slice_in_dim(array, lax.rem(row + s, n) * size, size, axis) for s in range(n)
    ]


def interleave(first, second):
    return [array for pair in zip(first, second) for array in pair]


def cut(array, axis):
    return jnp.split(array, lax.axis_size("row"), axis)


def as_stat(*vectors):
    return jnp.concatenate([v.reshape(-1, LANES) for v in vectors], 0)


def per_device(
    tokens,
    cotangent,
    segments,
    routes,
    first_gain,
    query_proj,
    latent_down,
    latent_gain,
    latent_up,
    output_proj,
    second_gain,
    router_weight,
    expert_gate,
    expert_up,
    expert_down,
    shared_gate,
    shared_up,
    shared_down,
):
    row_count, share = tokens.shape
    n = lax.axis_size("col")
    width = share * n
    column = lax.axis_index("col")
    seqs = segments.shape[0]
    narrow = latent_down.shape[1]
    padding = -narrow % 16
    tables = rotary_tables()
    seg_flat = segments.reshape(-1)
    seg_col = jnp.broadcast_to(seg_flat[:, None], (row_count, LANES))
    seg_row = jnp.broadcast_to(seg_flat[None, :], (8, row_count))
    column_of = np.arange(n * narrow)
    turned_of = np.concatenate([column_of, column_of[LATENT + 32 :], column_of[LATENT : LATENT + 32]])
    wide_of = turned_of // narrow * (narrow + padding) + turned_of % narrow
    choose = jnp.asarray((np.arange(n * (narrow + padding))[:, None] == wide_of[None, :]).astype(BF16))

    experts = router_weight.shape[1]
    capacity = row_count * routes.shape[1] * 4 // (3 * experts)
    member = jnp.any(routes == column, 1)
    slot_number = jnp.where(member, jnp.cumsum(member.astype(jnp.int32)) - 1, -1)
    slot_row = jnp.broadcast_to(slot_number[None, :], (8, row_count))
    slot_col = jnp.broadcast_to(slot_number[:, None], (row_count, LANES))
    part = expert_gate.shape[1]
    gate_cut, up_cut, fall_first = part * 9 // 16, part * 3 // 8, 2 * LANES
    gate_low, gate_high = (0, (0, gate_cut)), (0, (gate_cut, part - gate_cut))
    up_low, up_high = (0, (0, up_cut)), (0, (up_cut, part - up_cut))
    pick_back = (slot_number[:, None] == jnp.arange(capacity)[None, :]).astype(BF16)

    latent_gains = jnp.broadcast_to(latent_gain[None, :], (8, LATENT))
    (
        normed,
        queries,
        keys,
        values,
        latent,
        low,
        first_root,
        latent_root,
        mixed,
        log_total,
        query_full,
        down_full,
        up_full,
        *got,
    ) = attention_forward(
        tokens,
        jnp.broadcast_to(first_gain[None, :], (8, share)),
        query_proj.T,
        jnp.pad(latent_down.T, ((0, padding), (0, 0))),
        latent_up,
        choose,
        latent_gains,
        tables,
        seg_col,
        seg_row,
        1,
        to_others(
            output_proj, shared_gate.T, shared_up.T, router_weight.T, (expert_gate, gate_low)
        ),
    )
    out_full = jnp.concatenate([output_proj] + from_others(got, 0), 1)
    shared_gate_parts = [shared_gate.T] + from_others(got, 1)
    shared_up_parts = [shared_up.T] + from_others(got, 2)
    router_parts = [router_weight.T] + from_others(got, 3)
    gate_first = from_others(got, 4)
    first_root = first_root[:, :1]
    branch, *got = scatter_cols(
        [("nn", mixed, out_full)], None, 2, 2, to_others((expert_gate, gate_high), (expert_up, up_low))
    )
    gate_pieces = [expert_gate] + interleave(gate_first, from_others(got, 0))
    up_first = from_others(got, 1)
    hidden = tokens.astype(F32) + branch
    (
        normed_two,
        picked,
        shared_in,
        shared_lift,
        shared_act,
        logits,
        second_root,
        slot_gate,
        shared_gate_full,
        shared_up_full,
        router_full,
        *got,
    ) = hidden_rows(
        (hidden * second_gain).astype(BF16),
        as_stat(jnp.sum(hidden * hidden, 1)),
        slot_row,
        shared_gate_parts + shared_up_parts + router_parts,
        capacity,
        3,
        to_others((expert_up, up_high), shared_down, (expert_down, (0, (0, fall_first)))),
    )
    second_root = second_root[:, :1]
    up_pieces = [expert_up] + interleave(up_first, from_others(got, 0))
    (
        fall_full,
        picked_back,
        activation,
        grad_gate_in,
        grad_up_in,
        slot_grad,
        shared_gin,
        shared_gup,
        coefficient,
        stat,
        grad_full,
        shared_down_full,
        probs,
        *fall_sent,
    ) = mixture(
        cotangent,
        picked,
        slot_row,
        slot_col,
        logits,
        slot_gate,
        shared_in,
        shared_lift,
        gate_pieces,
        up_pieces,
        expert_down,
        from_others(got, 2),
        [shared_down] + from_others(got, 1),
        4,
    )
    n_row = lax.axis_size("row")
    units = activation.shape[1]
    other = range(1, n_row)

    def part_of(array, p):
        return (array, ((0, array.shape[0]), (p * part, part)))

    part_tiles = [(at, min(TILE, part - at), 0, units) for at in range(0, part, TILE)]
    fall_tiles = [(at, min(3 * LANES, units - at), 0, part) for at in range(0, units, 3 * LANES)]

    def sent_rows(arrays, tiles, some):
        return [
            Swap(array, t, ((tiles[i][0], tiles[i][1]),))
            for i in some
            for t, array in enumerate(arrays, 1)
        ]

    fall_split = max(1, len(fall_tiles) * 3 // 4)
    fall_now, fall_late = range(fall_split), range(fall_split, len(fall_tiles))
    part_split = max(1, len(part_tiles) * 3 // 4)
    part_now, part_late = range(part_split), range(part_split, len(part_tiles))
    rows_all = (0, row_count)
    expert_tiles = [(at, TILE, 0, width) for at in range(0, capacity, TILE)]

    grad_normed_two, stats, *got = scatter_cols(
        [
            ("nn", pick_back, picked_back),
            ("nn", shared_gin, shared_gate_full),
            ("nn", shared_gup, shared_up_full),
            ("nn", coefficient, router_full),
        ],
        as_stat(stat[:, 0], stat[:, 1]),
        2,
        5,
        sent_rows(fall_sent, fall_tiles, fall_now),
        jobs=[Job("tn", part_of(picked, p), (grad_gate_in, ()), part_tiles, BF16) for p in other]
        + [Job("tn", part_of(picked, p), (grad_up_in, ()), part_tiles, BF16) for p in other]
        + [Job("nn", (activation, ()), (fall_full, ()), expert_tiles, BF16, scale=(slot_gate, ()))],
    )
    fall_got, got = got[: len(fall_now) * len(other)], got[len(fall_now) * len(other) :]
    gate_sent, up_sent, (expert_out,) = got[: len(other)], got[len(other) : 2 * len(other)], got[-1:]

    stats = stats.reshape(n, 2, row_count)
    inner_total = jnp.sum(stats[:, 0], 0)[:, None]
    shares = stats[:, 1]
    logit_grad = (shares - probs.T * jnp.sum(shares, 0, keepdims=True)).astype(BF16)
    router_tiles = [(0, experts, at, 4 * LANES) for at in range(0, width, 4 * LANES)]
    wide_tiles = [(0, shared_act.shape[1], at, 4 * LANES) for at in range(0, width, 4 * LANES)]
    branch, *got = scatter_cols(
        [("nn", pick_back, expert_out), ("nn", shared_act, shared_down_full)],
        None,
        2,
        7,
        sent_rows(fall_sent, fall_tiles, fall_late) + sent_rows(gate_sent, part_tiles, part_now),
        jobs=[
            Job("tn", (shared_gin, ()), (normed_two, ()), wide_tiles, BF16),
            Job("tn", (shared_gup, ()), (normed_two, ()), wide_tiles, BF16),
            Job("tn", (shared_act, ()), (grad_full, ()), wide_tiles, BF16),
            Job("nn", (logit_grad, ()), (normed_two, ()), router_tiles, BF16),
        ],
    )
    fall_got += got[: len(fall_late) * len(other)]
    gate_got = got[len(fall_late) * len(other) : -4]
    shared_grads = got[-4:]
    output = (hidden + branch).astype(BF16)
    grad_stream = cotangent.astype(F32)
    grad_hidden = (
        grad_stream
        + second_root * (grad_normed_two * second_gain)
        - hidden * (second_root * second_root * inner_total / width)
    )
    second_gain_grad = jnp.sum(grad_normed_two * hidden * second_root, 0)
    up_now = range(len(part_tiles) // 2)

    def others_of(array, count=None):
        return [Swap(array, t, ((0, count or array.shape[0]), (t * part, part))) for t in other]

    (
        latent_gain_grad,
        output_grad,
        query_grad,
        up_grad,
        query_back,
        low_long,
        low_wide,
        inner,
        *got,
    ) = attention_backward(
        grad_hidden.astype(BF16),
        (
            out_full,
            queries,
            keys,
            values,
            latent,
            low,
            latent_root,
            mixed,
            log_total,
            up_full,
            choose,
            latent_gains,
            *tables,
            seg_col,
            seg_row,
            normed,
        ),
        6,
        sent_rows(gate_sent, part_tiles, part_late)
        + sent_rows(up_sent, part_tiles, up_now)
        + others_of(shared_grads[0]),
    )
    gate_count, up_count = len(part_late) * len(other), len(up_now) * len(other)
    gate_got += got[:gate_count]
    up_got = got[gate_count : gate_count + up_count]
    shared_got = [got[gate_count + up_count :]]

    up_grads = own_parts(up_grad, 1)
    swaps = sent_rows(up_sent, part_tiles, range(len(up_now), len(part_tiles)))
    in_flight = len(swaps)

    def by_tile(got, count):
        return [list(got[i * len(other) : (i + 1) * len(other)]) for i in range(count)]

    grad_normed, low_own, stats, *got = scatter_cols(
        [("nn", query_back, query_full), ("nn", low_long, down_full)],
        as_stat(inner[:, 0], latent_gain_grad[0], jnp.zeros((-LATENT % 1024,), F32)),
        2,
        8,
        swaps
        + [swap for array in shared_grads[1:] for swap in others_of(array)]
        + others_of(query_grad, QK)
        + others_of(output_grad)
        + [Swap(array, t) for t, array in enumerate(up_grads[1:], 1)],
        low_wide,
        jobs=[
            Job(
                "tn", (activation, ()), part_of(slot_grad, 0), fall_tiles, F32,
                add=by_tile(fall_got, len(fall_tiles)),
            ),
            Job(
                "tn", part_of(picked, 0), (grad_gate_in, ()), part_tiles, F32,
                add=by_tile(gate_got, len(part_tiles)),
            ),
            Job(
                "tn", part_of(picked, 0), (grad_up_in, ()), part_tiles, F32,
                add=by_tile(up_got + list(range(in_flight)), len(part_tiles)),
            ),
        ],
    )
    fall_grad, gate_grad, up_proj_grad = got[-3:]
    got = [shared_got[0]] + by_tile(got[in_flight:-3], 6)
    stats = jnp.sum(stats, 0).reshape(-1)
    inner_total = stats[:row_count, None]
    latent_gain_sum = stats[row_count : row_count + LATENT]
    stream = tokens.astype(F32)
    grad_input = (
        grad_hidden
        + first_root * (grad_normed * first_gain)
        - stream * (first_root * first_root * inner_total / width)
    )
    first_gain_grad = jnp.sum(grad_normed * stream * first_root, 0)
    firsts = [array[:, :part] for array in [*shared_grads, query_grad[:QK], output_grad]] + [up_grads[0]]
    totals = [row_sum_of(a.astype(F32), b) for a, b in zip(firsts, got)]
    gains = jnp.concatenate([first_gain_grad, second_gain_grad, latent_gain_sum])
    gains = gains + sum(row_shift(gains, t) for t in other)
    gain_grads = jnp.split(gains, [share, 2 * share])
    return (
        output,
        grad_input.astype(BF16),
        gain_grads[0],
        totals[4].T,
        row_sum(cut(dot_nn(low_own.astype(BF16), normed)[:narrow].T, 0)),
        gain_grads[2],
        totals[6].T,
        totals[5],
        gain_grads[1],
        totals[3].T,
        gate_grad[None],
        up_proj_grad[None],
        fall_grad[None],
        totals[0].T,
        totals[1].T,
        totals[2],
    )


def solution(mesh):
    return jax.shard_map(
        per_device,
        mesh=mesh,
        in_specs=(
            P("row", "col"),
            P("row", "col"),
            P("row", None),
            P("row", None),
            P("col"),
            P("row", "col"),
            P("row", "col"),
            P(),
            P("row", "col"),
            P("col", "row"),
            P("col"),
            P("row", None),
            P("col", "row", None),
            P("col", "row", None),
            P("col", None, "row"),
            P("row", "col"),
            P("row", "col"),
            P("col", "row"),
        ),
        out_specs=(
            P("row", "col"),
            P("row", "col"),
            P("col"),
            P("row", "col"),
            P("row", "col"),
            P(),
            P("row", "col"),
            P("col", "row"),
            P("col"),
            P("row", None),
            P("col", "row", None),
            P("col", "row", None),
            P("col", None, "row"),
            P("row", "col"),
            P("row", "col"),
            P("col", "row"),
        ),
        check_vma=False,
    )
```
